32 devices in a mesh: dp: 16 (over z, x, core), expert: 2 (over y).
Axes of the slice: x: 2, y: 2, z: 4, core: 2. Of those that a mesh axis runs over, the one named last changes fastest.
Arguments:
- tokens: bfloat16 [16384, 512], P('dp'), may hold values from -6 to 6
- gain_attn: float32 [512], replicated, may hold values from 0.1 to 1.9
- w_key: bfloat16 [512, 64], P('dp'), may hold values from -0.25 to 0.25
- w_value: bfloat16 [512, 64], P('dp'), may hold values from -0.25 to 0.25
- w_router: bfloat16 [512, 24], replicated, may hold values from -0.125 to 0.125
- w_query: bfloat16 [512, 1536], P(None, 'expert'), may hold values from -0.25 to 0.25
- w_out: bfloat16 [1536, 512], P('expert'), may hold values from -33.75 to 33.75
- gain_ffn: float32 [512], replicated, may hold values from 0.1 to 1.9
- w_hidden: bfloat16 [512, 2048], P('dp', 'expert'), may hold values from -0.25 to 0.25
- w_output: bfloat16 [2048, 512], P('expert', 'dp'), may hold values from -0.1875 to 0.1875
- expert_ids: int32 [16384, 8], P('dp'), may hold values from 0 to 23, all different within a row
- lengths: int32 [16], P('dp'), may hold values from 64 to 1024, as said below
- grad_out: bfloat16 [16384, 512], P('dp', 'expert'), may hold values from -6 to 6
Outputs:
- output: bfloat16 [16384, 512], P('dp', 'expert')
- grad_tokens: bfloat16 [16384, 512], P('dp')
- grad_key: float32 [512, 64], P('dp')
- grad_value: float32 [512, 64], P('dp')
- grad_router: float32 [512, 24], replicated
- grad_query: float32 [512, 1536], P(None, 'expert')
- grad_outproj: float32 [1536, 512], P('expert')
- grad_hidden: float32 [512, 2048], P('dp', 'expert')
- grad_output: float32 [2048, 512], P('expert', 'dp')
- grad_gain_attn: float32 [512], replicated
- grad_gain_ffn: float32 [512], replicated
The draws below stay inside these ranges and needn't reach their ends.
Inputs may be any that keep to these rules, and one draw needn't show every extreme that they name: `lengths`: in every draw one sequence has exactly 1024 real tokens and another exactly 64.
All inputs are finite; a program needn't handle non-finite values.
Results may differ from the reference program's by a relative error of at most 0.012.
The reference program's roundings to bfloat16 on the way count: a program that leaves them out, or rounds other values in their place, can miss the bound.
Values may be sent and summed in bfloat16 or wider, within the bound.
A program may use at most 192 MiB of HBM per device.

```python
import jax
import jax.numpy as jnp
from jax import lax

D = 512
EXPERTS = 24
HD = 64
TOP = 8
FF = 2048
SEQ_LEN = 1024
SHORT = 64
SEQS = 16
TOKENS = 16384


def draw_lengths(key, part):
    count = SEQS
    drawn = jax.random.randint(key, (count,), SHORT, SEQ_LEN + 1)
    first = jax.random.randint(jax.random.fold_in(key, 1), (), 0, count)
    second = (first + jax.random.randint(jax.random.fold_in(key, 2), (), 1, count)) % count
    drawn = drawn.at[first].set(SEQ_LEN)
    drawn = drawn.at[second].set(SHORT)
    return drawn.astype(jnp.int32)


def levels(stream_key, extent, split, smallest, largest):
    level, own = 1.0, jax.random.fold_in(stream_key, 6)
    for axis_at, blocks in split:
        heights = jnp.exp(jax.random.uniform(jax.random.fold_in(own, axis_at), (blocks,), jnp.float32, smallest / len(split), largest / len(split)))
        level = level * jnp.repeat(heights, extent[axis_at] // blocks).reshape([-1 if axis == axis_at else 1 for axis in range(len(extent))])
    return level


def choose_distinct(stream_key, rows, count, top, lift):
    ranking = jax.random.permutation(jax.random.fold_in(stream_key, 1), count)
    favour = ranking
    for power in range(3):
        favour = favour * favour // count
    favour = favour * lift // count
    lots = jax.random.randint(jax.random.fold_in(stream_key, 2), (rows, count), 0, 4096) + favour
    sure = jax.random.permutation(jax.random.fold_in(stream_key, 3), rows)[jnp.arange(count) % rows]
    lots = jnp.where(jnp.arange(rows)[:, None] == sure[None, :], 1 << 14, lots)
    priority = lots * count + jnp.arange(count)
    return lax.top_k(priority.astype(jnp.int32), top)[1].astype(jnp.int32)


def scatter_about(own_key, extent, spread, most, pieces=(), held_as=jnp.bfloat16):
    values = spread * jax.random.normal(own_key, extent, jnp.float32)
    if pieces:
        values = values * levels(own_key, extent, pieces, -0.22, 0.18)
    return jnp.clip(values, -most, most).astype(held_as)


def setup_inputs(seed: int = 0) -> dict:
    arg_keys = jax.random.split(jax.random.key(seed), 14)
    tokens = scatter_about(arg_keys[0], (TOKENS, D), 1.0, 6.0, ((0, 16),))
    gain_attn = jnp.clip(1.0 + 0.18 * jax.random.normal(arg_keys[1], (D,), jnp.float32), 0.1, 1.9)
    w_key = scatter_about(arg_keys[2], (D, HD), D ** -0.5, 0.25, ((0, 16),))
    w_value = scatter_about(arg_keys[3], (D, HD), D ** -0.5, 0.25, ((0, 16),))
    w_router = scatter_about(arg_keys[4], (D, EXPERTS), (4 * D) ** -0.5, 0.125)
    w_query = scatter_about(arg_keys[5], (D, EXPERTS * HD), D ** -0.5, 0.25, ((1, 2),))
    w_out = scatter_about(arg_keys[6], (EXPERTS * HD, D), ((TOP * SEQ_LEN // (4 * HD)) ** 0.5), 33.75, ((0, 2),))
    gain_ffn = jnp.clip(1.0 + 0.18 * jax.random.normal(arg_keys[7], (D,), jnp.float32), 0.1, 1.9)
    w_hidden = scatter_about(arg_keys[8], (D, FF), D ** -0.5, 0.25, ((0, 16), (1, 2)))
    w_output = scatter_about(arg_keys[9], (FF, D), (FF // 2) ** -0.5, 0.1875, ((0, 2), (1, 16)))
    expert_ids = choose_distinct(arg_keys[10], TOKENS, EXPERTS, TOP, 2730)
    lengths = draw_lengths(jax.random.fold_in(arg_keys[13], 71), 0)
    grad_out = scatter_about(arg_keys[12], (TOKENS, D), 1.0, 6.0, ((0, 16), (1, 2)))
    return {"tokens": tokens, "gain_attn": gain_attn, "w_key": w_key, "w_value": w_value, "w_router": w_router, "w_query": w_query, "w_out": w_out, "gain_ffn": gain_ffn, "w_hidden": w_hidden, "w_output": w_output, "expert_ids": expert_ids, "lengths": lengths, "grad_out": grad_out}


@jax.custom_vjp
def low(v):
    return lax.optimization_barrier(v.astype(jnp.bfloat16)).astype(jnp.float32)

@jax.custom_vjp
def low_back(v):
    return v

def low_keep(v):
    return (low(v), None)

def low_pass(kept, grad):
    return (grad,)

def back_keep(v):
    return (v, None)

def back_low(kept, grad):
    return (low(grad),)
low.defvjp(low_keep, low_pass)
low_back.defvjp(back_keep, back_low)
eps = 1e-05
big_neg = -1000000000.0

def matmul_hi(left, right):
    return jnp.dot(left, right, precision=lax.Precision.HIGHEST)

def norm_rows(values, gain):
    row_mean = lax.optimization_barrier(jnp.mean(values, axis=-1, keepdims=True))
    centred = values - row_mean
    row_var = lax.optimization_barrier(jnp.mean(centred * centred, axis=-1, keepdims=True))
    return centred * lax.rsqrt(row_var + eps) * gain

def attend_seq(query_seq, key_seq, value_seq, seq_length):
    slots = jnp.arange(SEQ_LEN)
    allowed = (slots[None, :] <= slots[:, None]) & (slots[None, :] < seq_length)
    scores = low_back(jnp.einsum('qeh,kh->eqk', query_seq, key_seq, precision=lax.Precision.HIGHEST))
    scores = jnp.where(allowed[None], scores, big_neg)
    row_top = lax.optimization_barrier(jnp.max(scores, axis=-1, keepdims=True))
    exponent = jnp.exp(scores - row_top)
    probs = low(exponent / lax.optimization_barrier(jnp.sum(exponent, axis=-1, keepdims=True)))
    return low_back(jnp.einsum('eqk,kh->qeh', probs, value_seq, precision=lax.Precision.HIGHEST))

def reference(tokens, gain_attn, w_key, w_value, w_router, w_query, w_out, gain_ffn, w_hidden, w_output, expert_ids, lengths, grad_out):
    slots = jnp.arange(SEQ_LEN)
    valid_rows = (slots[None, :] < lengths[:, None]).astype(jnp.float32).reshape(TOKENS, 1)
    choose = (expert_ids[:, :, None] == jnp.arange(EXPERTS)[None, None, :]).astype(jnp.float32)
    query_scale = HD ** (-0.5)

    def forward(inputs, gain_one, key_weight, value_weight, router_weight, query_weight, out_weight, gain_two, hidden_weight, output_weight):
        normed_one = low(norm_rows(inputs, gain_one))
        keys = low(low_back(matmul_hi(normed_one, key_weight)))
        values = low(low_back(matmul_hi(normed_one, value_weight)))
        logits = low_back(matmul_hi(normed_one, router_weight))
        picked = lax.optimization_barrier(jnp.sum(logits[:, None, :] * choose, axis=-1))
        row_top = lax.optimization_barrier(jnp.max(picked, axis=-1, keepdims=True))
        exponent = jnp.exp(picked - row_top)
        gate_weights = exponent / lax.optimization_barrier(jnp.sum(exponent, axis=-1, keepdims=True))
        dense_gate = lax.optimization_barrier(jnp.sum(gate_weights[:, :, None] * choose, axis=1))
        queries = low(low_back(query_scale * matmul_hi(normed_one, query_weight)))
        step_fn = jax.checkpoint(lambda packed: attend_seq(packed[0], packed[1], packed[2], packed[3]))
        head_out = lax.map(step_fn, (queries.reshape(SEQS, SEQ_LEN, EXPERTS, HD), keys.reshape(SEQS, SEQ_LEN, HD), values.reshape(SEQS, SEQ_LEN, HD), lengths))
        head_out = head_out.reshape(TOKENS, EXPERTS, HD)
        gated = low((dense_gate[:, :, None] * head_out).reshape(TOKENS, EXPERTS * HD))
        attended = low_back(matmul_hi(gated, out_weight))
        residual = inputs + valid_rows * attended
        normed_two = low(norm_rows(residual, gain_two))
        active = low(jax.nn.gelu(low_back(matmul_hi(normed_two, hidden_weight))))
        ffn_value = low_back(matmul_hi(active, output_weight))
        return residual + valid_rows * ffn_value
    primals = (tokens.astype(jnp.float32), gain_attn, w_key.astype(jnp.float32), w_value.astype(jnp.float32), w_router.astype(jnp.float32), w_query.astype(jnp.float32), w_out.astype(jnp.float32), gain_ffn, w_hidden.astype(jnp.float32), w_output.astype(jnp.float32))
    result, pull = jax.vjp(forward, *primals)
    grads = pull(grad_out.astype(jnp.float32))
    return (result.astype(jnp.bfloat16), grads[0].astype(jnp.bfloat16), grads[2], grads[3], grads[4], grads[5], grads[6], grads[8], grads[9], grads[1], grads[7])
```

```python
import functools

import jax
import jax.numpy as jnp
from jax import lax
from jax.experimental import pallas as pl
from jax.experimental.pallas import tpu as pltpu
from jax.sharding import PartitionSpec as P

f32 = jnp.float32
bf16 = jnp.bfloat16
eps = 1e-05
lowest = -1e30
rb = 128


def nn(left, right):
    return jnp.dot(left, right, preferred_element_type=f32)


def nt(left, right):
    return lax.dot_general(left, right, (((1,), (1,)), ((), ())), preferred_element_type=f32)


def tn(left, right):
    return lax.dot_general(left, right, (((0,), (0,)), ((), ())), preferred_element_type=f32)


def norm_rows(x):
    centred = x - jnp.mean(x, axis=-1, keepdims=True)
    inv = lax.rsqrt(jnp.mean(centred * centred, axis=-1, keepdims=True) + eps)
    return centred * inv, inv


def norm_back(u, normed, inv, gain):
    w = u * gain
    return inv * (
        w
        - jnp.mean(w, axis=-1, keepdims=True)
        - normed * jnp.mean(w * normed, axis=-1, keepdims=True)
    )


def lanes(shape):
    return lax.broadcasted_iota(jnp.int32, shape, len(shape) - 1)


def main_kernel(
    len_ref, tok, gain1, wkv, wr, wq, wo, gain2, W, ids, go,
    out_ref, gres_ref, h1_own, h1T, gh1q, kvg, glog, gF, gwo, gwq, gain2_ref,
    h1, KK, VV, KKT, VVT, idl, gateb, dense, Qs, PT, O, qf, gated, n2, r2, res,
    h2, h2T, gfT, gf, actS, giS, gh2, acc, gatt, gg, dOs, gdense, DS, gK, gV, dQ, gq,
):
    rows, width = tok.shape[0] * rb, tok.shape[2]
    nb = tok.shape[0] // 2
    top = ids.shape[2]
    groups = wq.shape[1] // 128
    ffh = W.shape[3] // 2
    y = lax.axis_index("expert")
    length = len_ref[0]

    def own(i):
        return 2 * i + y

    @pl.loop(0, 2 * nb)
    def _(b):
        normed, _ = norm_rows(tok[b].astype(f32))
        h = (normed * gain1[...]).astype(bf16)
        h1[b] = h
        kv = nn(h, wkv[...])
        at = pl.ds(pl.multiple_of(b * rb, rb), rb)
        k2, v2 = kv[:, :128], kv[:, 128:]
        KK[at, :] = k2.astype(bf16)
        VV[at, :] = v2.astype(bf16)
        KKT[:, at] = k2.T.astype(bf16)
        VVT[:, at] = v2.T.astype(bf16)

    lane = lanes((rb, 128))
    half = (lane >= 64).astype(jnp.int32)

    @pl.loop(0, nb)
    def _(i):
        h = h1[own(i)]
        at = pl.ds(pl.multiple_of(i * rb, rb), rb)
        h1_own[at, :] = h
        h1T[:, at] = h.astype(f32).T.astype(bf16)
        logits = nn(h, wr[...])
        here = ids[own(i)]
        spread = [jnp.broadcast_to(here[:, k : k + 1], (rb, 128)) for k in range(top)]
        chosen = lane == spread[0]
        for k in range(1, top):
            chosen = chosen | (lane == spread[k])
        most = jnp.max(jnp.where(chosen, logits, lowest), axis=-1, keepdims=True)
        e = jnp.where(chosen, jnp.exp(jnp.where(chosen, logits - most, 0.0)), 0.0)
        g = e / jnp.sum(e, axis=-1, keepdims=True)
        dense[at, :] = g
        for k in range(top):
            gk = jnp.sum(jnp.where(lane == spread[k], g, 0.0), axis=-1, keepdims=True)
            gateb[i, k] = jnp.broadcast_to(gk, (rb, 128))
            idl[i, k] = spread[k] - half
        qf[...] = 0.125 * nn(h, wq[...])

        @pl.loop(0, rb // 16)
        def _(c):
            cut = pl.ds(pl.multiple_of(c * 16, 16), 16)
            parts = [qf[cut, pl.ds(128 * g, 128)] for g in range(groups)]
            for k in range(top):
                mine = idl[i, k, cut, :]
                val = jnp.zeros((16, 128), f32)
                for g in range(groups):
                    val = jnp.where(mine == 2 * g, parts[g], val)
                Qs[i, k, cut, :] = val.astype(bf16)

    diag = lax.broadcasted_iota(jnp.int32, (256, 256), 0) <= rb * y + lanes((256, 256)) % 128
    for i in range(nb):
        nk = 256 * i
        start = 128 * i * (i + 1)

        @pl.loop(0, top // 2)
        def _(p):
            q = Qs[i, pl.ds(2 * p, 2)].reshape(256, 128)
            cols = pl.ds(pl.multiple_of(p * 256, 256), 256)
            s1 = nt(KK[nk : nk + 256, :], q)
            s1 = jnp.where(diag, s1, lowest)
            m = jnp.max(s1, axis=0, keepdims=True)
            if nk:
                s0 = nt(KK[0:nk, :], q)
                m = jnp.maximum(m, jnp.max(s0, axis=0, keepdims=True))
                p0 = jnp.exp(s0 - m)
            p1 = jnp.exp(s1 - m)
            tot = jnp.sum(p1, axis=0, keepdims=True)
            if nk:
                tot = tot + jnp.sum(p0, axis=0, keepdims=True)
            inv = 1.0 / tot
            p1 = (p1 * inv).astype(bf16)
            PT[start + nk : start + nk + 256, cols] = p1
            o = nn(VVT[:, nk : nk + 256], p1)
            if nk:
                p0 = (p0 * inv).astype(bf16)
                PT[start : start + nk, cols] = p0
                o = o + nn(VVT[:, 0:nk], p0)
            O[i, pl.ds(2 * p, 2)] = o.T.reshape(2, rb, 128)

    @pl.loop(0, nb)
    def _(i):
        at = pl.ds(pl.multiple_of(i * rb, rb), rb)

        @pl.loop(0, rb // 16)
        def _(c):
            cut = pl.ds(pl.multiple_of(c * 16, 16), 16)
            cutr = pl.ds(pl.multiple_of(i * rb + c * 16, 16), 16)
            mine = [idl[i, k, cut, :] for k in range(top)]
            vals = [gateb[i, k, cut, :] * O[i, k, cut, :] for k in range(top)]
            for g in range(groups):
                val = jnp.zeros((16, 128), f32)
                for k in range(top):
                    val = jnp.where(mine[k] == 2 * g, vals[k], val)
                gated[cutr, pl.ds(128 * g, 128)] = val.astype(bf16)

        valid = (rb * own(i) + lax.broadcasted_iota(jnp.int32, (rb, 1), 0) < length).astype(f32)
        r = tok[own(i)].astype(f32) + valid * nn(gated[at, :], wo[...])
        res[at, :] = r
        normed, inv = norm_rows(r)
        n2[at, :] = normed
        r2[at, :] = inv
        h = normed * gain2[...]
        h2[at, :] = h.astype(bf16)
        h2T[:, at] = h.T.astype(bf16)
        gfi = valid * go[at, :].astype(f32)
        gf[at, :] = gfi.astype(bf16)
        gfT[:, at] = gfi.T.astype(bf16)

    c0 = 0.7978845608028654
    c1 = 0.044715
    ch = 512
    for e in range(2):
        for j in range(ffh // ch):
            first = e == 0 and j == 0

            @pl.loop(0, nb)
            def _(i):
                at = pl.ds(pl.multiple_of(i * rb, rb), rb)
                w1 = W[e, :, :, j * ch : (j + 1) * ch].reshape(width, ch)
                w2 = W[e, :, :, ffh + j * ch : ffh + (j + 1) * ch].reshape(width, ch)
                v = nn(h2[at, :], w1)
                ga = nn(gf[at, :], w2)
                vv = v * v
                t = jnp.tanh(v * (c0 + (c0 * c1) * vv))
                hp = 0.5 + 0.5 * t
                act = (v * hp).astype(bf16)
                d = hp + (0.5 * v) * (1.0 - t * t) * (c0 + (3 * c0 * c1) * vv)
                gi = (d * ga).astype(bf16)
                actS[at, :] = act
                giS[at, :] = gi
                a = nt(act, w2)
                b = nt(gi, w1)
                if not first:
                    a = a + acc[at, :]
                    b = b + gh2[at, :]
                acc[at, :] = a
                gh2[at, :] = b

            gF[e, :, :, j * ch : (j + 1) * ch] = (
                nn(h2T[...], giS[...]).astype(bf16).reshape(16, width // 16, ch)
            )
            gF[e, :, :, ffh + j * ch : ffh + (j + 1) * ch] = (
                nn(gfT[...], actS[...]).astype(bf16).reshape(16, width // 16, ch)
            )

    gain2_ref[...] = jnp.zeros_like(gain2_ref)

    @pl.loop(0, nb)
    def _(i):
        at = pl.ds(pl.multiple_of(i * rb, rb), rb)
        valid = (rb * own(i) + lax.broadcasted_iota(jnp.int32, (rb, 1), 0) < length).astype(f32)
        out_ref[at, :] = (res[at, :] + valid * acc[at, :]).astype(bf16)
        u, normed = gh2[at, :], n2[at, :]
        gain2_ref[...] += jnp.sum(u * normed, axis=0, keepdims=True)
        gr = go[at, :].astype(f32) + norm_back(u, normed, r2[at, :], gain2[...])
        gres_ref[at, :] = gr
        ga = (valid * gr).astype(bf16)
        gatt[at, :] = ga
        gg[...] = nt(ga, wo[...])

        @pl.loop(0, rb // 16)
        def _(c):
            cut = pl.ds(pl.multiple_of(c * 16, 16), 16)
            cutr = pl.ds(pl.multiple_of(i * rb + c * 16, 16), 16)
            parts = [gg[cut, pl.ds(128 * g, 128)] for g in range(groups)]
            ln = lanes((16, 128))
            hf = (ln >= 64).astype(jnp.int32)
            gd = jnp.zeros((16, 128), f32)
            for k in range(top):
                mine = idl[i, k, cut, :]
                val = jnp.zeros((16, 128), f32)
                for g in range(groups):
                    val = jnp.where(mine == 2 * g, parts[g], val)
                dot = jnp.sum(val * O[i, k, cut, :], axis=-1, keepdims=True)
                gd = jnp.where(mine + hf == ln, dot, gd)
                dOs[i, k, cut, :] = (gateb[i, k, cut, :] * val).astype(bf16)
            dn = dense[cutr, :]
            gs = dn * (gd - jnp.sum(dn * gd, axis=-1, keepdims=True))
            glog[cutr, :] = gs.astype(bf16)

    gwo[...] = tn(gated[...], gatt[...]).astype(bf16)

    gK[...] = jnp.zeros_like(gK)
    gV[...] = jnp.zeros_like(gV)
    for i in range(nb):
        nk = 256 * (i + 1)
        start = 128 * i * (i + 1)

        @pl.loop(0, top // 2)
        def _(p):
            do = dOs[i, pl.ds(2 * p, 2)].reshape(256, 128)
            cols = pl.ds(pl.multiple_of(p * 256, 256), 256)
            dp = nt(VV[0:nk, :], do)
            pr = PT[start : start + nk, cols].astype(f32)
            d = jnp.sum(pr * dp, axis=0, keepdims=True)
            ds = (pr * (dp - d)).astype(bf16)
            DS[0:nk, cols] = ds
            dq = nn(KKT[:, 0:nk], ds)
            dQ[pl.ds(2 * p, 2)] = dq.T.reshape(2, rb, 128)

        gK[0:nk, :] += nn(DS[0:nk, :], Qs[i].reshape(top * rb, 128))
        gV[0:nk, :] += nn(PT[start : start + nk, :], dOs[i].reshape(top * rb, 128))

        @pl.loop(0, rb // 16)
        def _(c):
            cut = pl.ds(pl.multiple_of(c * 16, 16), 16)
            cutr = pl.ds(pl.multiple_of(i * rb + c * 16, 16), 16)
            mine = [idl[i, k, cut, :] for k in range(top)]
            vals = [dQ[k, cut, :] for k in range(top)]
            for g in range(groups):
                val = jnp.zeros((16, 128), f32)
                for k in range(top):
                    val = jnp.where(mine[k] == 2 * g, vals[k], val)
                gq[cutr, pl.ds(128 * g, 128)] = val.astype(bf16) * 0.125

    gwq[...] = nn(h1T[...], gq[...]).astype(bf16)
    gh1q[...] = nt(gq[...], wq[...])

    @pl.loop(0, 2 * nb)
    def _(b):
        at = pl.ds(pl.multiple_of(b * rb, rb), rb)
        a, c = gK[at, :], gV[at, :]
        a = a + pltpu.roll(a, 64, 1)
        c = c + pltpu.roll(c, 64, 1)
        kvg[b] = jnp.where(lane < 64, a, c)


def shards(
    tokens, gain_attn, w_key, w_value, w_router, w_query, w_out, gain_ffn,
    w_hidden, w_output, expert_ids, lengths, grad_out,
):
    rows, width = tokens.shape
    y = lax.axis_index("expert")
    nb = rows // rb // 2
    top = expert_ids.shape[1]
    n_experts = w_router.shape[1]
    hd = w_key.shape[1]
    own_rows = rows // 2
    pay = 2 * w_hidden.shape[1]
    kv_full = lax.all_gather(jnp.concatenate((w_key, w_value), 1), "dp", axis=0, tiled=True)
    wk, wv = kv_full[:, :hd], kv_full[:, hd:]
    wkv4 = jnp.concatenate((wk, wk, wv, wv), 1)
    wr = jnp.pad(w_router, ((0, 0), (0, 128 - n_experts)))
    W = lax.all_gather(
        jnp.concatenate((w_hidden, w_output.T), 1), ("expert", "dp"), axis=0, tiled=True
    ).reshape(2, 16, width // 16, pay)
    wq = lax.all_gather(w_query, "expert", axis=1, tiled=True)
    wo = lax.all_gather(w_out, "expert", axis=0, tiled=True)
    go_all = lax.all_gather(grad_out, "expert", axis=1, tiled=True)
    go = lax.dynamic_index_in_dim(
        go_all.reshape(nb, 2, rb, width), y, 1, keepdims=False
    ).reshape(own_rows, width)
    tok = tokens.reshape(2 * nb, rb, width)
    ids = expert_ids.reshape(2 * nb, rb, top)
    sds = jax.ShapeDtypeStruct
    fq = wq.shape[1]
    total = 128 * nb * (nb + 1)
    vm = pltpu.VMEM
    tk = top * rb
    outs = pl.pallas_call(
        main_kernel,
        out_shape=(
            sds((own_rows, width), bf16),
            sds((own_rows, width), f32),
            sds((own_rows, width), bf16),
            sds((width, own_rows), bf16),
            sds((own_rows, width), f32),
            sds((2 * nb, rb, 128), f32),
            sds((own_rows, 128), bf16),
            sds(W.shape, bf16),
            sds(wo.shape, bf16),
            sds(wq.shape, bf16),
            sds((1, width), f32),
        ),
        in_specs=[pl.BlockSpec(memory_space=pltpu.SMEM)]
        + [pl.BlockSpec(memory_space=pltpu.VMEM)] * 10,
        out_specs=[pl.BlockSpec(memory_space=pltpu.VMEM)] * 11,
        scratch_shapes=[
            vm((2 * nb, rb, width), bf16),
            vm((rows, 128), bf16),
            vm((rows, 128), bf16),
            vm((128, rows), bf16),
            vm((128, rows), bf16),
            vm((nb, top, rb, 128), jnp.int32),
            vm((nb, top, rb, 128), f32),
            vm((own_rows, 128), f32),
            vm((nb, top, rb, 128), bf16),
            vm((total, tk), bf16),
            vm((nb, top, rb, 128), f32),
            vm((rb, fq), f32),
            vm((own_rows, fq), bf16),
            vm((own_rows, width), f32),
            vm((own_rows, 1), f32),
            vm((own_rows, width), f32),
            vm((own_rows, width), bf16),
            vm((width, own_rows), bf16),
            vm((width, own_rows), bf16),
            vm((own_rows, width), bf16),
            vm((own_rows, 512), bf16),
            vm((own_rows, 512), bf16),
            vm((own_rows, width), f32),
            vm((own_rows, width), f32),
            vm((own_rows, width), bf16),
            vm((rb, fq), f32),
            vm((nb, top, rb, 128), bf16),
            vm((own_rows, 128), f32),
            vm((rows, tk), bf16),
            vm((rows, 128), f32),
            vm((rows, 128), f32),
            vm((top, rb, 128), f32),
            vm((own_rows, fq), bf16),
        ],
        compiler_params=pltpu.CompilerParams(vmem_limit_bytes=62 * 2**20),
    )(
        lengths, tok, gain_attn[None], wkv4, wr, wq, wo, gain_ffn[None], W, ids, go,
    )
    out_own, gres, h1_own, h1T, gh1q, kvg, glog, gF, gwo, gwq, gain2 = outs
    kv_sum = lax.psum(kvg, "expert")
    kv_own = (
        lax.dynamic_index_in_dim(kv_sum.reshape(nb, 2, rb, 128), y, 1, keepdims=False)
        .reshape(own_rows, 128)
        .astype(bf16)
    )
    gh1 = gh1q + nt(kv_own, kv_full) + nt(glog, wr)
    own_x = lax.dynamic_index_in_dim(
        tokens.reshape(nb, 2, rb, width), y, 1, keepdims=False
    ).reshape(own_rows, width)
    n1, r1 = norm_rows(own_x.astype(f32))
    gain1_rows = jnp.sum(gh1 * n1, axis=0)
    gt = (gres + norm_back(gh1, n1, r1, gain_attn)).astype(bf16)

    def weave(own):
        both = lax.all_gather(own.reshape(nb, 1, rb, -1), "expert", axis=1, tiled=True)
        return both.reshape(rows, -1)

    grad_tokens = weave(gt)
    both = lax.all_to_all(
        out_own.reshape(nb, 1, rb, width), "expert", split_axis=3, concat_axis=1, tiled=True
    )
    output = both.reshape(rows, width // 2)
    gkv = lax.psum_scatter(
        lax.psum(nn(h1T, kv_own), "expert"), "dp", scatter_dimension=0, tiled=True
    )
    gF_own = lax.psum_scatter(
        gF.reshape(2, width, pay), "expert", scatter_dimension=0, tiled=True
    ).reshape(width, pay).astype(f32)
    gF_own = lax.psum_scatter(gF_own, "dp", scatter_dimension=0, tiled=True)
    gwq_own = lax.psum_scatter(gwq, "expert", scatter_dimension=1, tiled=True)
    gwo_own = lax.psum_scatter(gwo, "expert", scatter_dimension=0, tiled=True)
    gwq_own, gwo_own = lax.psum((gwq_own.astype(f32), gwo_own.astype(f32)), "dp")
    grad_router, gain1g, gain2g = lax.psum(
        (nn(h1T, glog)[:, :n_experts], gain1_rows, gain2[0]), ("dp", "expert")
    )
    return (
        output, grad_tokens, gkv[:, :hd], gkv[:, hd:], grad_router, gwq_own, gwo_own,
        gF_own[:, : pay // 2], gF_own[:, pay // 2 :].T, gain1g, gain2g,
    )


def solution(mesh):
    placed = (
        P("dp", None), P(), P("dp", None), P("dp", None), P(), P(None, "expert"),
        P("expert", None), P(), P("dp", "expert"), P("expert", "dp"), P("dp", None),
        P("dp"), P("dp", "expert"),
    )
    return jax.shard_map(
        shards,
        mesh=mesh,
        in_specs=placed,
        out_specs=(
            P("dp", "expert"), P("dp", None), P("dp", None), P("dp", None), P(),
            P(None, "expert"), P("expert", None), P("dp", "expert"), P("expert", "dp"),
            P(), P(),
        ),
        check_vma=False,
    )
```

```python
import functools

import jax
import jax.numpy as jnp
from jax import lax
from jax.experimental import pallas as pl
from jax.experimental.pallas import tpu as pltpu
from jax.sharding import PartitionSpec as P

f32 = jnp.float32
bf16 = jnp.bfloat16
eps = 1e-05
lowest = -1e30
rb = 128


def nn(left, right):
    return jnp.dot(left, right, preferred_element_type=f32)


def nt(left, right):
    return lax.dot_general(left, right, (((1,), (1,)), ((), ())), preferred_element_type=f32)


def tn(left, right):
    return lax.dot_general(left, right, (((0,), (0,)), ((), ())), preferred_element_type=f32)


def norm_rows(x):
    centred = x - jnp.mean(x, axis=-1, keepdims=True)
    inv = lax.rsqrt(jnp.mean(centred * centred, axis=-1, keepdims=True) + eps)
    return centred * inv, inv


def norm_back(u, normed, inv, gain):
    w = u * gain
    return inv * (
        w
        - jnp.mean(w, axis=-1, keepdims=True)
        - normed * jnp.mean(w * normed, axis=-1, keepdims=True)
    )


def lanes(shape):
    return lax.broadcasted_iota(jnp.int32, shape, len(shape) - 1)


MESH = pl.DeviceIdType.MESH

in_names = [
    "len_ref",
    "tok",
    "gain1",
    "wr",
    "gain2",
    "ids",
    "wkv_in",
    "wq_in",
    "wo_in",
    "w_in",
    "go_in",
]
out_names = [
    "out",
    "gt",
    "gwq",
    "gwo",
    "gwh",
    "gwT",
    "gkv",
    "small",
]


def scratch(rows, width, nb, top, fq, ff, nz, shard):
    vm = pltpu.VMEM
    own = rows // 2
    half = fq // 2
    total = 128 * nb * (nb + 1)
    ring = (nz, 2, 2)
    ch = ff // 4
    woc = half // (4 * nz)
    return {
        "wkvg": vm(ring + (shard, 128), bf16),
        "W": vm((2, 2) + ring + (shard, 2 * ch), bf16),
        "WQ": vm((2, width, half), bf16),
        "WO": vm((2, half, width), bf16),
        "GO": vm((2, nb, rb, width // 2), bf16),
        "h1": vm((2 * nb, rb, width), bf16),
        "h1T": vm((width, own), bf16),
        "KK": vm((rows, 128), bf16),
        "VV": vm((rows, 128), bf16),
        "KKT": vm((128, rows), bf16),
        "VVT": vm((128, rows), bf16),
        "idl": vm((nb, top, rb, 128), jnp.int32),
        "gateb": vm((nb, top, rb, 128), f32),
        "dense": vm((own, 128), f32),
        "Qs": vm((nb, top, rb, 128), bf16),
        "PT": vm((total, top * rb), bf16),
        "O": vm((nb, top, rb, 128), f32),
        "wide": vm((rb, fq), f32),
        "gated": vm((own, fq), bf16),
        "n2": vm((own, width), f32),
        "r2": vm((own, 1), f32),
        "res": vm((own, width), f32),
        "h2": vm((own, width), bf16),
        "h2T": vm((width, own), bf16),
        "gfT": vm((width, own), bf16),
        "gf": vm((own, width), bf16),
        "gh2": vm((own, width), f32),
        "acc": vm((own, width), f32),
        "gatt": vm((own, width), bf16),
        "dOs": vm((nb, top, rb, 128), bf16),
        "glog": vm((own, 128), bf16),
        "DS": vm((rows, top * rb), bf16),
        "gK": vm((rows, 128), f32),
        "gV": vm((rows, 128), f32),
        "dQ": vm((top, rb, 128), f32),
        "gain_rows": vm((2, width), f32),
        "outx": vm((nb, rb, width // 2), bf16),
        "kvs": vm((nb, 2, rb, 128), bf16),
        "kvr": vm((nb, rb, 128), bf16),
        "F": vm((2, 2) + ring + (shard, 2 * ch), bf16),
        "FC": vm((2, 2, nz, 2, shard, 2 * ch), bf16),
        "FY0": vm((nz, 2, shard, 2 * ch), bf16),
        "FX0": vm((nz, shard, 2 * ch), bf16),
        "FZ0": vm((nz - 1, shard, 2 * ch), bf16),
        "FX1": vm((2, nz, shard, 2 * ch), bf16),
        "FZ1": vm((nz - 1, 2, shard, 2 * ch), bf16),
        "FY1": vm((shard, 2 * ch), bf16),
        "Q": vm((2,) + ring + (shard, half), bf16),
        "QC": vm((2, nz, 2, shard, half), bf16),
        "QX": vm((2, nz, shard, half), bf16),
        "QY": vm((nz, shard, half), bf16),
        "QZ": vm((nz - 1, shard, half), bf16),
        "QA": vm(ring + (shard, half), bf16),
        "P": vm((2,) + ring + (woc, width), bf16),
        "PC": vm((2, nz, 2, woc, width), bf16),
        "PX": vm((2, nz, woc, width), bf16),
        "PY": vm((nz, woc, width), bf16),
        "PZ": vm((nz - 1, woc, width), bf16),
        "PA": vm(ring + (woc, width), bf16),
        "K": vm(ring + (shard, 128), f32),
        "KC": vm((nz, 2, shard, 128), f32),
        "KX": vm((nz, shard, 128), f32),
        "KZ": vm((nz - 1, shard, 128), f32),
        "KY": vm((2, shard, 128), f32),
        "S": vm((4, 32, width), f32),
        "SR": vm((3, 32, width), f32),
        "SZ": vm((nz, 32, width), f32),
        "send": pltpu.SemaphoreType.DMA((96,)),
        "recv": pltpu.SemaphoreType.DMA((96,)),
        "local": pltpu.SemaphoreType.DMA((8,)),
    }


class Refs:
    pass


def kernel(names, outer, *refs):
    r = Refs()
    for name, ref in zip(names, refs):
        setattr(r, name, ref)
    nb = r.tok.shape[0] // 2
    width = r.tok.shape[2]
    top = r.ids.shape[2]
    fq = r.gated.shape[1]
    half = fq // 2
    groups = fq // 128
    r.gq = r.gated
    r.actS = r.DS.at[0 : nb * rb, 0 : r.W.shape[6] // 2]
    r.giS = r.DS.at[0 : nb * rb, r.W.shape[6] // 2 : r.W.shape[6]]
    nz = r.W.shape[2]
    ch = r.W.shape[6] // 2
    shard = r.W.shape[5]
    d = lax.axis_index("dp")
    y = lax.axis_index("expert")
    n, m = d // outer, d % outer
    z, x, c = n // 4, (n // 2) % 2, n % 2
    length = r.len_ref[0]

    def device(z, x, c, y):
        return ((z * 4 + x * 2 + c) * outer + m, y)

    over_c = device(z, x, 1 - c, y)
    over_x = device(z, 1 - x, c, y)
    over_y = device(z, x, c, 1 - y)
    zs = [(z + k) % nz for k in range(1, nz)]
    over_z = [device(k, x, c, y) for k in zs]
    used = [0]
    sent = []

    def send(source, target, to):
        k = used[0]
        used[0] += 1
        copy = pltpu.make_async_remote_copy(
            src_ref=source, dst_ref=target, send_sem=r.send.at[k], recv_sem=r.recv.at[k],
            device_id=to, device_id_type=MESH,
        )
        copy.start()
        sent.append(copy)
        return copy

    def here(k, source, target):
        copy = pltpu.make_async_copy(source, target, r.local.at[k])
        copy.start()
        return copy

    def got(*copies):
        for copy in copies:
            copy.wait_recv()

    def own(i):
        return 2 * i + y

    def cut(i, size):
        return pl.ds(pl.multiple_of(i * size, size), size)

    def valid_rows(i):
        return (rb * own(i) + lax.broadcasted_iota(jnp.int32, (rb, 1), 0) < length).astype(f32)

    l_w = here(0, r.w_in, r.W.at[:, y, z, x, c])
    l_q = here(1, r.wq_in, r.WQ.at[y])
    l_o = here(2, r.wo_in, r.WO.at[y])
    l_g = here(3, r.go_in.at[:, y], r.GO.at[y])
    l_kv = here(4, r.wkv_in, r.wkvg.at[z, x, c])
    barrier = pltpu.get_barrier_semaphore()
    peers = [over_c, over_x, over_y] + over_z
    for peer in peers:
        pl.semaphore_signal(barrier, inc=1, device_id=peer, device_id_type=MESH)
    pl.semaphore_wait(barrier, len(peers))
    kv_c = send(r.wkv_in, r.wkvg.at[z, x, c], over_c)
    w_y = send(r.w_in, r.W.at[:, y, z, x, c], over_y)
    qrows = cut(c, width // 2)
    q_y = send(r.wq_in.at[qrows, :], r.WQ.at[y, qrows, :], over_y)
    l_w.wait()
    l_kv.wait()

    @pl.loop(0, 2 * nb)
    def _(b):
        normed, _ = norm_rows(r.tok[b].astype(f32))
        r.h1[b] = (normed * r.gain1[...]).astype(bf16)

    got(kv_c)
    kv_x = send(r.wkvg.at[z, x], r.wkvg.at[z, x], over_x)
    got(w_y)

    def w_over_z(j):
        return [
            send(r.W.at[j, :, z, x, c], r.W.at[j, :, z, x, c], to) for to in over_z
        ]

    w0_z = w_over_z(0)

    lane = lanes((rb, 128))
    upper = (lane >= 64).astype(jnp.int32)

    def gates(i):
        h = r.h1[own(i)]
        at = cut(i, rb)
        r.h1T[:, at] = h.astype(f32).T.astype(bf16)
        logits = nn(h, r.wr[...])
        ids = r.ids[own(i)]
        spread = [jnp.broadcast_to(ids[:, k : k + 1], (rb, 128)) for k in range(top)]
        chosen = lane == spread[0]
        for k in range(1, top):
            chosen = chosen | (lane == spread[k])
        most = jnp.max(jnp.where(chosen, logits, lowest), axis=-1, keepdims=True)
        e = jnp.where(chosen, jnp.exp(jnp.where(chosen, logits - most, 0.0)), 0.0)
        g = e / jnp.sum(e, axis=-1, keepdims=True)
        r.dense[at, :] = g
        for k in range(top):
            gk = jnp.sum(jnp.where(lane == spread[k], g, 0.0), axis=-1, keepdims=True)
            r.gateb[i, k] = jnp.broadcast_to(gk, (rb, 128))
            r.idl[i, k] = spread[k] - upper

    pl.loop(0, nb // 2)(gates)
    got(kv_x)
    kv_z = [send(r.wkvg.at[z], r.wkvg.at[z], to) for to in over_z]
    pl.loop(nb // 2, nb)(gates)

    got(*kv_z)

    @pl.loop(0, 2 * nb)
    def _(b):
        kv = nn(r.h1[b], r.wkvg[...].reshape(width, 128))
        at = cut(b, rb)
        swapped = pltpu.roll(kv, 64, 1)
        k2 = jnp.where(lane < 64, kv, swapped)
        v2 = jnp.where(lane < 64, swapped, kv)
        r.KK[at, :] = k2.astype(bf16)
        r.VV[at, :] = v2.astype(bf16)
        r.KKT[:, at] = k2.T.astype(bf16)
        r.VVT[:, at] = v2.T.astype(bf16)

    got(q_y)
    q_c = send(r.WQ.at[1 - y, qrows, :], r.WQ.at[1 - y, qrows, :], over_c)
    orows = cut(c, half // 2)
    o_y = send(r.wo_in.at[orows, :], r.WO.at[y, orows, :], over_y)
    l_q.wait()
    got(q_c)

    @pl.loop(0, nb)
    def _(i):
        h = r.h1[own(i)]
        for e in range(2):
            r.wide[:, e * half : (e + 1) * half] = 0.125 * nn(h, r.WQ[e])

        @pl.loop(0, rb // 16)
        def _(t):
            at = cut(t, 16)
            parts = [r.wide[at, pl.ds(128 * g, 128)] for g in range(groups)]
            for k in range(top):
                mine = r.idl[i, k, at, :]
                val = jnp.zeros((16, 128), f32)
                for g in range(groups):
                    val = jnp.where(mine == 2 * g, parts[g], val)
                r.Qs[i, k, at, :] = val.astype(bf16)

    diag = lax.broadcasted_iota(jnp.int32, (256, 256), 0) <= rb * y + lanes((256, 256)) % 128

    def attend(i):
        nk = 256 * i
        start = 128 * i * (i + 1)

        @pl.loop(0, top // 2)
        def _(p):
            q = r.Qs[i, pl.ds(2 * p, 2)].reshape(256, 128)
            cols = cut(p, 256)
            s1 = nt(r.KK[nk : nk + 256, :], q)
            s1 = jnp.where(diag, s1, lowest)
            most = jnp.max(s1, axis=0, keepdims=True)
            if nk:
                s0 = nt(r.KK[0:nk, :], q)
                most = jnp.maximum(most, jnp.max(s0, axis=0, keepdims=True))
                p0 = jnp.exp(s0 - most)
            p1 = jnp.exp(s1 - most)
            tot = jnp.sum(p1, axis=0, keepdims=True)
            if nk:
                tot = tot + jnp.sum(p0, axis=0, keepdims=True)
            inv = 1.0 / tot
            p1 = (p1 * inv).astype(bf16)
            r.PT[start + nk : start + nk + 256, cols] = p1
            o = nn(r.VVT[:, nk : nk + 256], p1)
            if nk:
                p0 = (p0 * inv).astype(bf16)
                r.PT[start : start + nk, cols] = p0
                o = o + nn(r.VVT[:, 0:nk], p0)
            r.O[i, pl.ds(2 * p, 2)] = o.T.reshape(2, rb, 128)

    attend(0)
    attend(1)
    got(*w0_z)
    w0_x = send(r.W.at[0, :, :, x, c], r.W.at[0, :, :, x, c], over_x)
    w1_z = w_over_z(1)
    attend(2)
    g_y = send(r.go_in.at[:, 1 - y], r.GO.at[y], over_y)
    attend(3)
    for i in range(4, nb):
        attend(i)
    got(w0_x)
    w0_c = send(r.W.at[0, :, :, :, c], r.W.at[0, :, :, :, c], over_c)
    got(o_y)
    o_c = send(r.WO.at[1 - y, orows, :], r.WO.at[1 - y, orows, :], over_c)
    got(*w1_z)
    w1_x = send(r.W.at[1, :, :, x, c], r.W.at[1, :, :, x, c], over_x)
    l_o.wait()
    l_g.wait()
    got(o_c)
    got(g_y)

    def project(i):
        at = cut(i, rb)

        @pl.loop(0, rb // 16)
        def _(t):
            at = cut(t, 16)
            atr = pl.ds(pl.multiple_of(i * rb + t * 16, 16), 16)
            mine = [r.idl[i, k, at, :] for k in range(top)]
            vals = [r.gateb[i, k, at, :] * r.O[i, k, at, :] for k in range(top)]
            for g in range(groups):
                val = jnp.zeros((16, 128), f32)
                for k in range(top):
                    val = jnp.where(mine[k] == 2 * g, vals[k], val)
                r.gated[atr, pl.ds(128 * g, 128)] = val.astype(bf16)

        valid = valid_rows(i)
        att = nn(r.gated[at, 0:half], r.WO[0]) + nn(r.gated[at, half:fq], r.WO[1])
        row = r.tok[own(i)].astype(f32) + valid * att
        r.res[at, :] = row
        normed, inv = norm_rows(row)
        r.n2[at, :] = normed
        r.r2[at, :] = inv
        h = normed * r.gain2[...]
        r.h2[at, :] = h.astype(bf16)
        r.h2T[:, at] = h.T.astype(bf16)
        for s in range(2):
            side = pl.ds(s * (width // 2), width // 2)
            g = valid * r.GO[s, i].astype(f32)
            r.gf[at, side] = g.astype(bf16)
            r.gfT[side, at] = g.T.astype(bf16)

    pl.loop(0, nb)(project)

    c0 = 0.7978845608028654
    c1 = 0.044715

    def feed(j, e):
        first = j == 0 and e == 0

        @pl.loop(0, nb)
        def _(i):
            at = cut(i, rb)
            w1 = r.W[j, e, :, :, :, :, 0:ch].reshape(width, ch)
            w2 = r.W[j, e, :, :, :, :, ch : 2 * ch].reshape(width, ch)
            v = nn(r.h2[at, :], w1)
            ga = nn(r.gf[at, :], w2)
            vv = v * v
            t = jnp.tanh(v * (c0 + (c0 * c1) * vv))
            hp = 0.5 + 0.5 * t
            act = (v * hp).astype(bf16)
            slope = hp + (0.5 * v) * (1.0 - t * t) * (c0 + (3 * c0 * c1) * vv)
            gi = (slope * ga).astype(bf16)
            r.actS[at, :] = act
            r.giS[at, :] = gi
            a = nt(act, w2)
            b = nt(gi, w1)
            if not first:
                a = a + r.acc[at, :]
                b = b + r.gh2[at, :]
            r.acc[at, :] = a
            r.gh2[at, :] = b

        shape = (nz, 2, 2, shard, ch)
        r.F[j, e, :, :, :, :, 0:ch] = nn(r.h2T[...], r.giS[...]).astype(bf16).reshape(shape)
        r.F[j, e, :, :, :, :, ch : 2 * ch] = (
            nn(r.gfT[...], r.actS[...]).astype(bf16).reshape(shape)
        )
        return send(r.F.at[j, e, :, :, 1 - c], r.FC.at[j, e], over_c)

    def f_add_c(j, e):
        @pl.loop(0, 2 * nz)
        def _(t):
            a, b = t // 2, t % 2
            r.F[j, e, a, b, c] = r.F[j, e, a, b, c] + r.FC[j, e, a, b]

    got(w0_c)
    f00 = feed(0, 0)
    got(w1_x)
    w1_c = send(r.W.at[1, :, :, :, c], r.W.at[1, :, :, :, c], over_c)
    f01 = feed(0, 1)
    got(f00)
    f_add_c(0, 0)
    got(f01)
    f_add_c(0, 1)
    f0_y = send(r.F.at[0, 1 - y, :, :, c], r.FY0, over_y)
    got(w1_c)
    f10 = feed(1, 0)
    f11 = feed(1, 1)
    got(f10)
    f_add_c(1, 0)
    got(f11)
    f_add_c(1, 1)
    f1_x = send(r.F.at[1, :, :, 1 - x, c], r.FX1, over_x)

    r.gain_rows[...] = jnp.zeros_like(r.gain_rows)

    def turn(i):
        at = cut(i, rb)
        valid = valid_rows(i)
        outs = (r.res[at, :] + valid * r.acc[at, :]).astype(bf16)
        mine, other = outs[:, : width // 2], outs[:, width // 2 :]
        low = y == 0
        r.out[i, y] = jnp.where(low, mine, other)
        r.outx[i] = jnp.where(low, other, mine)
        u, normed = r.gh2[at, :], r.n2[at, :]
        r.gain_rows[1:2, :] += jnp.sum(u * normed, axis=0, keepdims=True)
        back = norm_back(u, normed, r.r2[at, :], r.gain2[...])
        go = jnp.concatenate((r.GO[0, i], r.GO[1, i]), axis=1).astype(f32)
        gr = go + back
        r.res[at, :] = gr
        ga = (valid * gr).astype(bf16)
        r.gatt[at, :] = ga
        for e in range(2):
            r.wide[:, e * half : (e + 1) * half] = nt(ga, r.WO[e])

        @pl.loop(0, rb // 16)
        def _(t):
            at = cut(t, 16)
            atr = pl.ds(pl.multiple_of(i * rb + t * 16, 16), 16)
            parts = [r.wide[at, pl.ds(128 * g, 128)] for g in range(groups)]
            ln = lanes((16, 128))
            hf = (ln >= 64).astype(jnp.int32)
            gd = jnp.zeros((16, 128), f32)
            for k in range(top):
                mine = r.idl[i, k, at, :]
                val = jnp.zeros((16, 128), f32)
                for g in range(groups):
                    val = jnp.where(mine == 2 * g, parts[g], val)
                dot = jnp.sum(val * r.O[i, k, at, :], axis=-1, keepdims=True)
                gd = jnp.where(mine + hf == ln, dot, gd)
                r.dOs[i, k, at, :] = (r.gateb[i, k, at, :] * val).astype(bf16)
            dn = r.dense[atr, :]
            gs = dn * (gd - jnp.sum(dn * gd, axis=-1, keepdims=True))
            r.glog[atr, :] = gs.astype(bf16)

    pl.loop(0, nb)(turn)
    out_y = send(r.outx, r.out.at[:, y], over_y)

    woc = r.P.shape[4]
    for e in range(2):
        r.P[e] = (
            tn(r.gated[:, e * half : (e + 1) * half], r.gatt[...])
            .astype(bf16)
            .reshape(nz, 2, 2, woc, width)
        )
    p_c = send(r.P.at[:, :, :, 1 - c], r.PC, over_c)

    r.gK[...] = jnp.zeros_like(r.gK)
    r.gV[...] = jnp.zeros_like(r.gV)

    def back(i):
        nk = 256 * (i + 1)
        start = 128 * i * (i + 1)

        @pl.loop(0, top // 2)
        def _(p):
            do = r.dOs[i, pl.ds(2 * p, 2)].reshape(256, 128)
            cols = cut(p, 256)
            dp = nt(r.VV[0:nk, :], do)
            pr = r.PT[start : start + nk, cols].astype(f32)
            s = jnp.sum(pr * dp, axis=0, keepdims=True)
            ds = (pr * (dp - s)).astype(bf16)
            r.DS[0:nk, cols] = ds
            dq = nn(r.KKT[:, 0:nk], ds)
            r.dQ[pl.ds(2 * p, 2)] = dq.T.reshape(2, rb, 128)

        r.gK[0:nk, :] += nn(r.DS[0:nk, :], r.Qs[i].reshape(top * rb, 128))
        r.gV[0:nk, :] += nn(r.PT[start : start + nk, :], r.dOs[i].reshape(top * rb, 128))

        @pl.loop(0, rb // 16)
        def _(t):
            at = cut(t, 16)
            atr = pl.ds(pl.multiple_of(i * rb + t * 16, 16), 16)
            mine = [r.idl[i, k, at, :] for k in range(top)]
            vals = [r.dQ[k, at, :] for k in range(top)]
            for g in range(groups):
                val = jnp.zeros((16, 128), f32)
                for k in range(top):
                    val = jnp.where(mine[k] == 2 * g, vals[k], val)
                r.gq[atr, pl.ds(128 * g, 128)] = val.astype(bf16) * 0.125

    back(0)
    got(p_c)

    @pl.loop(0, 4 * nz)
    def _(t):
        e, a, b = t // (2 * nz), (t // 2) % nz, t % 2
        r.P[e, a, b, c] = r.P[e, a, b, c] + r.PC[e, a, b]

    p_x = send(r.P.at[:, :, 1 - x, c], r.PX, over_x)
    back(1)
    got(f0_y)

    @pl.loop(0, 2 * nz)
    def _(t):
        a, b = t // 2, t % 2
        r.F[0, y, a, b, c] = r.F[0, y, a, b, c] + r.FY0[a, b]

    f0_x = send(r.F.at[0, y, :, 1 - x, c], r.FX0, over_x)
    back(2)
    got(f1_x)

    @pl.loop(0, 2 * nz)
    def _(t):
        e, a = t // nz, t % nz
        r.F[1, e, a, x, c] = r.F[1, e, a, x, c] + r.FX1[e, a]

    f1_z = [send(r.F.at[1, :, k, x, c], r.FZ1.at[i], to) for i, (k, to) in enumerate(zip(zs, over_z))]
    got(p_x)

    @pl.loop(0, 2 * nz)
    def _(t):
        e, a = t // nz, t % nz
        r.P[e, a, x, c] = r.P[e, a, x, c] + r.PX[e, a]

    p_y = send(r.P.at[1 - y, :, x, c], r.PY, over_y)
    back(3)
    for i in range(4, nb):
        back(i)

    @pl.loop(0, nb)
    def _(i):
        for s in range(2):
            at = pl.ds(pl.multiple_of((2 * i + s) * rb, rb), rb)
            a, b = r.gK[at, :], r.gV[at, :]
            a = a + pltpu.roll(a, 64, 1)
            b = b + pltpu.roll(b, 64, 1)
            r.kvs[i, s] = jnp.where(lane < 64, a, b).astype(bf16)

    kv_y = send(r.kvs.at[:, 1 - y], r.kvr, over_y)
    for e in range(2):
        r.Q[e] = (
            nn(r.h1T[...], r.gq[:, e * half : (e + 1) * half])
            .astype(bf16)
            .reshape(nz, 2, 2, shard, half)
        )
    q_c2 = send(r.Q.at[:, :, :, 1 - c], r.QC, over_c)
    got(f0_x)

    @pl.loop(0, nz)
    def _(a):
        r.F[0, y, a, x, c] = r.F[0, y, a, x, c] + r.FX0[a]

    f0_z = [send(r.F.at[0, y, k, x, c], r.FZ0.at[i], to) for i, (k, to) in enumerate(zip(zs, over_z))]
    got(q_c2)

    @pl.loop(0, 4 * nz)
    def _(t):
        e, a, b = t // (2 * nz), (t // 2) % nz, t % 2
        r.Q[e, a, b, c] = r.Q[e, a, b, c] + r.QC[e, a, b]

    q_x = send(r.Q.at[:, :, 1 - x, c], r.QX, over_x)

    got(kv_y)

    def finish(i):
        at = cut(i, rb)
        low = (r.kvs[i, y].astype(f32) + r.kvr[i].astype(f32)).astype(bf16)
        r.kvr[i] = low
        g = nt(low, r.wkvg[...].reshape(width, 128)) + nt(r.glog[at, :], r.wr[...])
        for e in range(2):
            g = g + nt(r.gq[at, e * half : (e + 1) * half], r.WQ[e])
        normed, inv = norm_rows(r.tok[own(i)].astype(f32))
        r.gain_rows[0:1, :] += jnp.sum(g * normed, axis=0, keepdims=True)
        r.gt[i, y] = (r.res[at, :] + norm_back(g, normed, inv, r.gain1[...])).astype(bf16)

    pl.loop(0, nb)(finish)
    gt_y = send(r.gt.at[:, y], r.gt.at[:, y], over_y)

    r.K[...] = nn(r.h1T[...], r.kvr[...].reshape(nb * rb, 128)).reshape(nz, 2, 2, shard, 128)
    k_c = send(r.K.at[:, :, 1 - c], r.KC, over_c)
    routed = jnp.zeros((128, width), f32)
    for i in range(nb):
        routed = routed + tn(r.glog[i * rb : (i + 1) * rb, :], r.h1[own(i)])
    r.S[0] = routed[0:32]
    r.S[0, 30:32, :] = r.gain_rows[...]
    s_c = send(r.S.at[0], r.SR.at[0], over_c)

    got(k_c)

    @pl.loop(0, 2 * nz)
    def _(t):
        a, b = t // 2, t % 2
        r.K[a, b, c] = r.K[a, b, c] + r.KC[a, b]

    k_x = send(r.K.at[:, 1 - x, c], r.KX, over_x)
    got(s_c)
    r.S[1] = r.S[0] + r.SR[0]
    s_x = send(r.S.at[1], r.SR.at[1], over_x)

    got(p_y)

    @pl.loop(0, nz)
    def _(a):
        r.P[y, a, x, c] = r.P[y, a, x, c] + r.PY[a]

    p_z = [send(r.P.at[y, k, x, c], r.PZ.at[i], to) for i, (k, to) in enumerate(zip(zs, over_z))]
    got(*f1_z)
    for e in range(2):
        v = r.F[1, e, z, x, c].astype(f32)
        for k in range(nz - 1):
            v = v + r.FZ1[k, e].astype(f32)
        r.F[1, e, z, x, c] = v.astype(bf16)
    f1_y = send(r.F.at[1, 1 - y, z, x, c], r.FY1, over_y)
    got(k_x)

    @pl.loop(0, nz)
    def _(a):
        r.K[a, x, c] = r.K[a, x, c] + r.KX[a]

    k_z = [send(r.K.at[k, x, c], r.KZ.at[i], to) for i, (k, to) in enumerate(zip(zs, over_z))]
    got(s_x)
    r.S[2] = r.S[1] + r.SR[1]
    s_y = send(r.S.at[2], r.SR.at[2], over_y)
    got(*f0_z)
    v = r.F[0, y, z, x, c].astype(f32)
    for k in range(nz - 1):
        v = v + r.FZ0[k].astype(f32)
    r.gwh[:, 0:ch] = v[:, 0:ch]
    r.gwT[:, 0:ch] = v[:, ch : 2 * ch]

    got(q_x)

    @pl.loop(0, 2 * nz)
    def _(t):
        e, a = t // nz, t % nz
        r.Q[e, a, x, c] = r.Q[e, a, x, c] + r.QX[e, a]

    q_y2 = send(r.Q.at[1 - y, :, x, c], r.QY, over_y)
    got(*p_z)
    v = r.P[y, z, x, c].astype(f32)
    for k in range(nz - 1):
        v = v + r.PZ[k].astype(f32)
    r.PA[z, x, c] = v.astype(bf16)
    pa_z = [send(r.PA.at[z, x, c], r.PA.at[z, x, c], to) for to in over_z]
    got(*k_z)
    v = r.K[z, x, c]
    for k in range(nz - 1):
        v = v + r.KZ[k]
    r.KY[0] = v
    k_y = send(r.KY.at[0], r.KY.at[1], over_y)
    got(s_y)
    r.S[3] = r.S[2] + r.SR[2]
    r.SZ[z] = r.S[3]
    s_z = [send(r.S.at[3], r.SZ.at[z], to) for to in over_z]
    got(f1_y)
    v = r.F[1, y, z, x, c].astype(f32) + r.FY1[...].astype(f32)
    r.gwh[:, ch : 2 * ch] = v[:, 0:ch]
    r.gwT[:, ch : 2 * ch] = v[:, ch : 2 * ch]
    got(*pa_z)
    pa_x = send(r.PA.at[:, x, c], r.PA.at[:, x, c], over_x)
    got(q_y2)

    @pl.loop(0, nz)
    def _(a):
        r.Q[y, a, x, c] = r.Q[y, a, x, c] + r.QY[a]

    q_z = [send(r.Q.at[y, k, x, c], r.QZ.at[i], to) for i, (k, to) in enumerate(zip(zs, over_z))]
    got(k_y)
    r.gkv[...] = r.KY[0] + r.KY[1]
    got(*s_z)
    v = r.SZ[0]
    for k in range(1, nz):
        v = v + r.SZ[k]
    r.small[...] = v
    got(*q_z)
    v = r.Q[y, z, x, c].astype(f32)
    for k in range(nz - 1):
        v = v + r.QZ[k].astype(f32)
    r.QA[z, x, c] = v.astype(bf16)
    qa_z = [send(r.QA.at[z, x, c], r.QA.at[z, x, c], to) for to in over_z]
    got(pa_x)
    pa_c = send(r.PA.at[:, :, c], r.PA.at[:, :, c], over_c)
    got(*qa_z)
    qa_x = send(r.QA.at[:, x, c], r.QA.at[:, x, c], over_x)
    got(pa_c)

    @pl.loop(0, 4 * nz)
    def _(t):
        at = cut(t, woc)
        r.gwo[at, :] = r.PA[t // 4, (t // 2) % 2, t % 2].astype(f32)

    got(qa_x)
    qa_c = send(r.QA.at[:, :, c], r.QA.at[:, :, c], over_c)
    got(qa_c)

    @pl.loop(0, 4 * nz)
    def _(t):
        at = cut(t, shard)
        r.gwq[at, :] = r.QA[t // 4, (t // 2) % 2, t % 2].astype(f32)

    got(out_y, gt_y)
    for copy in sent:
        copy.wait_send()


def shards(
    tokens, gain_attn, w_key, w_value, w_router, w_query, w_out, gain_ffn,
    w_hidden, w_output, expert_ids, lengths, grad_out,
):
    rows, width = tokens.shape
    dp = lax.axis_size("dp")
    inner = min(dp, 16)
    outer = dp // inner
    nz = inner // 4
    nb = rows // rb // 2
    top = expert_ids.shape[1]
    n_experts = w_router.shape[1]
    hd = w_key.shape[1]
    half = w_query.shape[1]
    ffh = w_hidden.shape[1]
    ch = ffh // 2
    near = [[g * outer + k for k in range(outer)] for g in range(inner)]
    wkv = jnp.concatenate((w_key, w_value), 1)
    wt = w_output.T
    w_in = jnp.stack(
        [
            jnp.concatenate((w_hidden[:, :ch], wt[:, :ch]), 1),
            jnp.concatenate((w_hidden[:, ch:], wt[:, ch:]), 1),
        ]
    )
    if outer > 1:
        wkv = lax.all_gather(wkv, "dp", axis=0, tiled=True, axis_index_groups=near)
        w_in = lax.all_gather(w_in, "dp", axis=1, tiled=True, axis_index_groups=near)
    wr = jnp.pad(w_router, ((0, 0), (0, 128 - n_experts)))
    shard = width // inner
    sds = jax.ShapeDtypeStruct
    spec = scratch(rows, width, nb, top, 2 * half, 2 * ffh, nz, shard)
    names = in_names + out_names + list(spec)
    vmem = pl.BlockSpec(memory_space=pltpu.VMEM)
    anyw = pl.BlockSpec(memory_space=pl.ANY)
    out, gt, gwq, gwo, gwh, gwT, gkv, small = pl.pallas_call(
        functools.partial(kernel, names, outer),
        out_shape=(
            sds((nb, 2, rb, width // 2), bf16),
            sds((nb, 2, rb, width), bf16),
            sds((width, half), f32),
            sds((half, width), f32),
            sds((shard, ffh), f32),
            sds((shard, ffh), f32),
            sds((shard, 128), f32),
            sds((32, width), f32),
        ),
        in_specs=[pl.BlockSpec(memory_space=pltpu.SMEM)] + [vmem] * 5 + [anyw] * 5,
        out_specs=[vmem] * 8,
        scratch_shapes=list(spec.values()),
        compiler_params=pltpu.CompilerParams(
            collective_id=0, has_side_effects=True, vmem_limit_bytes=63 * 2**20
        ),
    )(
        lengths, tokens.reshape(2 * nb, rb, width), gain_attn[None], wr, gain_ffn[None],
        expert_ids.reshape(2 * nb, rb, top), wkv, w_query, w_out, w_in,
        grad_out.reshape(nb, 2, rb, width // 2),
    )
    if outer > 1:
        gwq, gwo, small = lax.psum((gwq, gwo, small), "dp", axis_index_groups=near)
        gwh, gwT, gkv = (
            lax.psum_scatter(v, "dp", scatter_dimension=0, tiled=True, axis_index_groups=near)
            for v in (gwh, gwT, gkv)
        )
    return (
        out.reshape(rows, width // 2), gt.reshape(rows, width), gkv[:, :hd], gkv[:, hd:],
        small[:n_experts].T, gwq, gwo, gwh, gwT.T, small[30], small[31],
    )


def solution(mesh):
    placed = (
        P("dp", None), P(), P("dp", None), P("dp", None), P(), P(None, "expert"),
        P("expert", None), P(), P("dp", "expert"), P("expert", "dp"), P("dp", None),
        P("dp"), P("dp", "expert"),
    )
    return jax.shard_map(
        shards,
        mesh=mesh,
        in_specs=placed,
        out_specs=(
            P("dp", "expert"), P("dp", None), P("dp", None), P("dp", None), P(),
            P(None, "expert"), P("expert", None), P("dp", "expert"), P("expert", "dp"),
            P(), P(),
        ),
        check_vma=False,
    )
```

```python
import functools

import jax
import jax.numpy as jnp
from jax import lax
from jax.experimental import pallas as pl
from jax.experimental.pallas import tpu as pltpu
from jax.sharding import PartitionSpec as P

f32 = jnp.float32
bf16 = jnp.bfloat16
eps = 1e-05
lowest = -1e30
rb = 128


def nn(left, right):
    return jnp.dot(left, right, preferred_element_type=f32)


def nt(left, right):
    return lax.dot_general(left, right, (((1,), (1,)), ((), ())), preferred_element_type=f32)


def tn(left, right):
    return lax.dot_general(left, right, (((0,), (0,)), ((), ())), preferred_element_type=f32)


def norm_rows(x):
    centred = x - jnp.mean(x, axis=-1, keepdims=True)
    inv = lax.rsqrt(jnp.mean(centred * centred, axis=-1, keepdims=True) + eps)
    return centred * inv, inv


def norm_back(u, normed, inv, gain):
    w = u * gain
    return inv * (
        w
        - jnp.mean(w, axis=-1, keepdims=True)
        - normed * jnp.mean(w * normed, axis=-1, keepdims=True)
    )


def lanes(shape):
    return lax.broadcasted_iota(jnp.int32, shape, len(shape) - 1)


MESH = pl.DeviceIdType.MESH

in_names = [
    "len_ref",
    "tok",
    "gain1",
    "wrt",
    "gain2",
    "idst",
    "wk_in",
    "wv_in",
    "wq_in",
    "wo_in",
    "wh_in",
    "wt_in",
    "go_in",
]
out_names = [
    "out",
    "gt",
    "QA",
    "PA",
    "gwh",
    "gwT",
    "gkv",
    "small",
]


def scratch(rows, width, nb, top, fq, ff, nz, shard):
    vm = pltpu.VMEM
    own = rows // 2
    half = fq // 2
    total = 128 * nb * (nb + 1)
    ring = (nz, 2, 2)
    ch = ff // 4
    woc = half // (4 * nz)
    return {
        "wkvg": vm(ring + (shard, 128), bf16),
        "W": vm((2, 2) + ring + (shard, 2 * ch), bf16),
        "WQ": vm((2, width, half), bf16),
        "WO": vm((2, half, width), bf16),
        "GO": vm((2, nb, rb, width // 2), bf16),
        "h1": vm((2 * nb, rb, width), bf16),
        "h1T": vm((width, own), bf16),
        "KK": vm((rows, 128), bf16),
        "VV": vm((rows, 128), bf16),
        "KKT": vm((128, rows), bf16),
        "VVT": vm((128, rows), bf16),
        "idl": vm((nb, top, rb, 128), jnp.int32),
        "gateb": vm((nb, top, rb, 128), f32),
        "dense": vm((own, 128), f32),
        "Qs": vm((nb, top, rb, 128), bf16),
        "PT": vm((total, top * rb), bf16),
        "O": vm((nb, top, rb, 128), f32),
        "wide": vm((rb, fq), f32),
        "gated": vm((own, fq), bf16),
        "n2": vm((own, width), f32),
        "r2": vm((own, 1), f32),
        "res": vm((own, width), f32),
        "h2": vm((own, width), bf16),
        "h2T": vm((width, own), bf16),
        "gfT": vm((width, own), bf16),
        "gf": vm((own, width), bf16),
        "gh2": vm((own, width), f32),
        "acc": vm((own, width), f32),
        "gatt": vm((own, width), bf16),
        "dOs": vm((nb, top, rb, 128), bf16),
        "glog": vm((own, 128), bf16),
        "AG": vm((own, 2 * ch), bf16),
        "wrp": vm((128, width), bf16),
        "gK": vm((rows, 128), f32),
        "gV": vm((rows, 128), f32),
        "dQ": vm((top, rb, 128), f32),
        "gain_rows": vm((2, width), f32),
        "outx": vm((nb, rb, width // 2), bf16),
        "kvs": vm((nb, 2, rb, 128), bf16),
        "kvr": vm((nb, rb, 128), bf16),
        "F": vm((2, 2) + ring + (shard, 2 * ch), bf16),
        "FC": vm((2, 2, nz, 2, shard, 2 * ch), bf16),
        "FY0": vm((nz, 2, shard, 2 * ch), bf16),
        "FZ0": vm((nz - 1, 2, shard, 2 * ch), bf16),
        "FX0": vm((shard, 2 * ch), bf16),
        "FX1": vm((2, nz, shard, 2 * ch), bf16),
        "FY1": vm((nz, shard, 2 * ch), bf16),
        "FZ1": vm((nz - 1, shard, 2 * ch), bf16),
        "QC": vm((2, nz, 2, shard, half), bf16),
        "QXA": vm((2, nz, shard, half // 2), bf16),
        "QYA": vm((nz, shard, half // 2), bf16),
        "QYB": vm((nz, 2, shard, half // 2), bf16),
        "QXB": vm((nz, shard, half // 2), bf16),
        "QZ": vm((nz - 1, shard, half), bf16),
        "P": vm((2,) + ring + (woc, width), bf16),
        "PC": vm((2, nz, 2, woc, width), bf16),
        "PX": vm((2, nz, woc, width), bf16),
        "PY": vm((nz, woc, width), bf16),
        "PZ": vm((nz - 1, woc, width), bf16),
        "K": vm(ring + (shard, 128), f32),
        "KC": vm((nz, 2, shard, 128), f32),
        "KX": vm((nz, shard, 128), f32),
        "KZ": vm((nz - 1, shard, 128), f32),
        "KY": vm((2, shard, 128), f32),
        "S": vm((4, 32, width), f32),
        "SR": vm((3, 32, width), f32),
        "SZ": vm((nz, 32, width), f32),
        "send": pltpu.SemaphoreType.DMA((96,)),
        "recv": pltpu.SemaphoreType.DMA((96,)),
        "local": pltpu.SemaphoreType.DMA((8,)),
    }


class Refs:
    pass


def kernel(names, outer, *refs):
    r = Refs()
    for name, ref in zip(names, refs):
        setattr(r, name, ref)
    nb = r.tok.shape[0] // 2
    width = r.tok.shape[2]
    top = r.idst.shape[0]
    fq = r.gated.shape[1]
    half = fq // 2
    groups = fq // 128
    r.gq = r.gated
    r.Q = r.W.at[0, :, :, :, :, :, 0:half]
    r.actS = r.AG.at[:, 0 : r.W.shape[6] // 2]
    r.giS = r.AG.at[:, r.W.shape[6] // 2 : r.W.shape[6]]
    nz = r.W.shape[2]
    ch = r.W.shape[6] // 2
    shard = r.W.shape[5]
    d = lax.axis_index("dp")
    y = lax.axis_index("expert")
    n, m = d // outer, d % outer
    z, x, c = n // 4, (n // 2) % 2, n % 2
    length = r.len_ref[0]

    def device(z, x, c, y):
        return ((z * 4 + x * 2 + c) * outer + m, y)

    over_c = device(z, x, 1 - c, y)
    over_x = device(z, 1 - x, c, y)
    over_y = device(z, x, c, 1 - y)
    zs = [(z + k) % nz for k in range(1, nz)]
    over_z = [device(k, x, c, y) for k in zs]
    used = [0]
    sent = []

    def send(source, target, to):
        k = used[0]
        used[0] += 1
        copy = pltpu.make_async_remote_copy(
            src_ref=source, dst_ref=target, send_sem=r.send.at[k], recv_sem=r.recv.at[k],
            device_id=to, device_id_type=MESH,
        )
        copy.start()
        sent.append(copy)
        return copy

    def here(k, source, target):
        copy = pltpu.make_async_copy(source, target, r.local.at[k])
        copy.start()
        return copy

    def got(*copies):
        for copy in copies:
            copy.wait_recv()

    def own(i):
        return 2 * i + y

    def cut(i, size):
        return pl.ds(pl.multiple_of(i * size, size), size)

    def valid_rows(i):
        return (rb * own(i) + lax.broadcasted_iota(jnp.int32, (rb, 1), 0) < length).astype(f32)

    l_w = [
        here(2 * j + k, ref.at[:, j * ch : (j + 1) * ch],
             r.W.at[j, y, z, x, c, :, k * ch : (k + 1) * ch])
        for j in range(2)
        for k, ref in enumerate((r.wh_in, r.wt_in))
    ]
    l_q = here(4, r.wq_in, r.WQ.at[y])
    l_o = here(5, r.wo_in, r.WO.at[y])
    l_g = here(6, r.go_in.at[:, y], r.GO.at[y])
    r.wkvg[z, x, c] = jnp.concatenate((r.wk_in[...], r.wv_in[...]), axis=1)
    barrier = pltpu.get_barrier_semaphore()
    peers = [over_c, over_x, over_y] + over_z
    for peer in peers:
        pl.semaphore_signal(barrier, inc=1, device_id=peer, device_id_type=MESH)
    pl.semaphore_wait(barrier, len(peers))
    kv_c = send(r.wkvg.at[z, x, c], r.wkvg.at[z, x, c], over_c)
    for copy in l_w:
        copy.wait()
    w_y = send(r.W.at[:, y, z, x, c], r.W.at[:, y, z, x, c], over_y)
    qrows = cut(c, width // 2)
    q_y = send(r.wq_in.at[qrows, :], r.WQ.at[y, qrows, :], over_y)
    spare = jnp.zeros((128 - r.wrt.shape[0], width), f32)
    r.wrp[...] = jnp.concatenate((r.wrt[...].astype(f32), spare), axis=0).astype(bf16)

    def w_part(k):
        return r.W.at[k // 2, :, :, :, :, :, pl.ds((k % 2) * ch, ch)]

    def w_over_z(k, both=False):
        view = w_part(k).at[:, z, :, c] if both else w_part(k).at[:, z, x, c]
        return [send(view, view, to) for to in over_z]

    def w_over_x(k, line=True):
        view = w_part(k).at[:, :, x, c] if line else w_part(k).at[:, z, x, c]
        return send(view, view, over_x)

    def w_over_c(k):
        view = w_part(k).at[:, :, :, c]
        return send(view, view, over_c)
    @pl.loop(0, 2 * nb)
    def _(b):
        normed, _ = norm_rows(r.tok[b].astype(f32))
        r.h1[b] = (normed * r.gain1[...]).astype(bf16)
    got(kv_c)
    kv_x = send(r.wkvg.at[z, x], r.wkvg.at[z, x], over_x)
    got(w_y)
    w0_z = w_over_z(0)
    w3_x = w_over_x(3, False)

    lane = lanes((rb, 128))
    upper = (lane >= 64).astype(jnp.int32)

    def gates(i):
        h = r.h1[own(i)]
        at = cut(i, rb)
        r.h1T[:, at] = h.astype(f32).T.astype(bf16)
        logits = nt(h, r.wrp[...])
        ids = r.idst[:, cut(own(i), rb)].astype(f32).T.astype(jnp.int32)
        spread = [jnp.broadcast_to(ids[:, k : k + 1], (rb, 128)) for k in range(top)]
        chosen = lane == spread[0]
        for k in range(1, top):
            chosen = chosen | (lane == spread[k])
        most = jnp.max(jnp.where(chosen, logits, lowest), axis=-1, keepdims=True)
        e = jnp.where(chosen, jnp.exp(jnp.where(chosen, logits - most, 0.0)), 0.0)
        g = e / jnp.sum(e, axis=-1, keepdims=True)
        r.dense[at, :] = g
        for k in range(top):
            gk = jnp.sum(jnp.where(lane == spread[k], g, 0.0), axis=-1, keepdims=True)
            r.gateb[i, k] = jnp.broadcast_to(gk, (rb, 128))
            r.idl[i, k] = spread[k] - upper

    pl.loop(0, nb // 2)(gates)
    got(kv_x)
    kv_z = [send(r.wkvg.at[z], r.wkvg.at[z], to) for to in over_z]
    pl.loop(nb // 2, nb)(gates)
    got(*kv_z)

    @pl.loop(0, 2 * nb)
    def _(b):
        kv = nn(r.h1[b], r.wkvg[...].reshape(width, 128))
        at = cut(b, rb)
        swapped = pltpu.roll(kv, 64, 1)
        k2 = jnp.where(lane < 64, kv, swapped)
        v2 = jnp.where(lane < 64, swapped, kv)
        r.KK[at, :] = k2.astype(bf16)
        r.VV[at, :] = v2.astype(bf16)
        r.KKT[:, at] = k2.T.astype(bf16)
        r.VVT[:, at] = v2.T.astype(bf16)
    got(*w0_z)
    w0_x = w_over_x(0)
    w1_z = w_over_z(1)
    got(q_y)
    q_c = send(r.WQ.at[1 - y, qrows, :], r.WQ.at[1 - y, qrows, :], over_c)
    orows = cut(c, half // 2)
    o_y = send(r.wo_in.at[orows, :], r.WO.at[y, orows, :], over_y)
    g_y = send(r.go_in.at[:, 1 - y], r.GO.at[y], over_y)
    l_q.wait()
    got(q_c)
    @pl.loop(0, nb)
    def _(i):
        h = r.h1[own(i)]
        for e in range(2):
            r.wide[:, e * half : (e + 1) * half] = 0.125 * nn(h, r.WQ[e])

        @pl.loop(0, rb // 16)
        def _(t):
            at = cut(t, 16)
            parts = [r.wide[at, pl.ds(128 * g, 128)] for g in range(groups)]
            for k in range(top):
                mine = r.idl[i, k, at, :]
                val = jnp.zeros((16, 128), f32)
                for g in range(groups):
                    val = jnp.where(mine == 2 * g, parts[g], val)
                r.Qs[i, k, at, :] = val.astype(bf16)
    diag = lax.broadcasted_iota(jnp.int32, (256, 256), 0) <= rb * y + lanes((256, 256)) % 128

    def attend(i):
        nk = 256 * i
        start = 128 * i * (i + 1)

        @pl.loop(0, top // 2, unroll=4)
        def _(p):
            q = r.Qs[i, pl.ds(2 * p, 2)].reshape(256, 128)
            cols = cut(p, 256)
            s1 = nt(r.KK[nk : nk + 256, :], q)
            s1 = jnp.where(diag, s1, lowest)
            most = jnp.max(s1, axis=0, keepdims=True)
            if nk:
                s0 = nt(r.KK[0:nk, :], q)
                most = jnp.maximum(most, jnp.max(s0, axis=0, keepdims=True))
                p0 = jnp.exp(s0 - most)
            p1 = jnp.exp(s1 - most)
            tot = jnp.sum(p1, axis=0, keepdims=True)
            if nk:
                tot = tot + jnp.sum(p0, axis=0, keepdims=True)
            inv = 1.0 / tot
            p1 = (p1 * inv).astype(bf16)
            r.PT[start + nk : start + nk + 256, cols] = p1
            o = nn(r.VVT[:, nk : nk + 256], p1)
            if nk:
                p0 = (p0 * inv).astype(bf16)
                r.PT[start : start + nk, cols] = p0
                o = o + nn(r.VVT[:, 0:nk], p0)
            r.O[i, pl.ds(2 * p, 2)] = o.T.reshape(2, rb, 128)

    attend(0)
    got(*w1_z)
    w1_x = w_over_x(1)
    w2_z = w_over_z(2)
    attend(1)
    attend(2)
    got(w0_x)
    w0_c = w_over_c(0)
    got(*w2_z)
    w2_x = w_over_x(2)
    got(w3_x)
    w3_z = w_over_z(3, True)
    for i in range(3, nb):
        attend(i)
    got(o_y)
    o_c = send(r.WO.at[1 - y, orows, :], r.WO.at[1 - y, orows, :], over_c)
    got(w1_x)
    w1_c = w_over_c(1)
    l_o.wait()
    l_g.wait()
    got(o_c)
    got(g_y)
    def project(i):
        at = cut(i, rb)

        @pl.loop(0, rb // 16)
        def _(t):
            at = cut(t, 16)
            atr = pl.ds(pl.multiple_of(i * rb + t * 16, 16), 16)
            mine = [r.idl[i, k, at, :] for k in range(top)]
            vals = [r.gateb[i, k, at, :] * r.O[i, k, at, :] for k in range(top)]
            for g in range(groups):
                val = jnp.zeros((16, 128), f32)
                for k in range(top):
                    val = jnp.where(mine[k] == 2 * g, vals[k], val)
                r.gated[atr, pl.ds(128 * g, 128)] = val.astype(bf16)

        valid = valid_rows(i)
        att = nn(r.gated[at, 0:half], r.WO[0]) + nn(r.gated[at, half:fq], r.WO[1])
        row = r.tok[own(i)].astype(f32) + valid * att
        r.res[at, :] = row
        normed, inv = norm_rows(row)
        r.n2[at, :] = normed
        r.r2[at, :] = inv
        h = normed * r.gain2[...]
        r.h2[at, :] = h.astype(bf16)
        r.h2T[:, at] = h.T.astype(bf16)
        for s in range(2):
            side = pl.ds(s * (width // 2), width // 2)
            g = valid * r.GO[s, i].astype(f32)
            r.gf[at, side] = g.astype(bf16)
            r.gfT[side, at] = g.T.astype(bf16)

    pl.loop(0, nb)(project)

    c0 = 0.7978845608028654
    c1 = 0.044715

    def feed(j, e, first=False):

        w1 = r.W[j, e, :, :, :, :, 0:ch].reshape(width, ch)
        w2 = r.W[j, e, :, :, :, :, ch : 2 * ch].reshape(width, ch)
        for i in range(nb // 2):
            at = pl.ds(i * 256, 256)
            v = nn(r.h2[at, :], w1)
            ga = nn(r.gf[at, :], w2)
            vv = v * v
            hp = 0.5 + 0.5 * jnp.tanh(v * (c0 + (c0 * c1) * vv))
            act = v * hp
            slope = hp + act * (1.0 - hp) * (2 * c0 + (6 * c0 * c1) * vv)
            r.actS[at, :] = act.astype(bf16)
            r.giS[at, :] = (slope * ga).astype(bf16)
        a = nt(r.actS[...], w2)
        b = nt(r.giS[...], w1)
        if first:
            r.acc[...] = a
            r.gh2[...] = b
        else:
            r.acc[...] += a
            r.gh2[...] += b

        shape = (nz, 2, 2, shard, ch)
        r.F[j, e, :, :, :, :, 0:ch] = nn(r.h2T[...], r.giS[...]).astype(bf16).reshape(shape)
        r.F[j, e, :, :, :, :, ch : 2 * ch] = (
            nn(r.gfT[...], r.actS[...]).astype(bf16).reshape(shape)
        )
        return send(r.F.at[j, e, :, :, 1 - c], r.FC.at[j, e], over_c)

    def f_add_c(j, e):
        @pl.loop(0, 2 * nz)
        def _(t):
            a, b = t // 2, t % 2
            r.F[j, e, a, b, c] = r.F[j, e, a, b, c] + r.FC[j, e, a, b]
    got(w0_c, w1_c)
    f0p = feed(0, 1 - y, True)
    got(w2_x)
    w2_c = w_over_c(2)
    f0m = feed(0, y)
    got(f0p)
    f_add_c(0, 1 - y)
    f0_y = send(r.F.at[0, 1 - y, :, :, c], r.FY0, over_y)
    got(*w3_z)
    w3_c = w_over_c(3)
    got(f0m)
    f_add_c(0, y)
    got(w2_c, w3_c)
    f1p = feed(1, 1 - y)
    f1m = feed(1, y)
    got(f1p)
    f_add_c(1, 1 - y)
    f1_xa = send(r.F.at[1, 1 - y, :, 1 - x, c], r.FX1.at[0], over_x)
    r.gain_rows[...] = jnp.zeros_like(r.gain_rows)

    def turn(i):
        at = cut(i, rb)
        valid = valid_rows(i)
        outs = (r.res[at, :] + valid * r.acc[at, :]).astype(bf16)
        mine, other = outs[:, : width // 2], outs[:, width // 2 :]
        low = y == 0
        r.out[i, y] = jnp.where(low, mine, other)
        r.outx[i] = jnp.where(low, other, mine)
        u, normed = r.gh2[at, :], r.n2[at, :]
        r.gain_rows[1:2, :] += jnp.sum(u * normed, axis=0, keepdims=True)
        back = norm_back(u, normed, r.r2[at, :], r.gain2[...])
        go = jnp.concatenate((r.GO[0, i], r.GO[1, i]), axis=1).astype(f32)
        gr = go + back
        r.res[at, :] = gr
        ga = (valid * gr).astype(bf16)
        r.gatt[at, :] = ga
        for e in range(2):
            r.wide[:, e * half : (e + 1) * half] = nt(ga, r.WO[e])

        @pl.loop(0, rb // 16)
        def _(t):
            at = cut(t, 16)
            atr = pl.ds(pl.multiple_of(i * rb + t * 16, 16), 16)
            parts = [r.wide[at, pl.ds(128 * g, 128)] for g in range(groups)]
            ln = lanes((16, 128))
            hf = (ln >= 64).astype(jnp.int32)
            gd = jnp.zeros((16, 128), f32)
            for k in range(top):
                mine = r.idl[i, k, at, :]
                val = jnp.zeros((16, 128), f32)
                for g in range(groups):
                    val = jnp.where(mine == 2 * g, parts[g], val)
                dot = jnp.sum(val * r.O[i, k, at, :], axis=-1, keepdims=True)
                gd = jnp.where(mine + hf == ln, dot, gd)
                r.dOs[i, k, at, :] = (r.gateb[i, k, at, :] * val).astype(bf16)
            dn = r.dense[atr, :]
            gs = dn * (gd - jnp.sum(dn * gd, axis=-1, keepdims=True))
            r.glog[atr, :] = gs.astype(bf16)

    pl.loop(0, nb // 2)(turn)
    got(f1m)
    f_add_c(1, y)
    f1_xb = send(r.F.at[1, y, :, 1 - x, c], r.FX1.at[1], over_x)
    pl.loop(nb // 2, nb)(turn)
    out_y = send(r.outx, r.out.at[:, y], over_y)
    got(f0_y)

    @pl.loop(0, 2 * nz)
    def _(t):
        a, b = t // 2, t % 2
        r.F[0, y, a, b, c] = r.F[0, y, a, b, c] + r.FY0[a, b]

    f0_z = [
        send(r.F.at[0, y, k, :, c], r.FZ0.at[i], to) for i, (k, to) in enumerate(zip(zs, over_z))
    ]

    woc = r.P.shape[4]
    for e in range(2):
        r.P[e] = (
            tn(r.gated[:, e * half : (e + 1) * half], r.gatt[...])
            .astype(bf16)
            .reshape(nz, 2, 2, woc, width)
        )
    p_c = send(r.P.at[:, :, :, 1 - c], r.PC, over_c)
    r.gK[...] = jnp.zeros_like(r.gK)
    r.gV[...] = jnp.zeros_like(r.gV)

    def back(i):
        nk = 256 * (i + 1)
        start = 128 * i * (i + 1)
        r.gV[0:nk, :] += nn(r.PT[start : start + nk, :], r.dOs[i].reshape(top * rb, 128))

        @pl.loop(0, top // 2, unroll=4)
        def _(p):
            do = r.dOs[i, pl.ds(2 * p, 2)].reshape(256, 128)
            cols = cut(p, 256)
            dp = nt(r.VV[0:nk, :], do)
            pr = r.PT[start : start + nk, cols].astype(f32)
            s = jnp.sum(pr * dp, axis=0, keepdims=True)
            ds = (pr * (dp - s)).astype(bf16)
            r.PT[start : start + nk, cols] = ds
            dq = nn(r.KKT[:, 0:nk], ds)
            r.dQ[pl.ds(2 * p, 2)] = dq.T.reshape(2, rb, 128)

        @pl.loop(0, rb // 16)
        def _(t):
            at = cut(t, 16)
            atr = pl.ds(pl.multiple_of(i * rb + t * 16, 16), 16)
            mine = [r.idl[i, k, at, :] for k in range(top)]
            vals = [r.dQ[k, at, :] for k in range(top)]
            for g in range(groups):
                val = jnp.zeros((16, 128), f32)
                for k in range(top):
                    val = jnp.where(mine[k] == 2 * g, vals[k], val)
                r.gq[atr, pl.ds(128 * g, 128)] = val.astype(bf16) * 0.125

    back(0)
    got(p_c)

    @pl.loop(0, 4 * nz)
    def _(t):
        e, a, b = t // (2 * nz), (t // 2) % nz, t % 2
        r.P[e, a, b, c] = r.P[e, a, b, c] + r.PC[e, a, b]

    p_x = send(r.P.at[:, :, 1 - x, c], r.PX, over_x)
    back(1)
    got(f1_xa, f1_xb)

    @pl.loop(0, nz)
    def _(a):
        r.F[1, 1 - y, a, x, c] = r.F[1, 1 - y, a, x, c] + r.FX1[0, a]
        r.F[1, y, a, x, c] = r.F[1, y, a, x, c] + r.FX1[1, a]

    f1_y = send(r.F.at[1, 1 - y, :, x, c], r.FY1, over_y)
    back(2)
    got(*f0_z)
    for b in range(2):
        v = r.F[0, y, z, b, c].astype(f32)
        for k in range(nz - 1):
            v = v + r.FZ0[k, b].astype(f32)
        r.F[0, y, z, b, c] = v.astype(bf16)
    f0_x = send(r.F.at[0, y, z, 1 - x, c], r.FX0, over_x)
    got(p_x)

    @pl.loop(0, 2 * nz)
    def _(t):
        e, a = t // nz, t % nz
        r.P[e, a, x, c] = r.P[e, a, x, c] + r.PX[e, a]

    p_y = send(r.P.at[1 - y, :, x, c], r.PY, over_y)
    got(f1_y)

    @pl.loop(0, nz)
    def _(a):
        r.F[1, y, a, x, c] = r.F[1, y, a, x, c] + r.FY1[a]

    f1_z = [
        send(r.F.at[1, y, k, x, c], r.FZ1.at[i], to) for i, (k, to) in enumerate(zip(zs, over_z))
    ]
    for i in range(3, nb):
        back(i)
    for copy in [w_y, w3_x, w0_x, w1_x, w2_x, w0_c, w1_c, w2_c, w3_c, *w0_z, *w1_z, *w2_z, *w3_z]:
        copy.wait_send()
        sent[:] = [other for other in sent if other is not copy]
    for e in range(2):
        r.Q[e] = (
            nn(r.h1T[...], r.gq[:, e * half : (e + 1) * half])
            .astype(bf16)
            .reshape(nz, 2, 2, shard, half)
        )
    q_c2 = send(r.Q.at[:, :, :, 1 - c], r.QC, over_c)
    for i in range(nb):
        nk = 256 * (i + 1)
        start = 128 * i * (i + 1)
        r.gK[0:nk, :] += nn(r.PT[start : start + nk, :], r.Qs[i].reshape(top * rb, 128))
    got(q_c2)

    @pl.loop(0, 4 * nz)
    def _(t):
        e, a, b = t // (2 * nz), (t // 2) % nz, t % 2
        r.Q[e, a, b, c] = r.Q[e, a, b, c] + r.QC[e, a, b]

    one, two = pl.ds(0, half // 2), pl.ds(half // 2, half // 2)
    qa_x = send(r.Q.at[:, :, 1 - x, c, :, one], r.QXA, over_x)
    qb_y = send(r.Q.at[1 - y, :, :, c, :, two], r.QYB, over_y)

    @pl.loop(0, nb)
    def _(i):
        for s in range(2):
            at = pl.ds(pl.multiple_of((2 * i + s) * rb, rb), rb)
            a, b = r.gK[at, :], r.gV[at, :]
            a = a + pltpu.roll(a, 64, 1)
            b = b + pltpu.roll(b, 64, 1)
            r.kvs[i, s] = jnp.where(lane < 64, a, b).astype(bf16)

    kv_y = send(r.kvs.at[:, 1 - y], r.kvr, over_y)
    g = nn(r.glog[...], r.wrp[...])
    for e in range(2):
        g = g + nt(r.gq[:, e * half : (e + 1) * half], r.WQ[e])
    r.acc[...] = g
    got(p_y)

    @pl.loop(0, nz)
    def _(a):
        r.P[y, a, x, c] = r.P[y, a, x, c] + r.PY[a]

    p_z = [send(r.P.at[y, k, x, c], r.PZ.at[i], to) for i, (k, to) in enumerate(zip(zs, over_z))]
    got(f0_x)
    v = r.F[0, y, z, x, c].astype(f32) + r.FX0[...].astype(f32)
    r.gwh[:, 0:ch] = v[:, 0:ch]
    r.gwT[:, 0:ch] = v[:, ch : 2 * ch]
    got(qa_x)

    @pl.loop(0, 2 * nz)
    def _(t):
        e, a = t // nz, t % nz
        r.Q[e, a, x, c, :, one] = r.Q[e, a, x, c, :, one] + r.QXA[e, a]

    qa_y = send(r.Q.at[1 - y, :, x, c, :, one], r.QYA, over_y)
    got(qb_y)

    @pl.loop(0, 2 * nz)
    def _(t):
        a, b = t // 2, t % 2
        r.Q[y, a, b, c, :, two] = r.Q[y, a, b, c, :, two] + r.QYB[a, b]

    qb_x = send(r.Q.at[y, :, 1 - x, c, :, two], r.QXB, over_x)
    got(kv_y)

    def finish(i):
        at = cut(i, rb)
        low = (r.kvs[i, y].astype(f32) + r.kvr[i].astype(f32)).astype(bf16)
        r.kvr[i] = low
        g = r.acc[at, :] + nt(low, r.wkvg[...].reshape(width, 128))
        normed, inv = norm_rows(r.tok[own(i)].astype(f32))
        r.gain_rows[0:1, :] += jnp.sum(g * normed, axis=0, keepdims=True)
        r.gt[i, y] = (r.res[at, :] + norm_back(g, normed, inv, r.gain1[...])).astype(bf16)

    pl.loop(0, nb)(finish)
    gt_y = send(r.gt.at[:, y], r.gt.at[:, y], over_y)

    r.K[...] = nn(r.h1T[...], r.kvr[...].reshape(nb * rb, 128)).reshape(nz, 2, 2, shard, 128)
    k_c = send(r.K.at[:, :, 1 - c], r.KC, over_c)
    routed = jnp.zeros((128, width), f32)
    for i in range(nb):
        routed = routed + tn(r.glog[i * rb : (i + 1) * rb, :], r.h1[own(i)])
    r.S[0] = routed[0:32]
    r.S[0, 30:32, :] = r.gain_rows[...]
    s_c = send(r.S.at[0], r.SR.at[0], over_c)

    got(qa_y, qb_x)

    @pl.loop(0, nz)
    def _(a):
        r.Q[y, a, x, c, :, one] = r.Q[y, a, x, c, :, one] + r.QYA[a]
        r.Q[y, a, x, c, :, two] = r.Q[y, a, x, c, :, two] + r.QXB[a]

    q_z = [send(r.Q.at[y, k, x, c], r.QZ.at[i], to) for i, (k, to) in enumerate(zip(zs, over_z))]
    got(k_c)

    @pl.loop(0, 2 * nz)
    def _(t):
        a, b = t // 2, t % 2
        r.K[a, b, c] = r.K[a, b, c] + r.KC[a, b]

    k_x = send(r.K.at[:, 1 - x, c], r.KX, over_x)
    got(s_c)
    r.S[1] = r.S[0] + r.SR[0]
    s_x = send(r.S.at[1], r.SR.at[1], over_x)
    got(*p_z)
    v = r.P[y, z, x, c].astype(f32)
    for k in range(nz - 1):
        v = v + r.PZ[k].astype(f32)
    r.PA[z, x, c] = v.astype(bf16)
    pa_z = [send(r.PA.at[z, x, c], r.PA.at[z, x, c], to) for to in over_z]
    got(*f1_z)
    v = r.F[1, y, z, x, c].astype(f32)
    for k in range(nz - 1):
        v = v + r.FZ1[k].astype(f32)
    r.gwh[:, ch : 2 * ch] = v[:, 0:ch]
    r.gwT[:, ch : 2 * ch] = v[:, ch : 2 * ch]
    got(k_x)

    @pl.loop(0, nz)
    def _(a):
        r.K[a, x, c] = r.K[a, x, c] + r.KX[a]

    k_z = [send(r.K.at[k, x, c], r.KZ.at[i], to) for i, (k, to) in enumerate(zip(zs, over_z))]
    got(s_x)
    r.S[2] = r.S[1] + r.SR[1]
    s_y = send(r.S.at[2], r.SR.at[2], over_y)
    got(*q_z)
    v = r.Q[y, z, x, c].astype(f32)
    for k in range(nz - 1):
        v = v + r.QZ[k].astype(f32)
    r.QA[z, x, c] = v.astype(bf16)
    view = r.QA.at[z, x, c, :, one]
    ga_z = [send(view, view, to) for to in over_z]
    view = r.QA.at[z, x, c, :, two]
    gb_x = send(view, view, over_x)
    got(*pa_z)
    pa_x = send(r.PA.at[:, x, c], r.PA.at[:, x, c], over_x)
    got(gb_x)
    view = r.QA.at[z, :, c, :, two]
    gb_z = [send(view, view, to) for to in over_z]
    got(*k_z)
    v = r.K[z, x, c]
    for k in range(nz - 1):
        v = v + r.KZ[k]
    r.KY[0] = v
    k_y = send(r.KY.at[0], r.KY.at[1], over_y)
    got(s_y)
    r.S[3] = r.S[2] + r.SR[2]
    r.SZ[z] = r.S[3]
    s_z = [send(r.S.at[3], r.SZ.at[z], to) for to in over_z]
    got(*ga_z)
    view = r.QA.at[:, x, c, :, one]
    ga_x = send(view, view, over_x)
    got(pa_x)
    pa_c = send(r.PA.at[:, :, c], r.PA.at[:, :, c], over_c)
    got(*gb_z)
    view = r.QA.at[:, :, c, :, two]
    gb_c = send(view, view, over_c)
    got(k_y)
    r.gkv[...] = r.KY[0] + r.KY[1]
    got(*s_z)
    v = r.SZ[0]
    for k in range(1, nz):
        v = v + r.SZ[k]
    r.small[...] = v
    got(ga_x)
    view = r.QA.at[:, :, c, :, one]
    ga_c = send(view, view, over_c)
    got(pa_c, gb_c, ga_c)
    got(out_y, gt_y)
    for copy in sent:
        copy.wait_send()


def close(out, gt, QA, PA, gwh, gwT, gkv, small,
          o_out, o_gt, o_wq, o_wo, o_wh, o_wT, o_k, o_v, o_wr, o_g1, o_g2, sem):
    first = pltpu.make_async_copy(out, o_out, sem.at[0])
    second = pltpu.make_async_copy(gt, o_gt, sem.at[1])
    first.start()
    second.start()
    o_wq[...] = QA[...].astype(f32)
    o_wo[...] = PA[...].astype(f32)
    o_wh[...] = gwh[...]
    o_wT[...] = gwT[...]
    o_k[...] = gkv[:, 0:64]
    o_v[...] = gkv[:, 64:128]
    o_wr[...] = small[0 : o_wr.shape[0], :]
    o_g1[...] = small[30:31, :]
    o_g2[...] = small[31:32, :]
    first.wait()
    second.wait()


def shards(
    tokens, gain_attn, w_key, w_value, w_router, w_query, w_out, gain_ffn,
    w_hidden, w_output, expert_ids, lengths, grad_out,
):
    rows, width = tokens.shape
    dp = lax.axis_size("dp")
    inner = min(dp, 16)
    outer = dp // inner
    nz = inner // 4
    nb = rows // rb // 2
    top = expert_ids.shape[1]
    n_experts = w_router.shape[1]
    half = w_query.shape[1]
    ffh = w_hidden.shape[1]
    near = [[g * outer + k for k in range(outer)] for g in range(inner)]
    wt = w_output.T
    if outer > 1:
        w_key, w_value, w_hidden, wt = (
            lax.all_gather(v, "dp", axis=0, tiled=True, axis_index_groups=near)
            for v in (w_key, w_value, w_hidden, wt)
        )
    shard = width // inner
    woc = half // inner
    sds = jax.ShapeDtypeStruct
    spec = scratch(rows, width, nb, top, 2 * half, 2 * ffh, nz, shard)
    names = in_names + out_names + list(spec)
    vmem = pl.BlockSpec(memory_space=pltpu.VMEM)
    anyw = pl.BlockSpec(memory_space=pl.ANY)
    out, gt, QA, PA, gwh, gwT, gkv, small = pl.pallas_call(
        functools.partial(kernel, names, outer),
        out_shape=(
            sds((nb, 2, rb, width // 2), bf16),
            sds((nb, 2, rb, width), bf16),
            sds((nz, 2, 2, shard, half), bf16),
            sds((nz, 2, 2, woc, width), bf16),
            sds((shard, ffh), f32),
            sds((shard, ffh), f32),
            sds((shard, 128), f32),
            sds((32, width), f32),
        ),
        in_specs=[pl.BlockSpec(memory_space=pltpu.SMEM)] + [vmem] * 7 + [anyw] * 5,
        out_specs=[vmem] * 8,
        scratch_shapes=list(spec.values()),
        compiler_params=pltpu.CompilerParams(
            collective_id=0, has_side_effects=True, vmem_limit_bytes=63 * 2**20
        ),
    )(
        lengths, tokens.reshape(2 * nb, rb, width), gain_attn[None], w_router.T, gain_ffn[None],
        expert_ids.T, w_key, w_value, w_query, w_out, w_hidden, wt,
        grad_out.reshape(nb, 2, rb, width // 2),
    )
    out, gt, gwq, gwo, gwh, gwT, gk, gv, gwr, g1, g2 = pl.pallas_call(
        close,
        out_shape=(
            sds(out.shape, bf16),
            sds(gt.shape, bf16),
            sds((width, half), f32),
            sds((half, width), f32),
            sds((shard, ffh), f32),
            sds((shard, ffh), f32),
            sds((shard, 64), f32),
            sds((shard, 64), f32),
            sds((n_experts, width), f32),
            sds((1, width), f32),
            sds((1, width), f32),
        ),
        in_specs=[anyw] * 2 + [vmem] * 6,
        out_specs=[anyw] * 2 + [vmem] * 9,
        scratch_shapes=[pltpu.SemaphoreType.DMA((2,))],
        compiler_params=pltpu.CompilerParams(vmem_limit_bytes=32 * 2**20),
    )(out, gt, QA.reshape(width, half), PA.reshape(half, width), gwh, gwT, gkv, small)
    if outer > 1:
        gwq, gwo, gwr, g1, g2 = lax.psum(
            (gwq, gwo, gwr, g1, g2), "dp", axis_index_groups=near
        )
        gwh, gwT, gk, gv = (
            lax.psum_scatter(v, "dp", scatter_dimension=0, tiled=True, axis_index_groups=near)
            for v in (gwh, gwT, gk, gv)
        )
    return (
        out.reshape(rows, width // 2), gt.reshape(rows, width), gk, gv, gwr.T, gwq, gwo,
        gwh, gwT.T, g1[0], g2[0],
    )


def solution(mesh):
    placed = (
        P("dp", None), P(), P("dp", None), P("dp", None), P(), P(None, "expert"),
        P("expert", None), P(), P("dp", "expert"), P("expert", "dp"), P("dp", None),
        P("dp"), P("dp", "expert"),
    )
    return jax.shard_map(
        shards,
        mesh=mesh,
        in_specs=placed,
        out_specs=(
            P("dp", "expert"), P("dp", None), P("dp", None), P("dp", None), P(),
            P(None, "expert"), P("expert", None), P("dp", "expert"), P("expert", "dp"),
            P(), P(),
        ),
        check_vma=False,
    )
```

```python
import functools

import jax
import jax.numpy as jnp
from jax import lax
from jax.experimental import pallas as pl
from jax.experimental.pallas import tpu as pltpu
from jax.sharding import PartitionSpec as P

f32 = jnp.float32
bf16 = jnp.bfloat16
eps = 1e-05
lowest = -1e30
rb = 128


def nn(left, right):
    return jnp.dot(left, right, preferred_element_type=f32)


def nt(left, right):
    return lax.dot_general(left, right, (((1,), (1,)), ((), ())), preferred_element_type=f32)


def tn(left, right):
    return lax.dot_general(left, right, (((0,), (0,)), ((), ())), preferred_element_type=f32)


def norm_rows(x):
    centred = x - jnp.mean(x, axis=-1, keepdims=True)
    inv = lax.rsqrt(jnp.mean(centred * centred, axis=-1, keepdims=True) + eps)
    return centred * inv, inv


def norm_back(u, normed, inv, gain):
    w = u * gain
    return inv * (
        w
        - jnp.mean(w, axis=-1, keepdims=True)
        - normed * jnp.mean(w * normed, axis=-1, keepdims=True)
    )


def lanes(shape):
    return lax.broadcasted_iota(jnp.int32, shape, len(shape) - 1)


MESH = pl.DeviceIdType.MESH

in_names = [
    "len_ref",
    "tok_in",
    "gain1",
    "wrt",
    "gain2",
    "idst",
    "wk_in",
    "wv_in",
    "wq_in",
    "wo_in",
    "wh_in",
    "wt_in",
    "go_in",
]
out_names = [
    "out",
    "gt",
    "QA",
    "PA",
    "gwh",
    "gwT",
    "gkv",
    "small",
    "gain1_out",
]


def scratch(rows, width, nb, top, fq, ff, nz, shard):
    vm = pltpu.VMEM
    own = rows // 2
    half = fq // 2
    total = 128 * nb * (nb + 1)
    ring = (nz, 2, 2)
    ch = ff // 4
    woc = half // (4 * nz)
    return {
        "tok": vm((2 * nb, rb, width), bf16),
        "outm": vm((nb, rb, width // 2), bf16),
        "gts": vm((nb, rb, width), bf16),
        "G": vm((4, 1, width), f32),
        "GR": vm((3, 1, width), f32),
        "GZ": vm((nz, 1, width), f32),
        "wkvg": vm(ring + (shard, 128), bf16),
        "W": vm((2, 2) + ring + (shard, 2 * ch), bf16),
        "WQ": vm((2, width, half), bf16),
        "WO": vm((2, half, width), bf16),
        "GO": vm((2, nb, rb, width // 2), bf16),
        "h1": vm((2 * nb, rb, width), bf16),
        "h1T": vm((width, own), bf16),
        "KK": vm((rows, 128), bf16),
        "VV": vm((rows, 128), bf16),
        "KKT": vm((128, rows), bf16),
        "VVT": vm((128, rows), bf16),
        "idl": vm((nb, top, rb, 128), jnp.int32),
        "gateb": vm((nb, top, rb, 128), f32),
        "dense": vm((own, 128), f32),
        "Qs": vm((nb, top, rb, 128), bf16),
        "PT": vm((total, top * rb), bf16),
        "O": vm((nb, top, rb, 128), f32),
        "wide": vm((rb, fq), f32),
        "gated": vm((own, fq), bf16),
        "n2": vm((own, width), f32),
        "r2": vm((own, 1), f32),
        "res": vm((own, width), f32),
        "h2": vm((own, width), bf16),
        "h2T": vm((width, own), bf16),
        "gfT": vm((width, own), bf16),
        "gf": vm((own, width), bf16),
        "gh2": vm((own, width), f32),
        "acc": vm((own, width), f32),
        "gatt": vm((own, width), bf16),
        "dOs": vm((nb, top, rb, 128), bf16),
        "glog": vm((own, 128), bf16),
        "AG": vm((own, 2 * ch), bf16),
        "wrp": vm((128, width), bf16),
        "gK": vm((rows, 128), f32),
        "gV": vm((rows, 128), f32),
        "dQ": vm((top, rb, 128), f32),
        "gain_rows": vm((2, width), f32),
        "outx": vm((nb, rb, width // 2), bf16),
        "kvs": vm((nb, 2, rb, 128), bf16),
        "kvr": vm((nb, rb, 128), bf16),
        "F": vm((2, 2) + ring + (shard, 2 * ch), bf16),
        "FC": vm((2, 2, nz, 2, shard, 2 * ch), bf16),
        "FY0": vm((nz, 2, shard, 2 * ch), bf16),
        "FZ0": vm((nz - 1, 2, shard, 2 * ch), bf16),
        "FX0": vm((shard, 2 * ch), bf16),
        "FX1": vm((2, nz, shard, 2 * ch), bf16),
        "FY1": vm((nz, shard, 2 * ch), bf16),
        "FZ1": vm((nz - 1, shard, 2 * ch), bf16),
        "QC": vm((2, nz, 2, shard, half), bf16),
        "QXA": vm((2, nz, shard, half // 2), bf16),
        "QYA": vm((nz, shard, half // 2), bf16),
        "QYB": vm((nz, 2, shard, half // 2), bf16),
        "QXB": vm((nz, shard, half // 2), bf16),
        "QZ": vm((nz - 1, shard, half), bf16),
        "P": vm((2,) + ring + (woc, width), bf16),
        "PC": vm((2, nz, 2, woc, width), bf16),
        "PX": vm((2, nz, woc, width), bf16),
        "PY": vm((nz, woc, width), bf16),
        "PZ": vm((nz - 1, woc, width), bf16),
        "K": vm(ring + (shard, 128), f32),
        "KC": vm((nz, 2, shard, 128), f32),
        "KX": vm((nz, shard, 128), f32),
        "KZ": vm((nz - 1, shard, 128), f32),
        "KY": vm((2, shard, 128), f32),
        "S": vm((4, 32, width), f32),
        "SR": vm((3, 32, width), f32),
        "SZ": vm((nz, 32, width), f32),
        "send": pltpu.SemaphoreType.DMA((128,)),
        "recv": pltpu.SemaphoreType.DMA((128,)),
        "local": pltpu.SemaphoreType.DMA((16,)),
    }


class Refs:
    pass


def kernel(names, outer, *refs):
    r = Refs()
    for name, ref in zip(names, refs):
        setattr(r, name, ref)
    nb = r.tok.shape[0] // 2
    width = r.tok.shape[2]
    top = r.idst.shape[0]
    fq = r.gated.shape[1]
    half = fq // 2
    groups = fq // 128
    r.gq = r.gated
    r.Q = r.W.at[0, :, :, :, :, :, 0:half]
    r.actS = r.AG.at[:, 0 : r.W.shape[6] // 2]
    r.giS = r.AG.at[:, r.W.shape[6] // 2 : r.W.shape[6]]
    nz = r.W.shape[2]
    ch = r.W.shape[6] // 2
    shard = r.W.shape[5]
    d = lax.axis_index("dp")
    y = lax.axis_index("expert")
    n, m = d // outer, d % outer
    z, x, c = n // 4, (n // 2) % 2, n % 2
    length = r.len_ref[0]

    def device(z, x, c, y):
        return ((z * 4 + x * 2 + c) * outer + m, y)

    over_c = device(z, x, 1 - c, y)
    over_x = device(z, 1 - x, c, y)
    over_y = device(z, x, c, 1 - y)
    zs = [(z + k) % nz for k in range(1, nz)]
    over_z = [device(k, x, c, y) for k in zs]
    used = [0]
    sent = []

    def send(source, target, to):
        k = used[0]
        used[0] += 1
        copy = pltpu.make_async_remote_copy(
            src_ref=source, dst_ref=target, send_sem=r.send.at[k], recv_sem=r.recv.at[k],
            device_id=to, device_id_type=MESH,
        )
        copy.start()
        sent.append(copy)
        return copy

    def here(k, source, target):
        copy = pltpu.make_async_copy(source, target, r.local.at[k])
        copy.start()
        return copy

    def got(*copies):
        for copy in copies:
            copy.wait_recv()

    def own(i):
        return 2 * i + y

    def cut(i, size):
        return pl.ds(pl.multiple_of(i * size, size), size)

    def valid_rows(i):
        return (rb * own(i) + lax.broadcasted_iota(jnp.int32, (rb, 1), 0) < length).astype(f32)

    l_tok = here(7, r.tok_in, r.tok)
    l_w = [
        here(2 * j + k, ref.at[:, j * ch : (j + 1) * ch],
             r.W.at[j, y, z, x, c, :, k * ch : (k + 1) * ch])
        for j in range(2)
        for k, ref in enumerate((r.wh_in, r.wt_in))
    ]
    l_q = here(4, r.wq_in, r.WQ.at[y])
    l_o = here(5, r.wo_in, r.WO.at[y])
    l_g = here(6, r.go_in.at[:, y], r.GO.at[y])
    r.wkvg[z, x, c] = jnp.concatenate((r.wk_in[...], r.wv_in[...]), axis=1)
    barrier = pltpu.get_barrier_semaphore()
    peers = [over_c, over_x, over_y] + over_z
    for peer in peers:
        pl.semaphore_signal(barrier, inc=1, device_id=peer, device_id_type=MESH)
    pl.semaphore_wait(barrier, len(peers))
    kv_z = [send(r.wkvg.at[z, x, c], r.wkvg.at[z, x, c], to) for to in over_z]
    l_w[0].wait()
    l_w[1].wait()
    w_y0 = send(r.W.at[0, y, z, x, c], r.W.at[0, y, z, x, c], over_y)
    qrows = cut(c, width // 2)
    q_y = send(r.wq_in.at[qrows, :], r.WQ.at[y, qrows, :], over_y)
    l_w[2].wait()
    l_w[3].wait()
    w_y1 = send(r.W.at[1, y, z, x, c], r.W.at[1, y, z, x, c], over_y)
    orows = cut(c, half // 2)
    o_y = send(r.wo_in.at[orows, :], r.WO.at[y, orows, :], over_y)
    g_y = send(r.go_in.at[:, 1 - y], r.GO.at[y], over_y)
    spare = jnp.zeros((128 - r.wrt.shape[0], width), f32)
    r.wrp[...] = jnp.concatenate((r.wrt[...].astype(f32), spare), axis=0).astype(bf16)

    def w_part(k):
        return r.W.at[k // 2, :, :, :, :, :, pl.ds((k % 2) * ch, ch)]

    def w_over_z(k, both=False):
        view = w_part(k).at[:, z, :, c] if both else w_part(k).at[:, z, x, c]
        return [send(view, view, to) for to in over_z]

    def w_over_x(k, line=True):
        view = w_part(k).at[:, :, x, c] if line else w_part(k).at[:, z, x, c]
        return send(view, view, over_x)

    def w_over_c(k):
        view = w_part(k).at[:, :, :, c]
        return send(view, view, over_c)
    l_tok.wait()

    @pl.loop(0, 2 * nb)
    def _(b):
        normed, _ = norm_rows(r.tok[b].astype(f32))
        r.h1[b] = (normed * r.gain1[...]).astype(bf16)
    got(*kv_z)
    kv_x = send(r.wkvg.at[:, x, c], r.wkvg.at[:, x, c], over_x)
    got(w_y0)
    w0_z = w_over_z(0)
    w1_z = w_over_z(1)

    lane = lanes((rb, 128))
    upper = (lane >= 64).astype(jnp.int32)

    def gates(i):
        h = r.h1[own(i)]
        at = cut(i, rb)
        r.h1T[:, at] = h.astype(f32).T.astype(bf16)
        logits = nt(h, r.wrp[...])
        ids = r.idst[:, cut(own(i), rb)].astype(f32).T.astype(jnp.int32)
        spread = [jnp.broadcast_to(ids[:, k : k + 1], (rb, 128)) for k in range(top)]
        chosen = lane == spread[0]
        for k in range(1, top):
            chosen = chosen | (lane == spread[k])
        most = jnp.max(jnp.where(chosen, logits, lowest), axis=-1, keepdims=True)
        e = jnp.where(chosen, jnp.exp(jnp.where(chosen, logits - most, 0.0)), 0.0)
        g = e / jnp.sum(e, axis=-1, keepdims=True)
        r.dense[at, :] = g
        for k in range(top):
            gk = jnp.sum(jnp.where(lane == spread[k], g, 0.0), axis=-1, keepdims=True)
            r.gateb[i, k] = jnp.broadcast_to(gk, (rb, 128))
            r.idl[i, k] = spread[k] - upper

    pl.loop(0, nb // 2)(gates)
    got(kv_x)
    kv_c = send(r.wkvg.at[:, :, c], r.wkvg.at[:, :, c], over_c)
    pl.loop(nb // 2, nb)(gates)
    got(kv_c)

    @pl.loop(0, 2 * nb)
    def _(b):
        kv = nn(r.h1[b], r.wkvg[...].reshape(width, 128))
        at = cut(b, rb)
        swapped = pltpu.roll(kv, 64, 1)
        k2 = jnp.where(lane < 64, kv, swapped)
        v2 = jnp.where(lane < 64, swapped, kv)
        r.KK[at, :] = k2.astype(bf16)
        r.VV[at, :] = v2.astype(bf16)
        r.KKT[:, at] = k2.T.astype(bf16)
        r.VVT[:, at] = v2.T.astype(bf16)
    got(*w0_z)
    w0_x = w_over_x(0)
    got(q_y)
    q_c = send(r.WQ.at[1 - y, qrows, :], r.WQ.at[1 - y, qrows, :], over_c)
    got(w_y1)
    w3_x = w_over_x(3, False)
    w2_z = w_over_z(2)
    l_q.wait()
    got(q_c)

    @pl.loop(0, nb)
    def _(i):
        h = r.h1[own(i)]
        for e in range(2):
            r.wide[:, e * half : (e + 1) * half] = 0.125 * nn(h, r.WQ[e])

        @pl.loop(0, rb // 16)
        def _(t):
            at = cut(t, 16)
            parts = [r.wide[at, pl.ds(128 * g, 128)] for g in range(groups)]
            for k in range(top):
                mine = r.idl[i, k, at, :]
                val = jnp.zeros((16, 128), f32)
                for g in range(groups):
                    val = jnp.where(mine == 2 * g, parts[g], val)
                r.Qs[i, k, at, :] = val.astype(bf16)
    diag = lax.broadcasted_iota(jnp.int32, (256, 256), 0) <= rb * y + lanes((256, 256)) % 128

    def attend(i):
        nk = 256 * i
        start = 128 * i * (i + 1)

        @pl.loop(0, top // 2, unroll=4)
        def _(p):
            q = r.Qs[i, pl.ds(2 * p, 2)].reshape(256, 128)
            cols = cut(p, 256)
            s1 = nt(r.KK[nk : nk + 256, :], q)
            s1 = jnp.where(diag, s1, lowest)
            most = jnp.max(s1, axis=0, keepdims=True)
            if nk:
                s0 = nt(r.KK[0:nk, :], q)
                most = jnp.maximum(most, jnp.max(s0, axis=0, keepdims=True))
                p0 = jnp.exp(s0 - most)
            p1 = jnp.exp(s1 - most)
            tot = jnp.sum(p1, axis=0, keepdims=True)
            if nk:
                tot = tot + jnp.sum(p0, axis=0, keepdims=True)
            inv = 1.0 / tot
            p1 = (p1 * inv).astype(bf16)
            r.PT[start + nk : start + nk + 256, cols] = p1
            o = nn(r.VVT[:, nk : nk + 256], p1)
            if nk:
                p0 = (p0 * inv).astype(bf16)
                r.PT[start : start + nk, cols] = p0
                o = o + nn(r.VVT[:, 0:nk], p0)
            r.O[i, pl.ds(2 * p, 2)] = o.T.reshape(2, rb, 128)

    got(w3_x)
    w3_z = w_over_z(3, True)
    got(*w1_z)
    w1_x = w_over_x(1)
    attend(0)
    attend(1)
    got(*w2_z)
    w2_x = w_over_x(2)
    got(w0_x)
    w0_c = w_over_c(0)
    attend(2)
    got(w1_x)
    w1_c = w_over_c(1)
    got(o_y)
    o_c = send(r.WO.at[1 - y, orows, :], r.WO.at[1 - y, orows, :], over_c)
    for i in range(3, nb):
        attend(i)
    l_o.wait()
    l_g.wait()
    got(o_c)
    got(g_y)
    def project(i):
        at = cut(i, rb)

        @pl.loop(0, rb // 16)
        def _(t):
            at = cut(t, 16)
            atr = pl.ds(pl.multiple_of(i * rb + t * 16, 16), 16)
            mine = [r.idl[i, k, at, :] for k in range(top)]
            vals = [r.gateb[i, k, at, :] * r.O[i, k, at, :] for k in range(top)]
            for g in range(groups):
                val = jnp.zeros((16, 128), f32)
                for k in range(top):
                    val = jnp.where(mine[k] == 2 * g, vals[k], val)
                r.gated[atr, pl.ds(128 * g, 128)] = val.astype(bf16)

        valid = valid_rows(i)
        att = nn(r.gated[at, 0:half], r.WO[0]) + nn(r.gated[at, half:fq], r.WO[1])
        row = r.tok[own(i)].astype(f32) + valid * att
        r.res[at, :] = row
        normed, inv = norm_rows(row)
        r.n2[at, :] = normed
        r.r2[at, :] = inv
        h = normed * r.gain2[...]
        r.h2[at, :] = h.astype(bf16)
        r.h2T[:, at] = h.T.astype(bf16)
        for s in range(2):
            side = pl.ds(s * (width // 2), width // 2)
            g = valid * r.GO[s, i].astype(f32)
            r.gf[at, side] = g.astype(bf16)
            r.gfT[side, at] = g.T.astype(bf16)

    pl.loop(0, nb)(project)

    c0 = 0.7978845608028654
    c1 = 0.044715

    def feed(j, e, first=False):

        w1 = r.W[j, e, :, :, :, :, 0:ch].reshape(width, ch)
        w2 = r.W[j, e, :, :, :, :, ch : 2 * ch].reshape(width, ch)
        for i in range(nb // 2):
            at = pl.ds(i * 256, 256)
            v = nn(r.h2[at, :], w1)
            ga = nn(r.gf[at, :], w2)
            vv = v * v
            hp = 0.5 + 0.5 * jnp.tanh(v * (c0 + (c0 * c1) * vv))
            act = v * hp
            slope = hp + act * (1.0 - hp) * (2 * c0 + (6 * c0 * c1) * vv)
            r.actS[at, :] = act.astype(bf16)
            r.giS[at, :] = (slope * ga).astype(bf16)
        a = nt(r.actS[...], w2)
        b = nt(r.giS[...], w1)
        if first:
            r.acc[...] = a
            r.gh2[...] = b
        else:
            r.acc[...] += a
            r.gh2[...] += b

        shape = (nz, 2, 2, shard, ch)
        r.F[j, e, :, :, :, :, 0:ch] = nn(r.h2T[...], r.giS[...]).astype(bf16).reshape(shape)
        r.F[j, e, :, :, :, :, ch : 2 * ch] = (
            nn(r.gfT[...], r.actS[...]).astype(bf16).reshape(shape)
        )
        return send(r.F.at[j, e, :, :, 1 - c], r.FC.at[j, e], over_c)

    def f_add_c(j, e):
        @pl.loop(0, 2 * nz)
        def _(t):
            a, b = t // 2, t % 2
            r.F[j, e, a, b, c] = r.F[j, e, a, b, c] + r.FC[j, e, a, b]
    got(w0_c, w1_c)
    f0p = feed(0, 1 - y, True)
    got(w2_x)
    w2_c = w_over_c(2)
    f0m = feed(0, y)
    got(f0p)
    f_add_c(0, 1 - y)
    f0_y = send(r.F.at[0, 1 - y, :, :, c], r.FY0, over_y)
    got(*w3_z)
    w3_c = w_over_c(3)
    got(f0m)
    f_add_c(0, y)
    got(w2_c, w3_c)
    f1p = feed(1, 1 - y)
    f1m = feed(1, y)
    got(f1p)
    f_add_c(1, 1 - y)
    f1_xa = send(r.F.at[1, 1 - y, :, 1 - x, c], r.FX1.at[0], over_x)
    r.gain_rows[...] = jnp.zeros_like(r.gain_rows)

    def turn(i):
        at = cut(i, rb)
        valid = valid_rows(i)
        outs = (r.res[at, :] + valid * r.acc[at, :]).astype(bf16)
        mine, other = outs[:, : width // 2], outs[:, width // 2 :]
        low = y == 0
        r.outm[i] = jnp.where(low, mine, other)
        r.outx[i] = jnp.where(low, other, mine)
        u, normed = r.gh2[at, :], r.n2[at, :]
        r.gain_rows[1:2, :] += jnp.sum(u * normed, axis=0, keepdims=True)
        back = norm_back(u, normed, r.r2[at, :], r.gain2[...])
        go = jnp.concatenate((r.GO[0, i], r.GO[1, i]), axis=1).astype(f32)
        gr = go + back
        r.res[at, :] = gr
        ga = (valid * gr).astype(bf16)
        r.gatt[at, :] = ga
        for e in range(2):
            r.wide[:, e * half : (e + 1) * half] = nt(ga, r.WO[e])

        @pl.loop(0, rb // 16)
        def _(t):
            at = cut(t, 16)
            atr = pl.ds(pl.multiple_of(i * rb + t * 16, 16), 16)
            parts = [r.wide[at, pl.ds(128 * g, 128)] for g in range(groups)]
            ln = lanes((16, 128))
            hf = (ln >= 64).astype(jnp.int32)
            gd = jnp.zeros((16, 128), f32)
            for k in range(top):
                mine = r.idl[i, k, at, :]
                val = jnp.zeros((16, 128), f32)
                for g in range(groups):
                    val = jnp.where(mine == 2 * g, parts[g], val)
                dot = jnp.sum(val * r.O[i, k, at, :], axis=-1, keepdims=True)
                gd = jnp.where(mine + hf == ln, dot, gd)
                r.dOs[i, k, at, :] = (r.gateb[i, k, at, :] * val).astype(bf16)
            dn = r.dense[atr, :]
            gs = dn * (gd - jnp.sum(dn * gd, axis=-1, keepdims=True))
            r.glog[atr, :] = gs.astype(bf16)

    pl.loop(0, nb // 2)(turn)
    got(f1m)
    f_add_c(1, y)
    f1_xb = send(r.F.at[1, y, :, 1 - x, c], r.FX1.at[1], over_x)
    pl.loop(nb // 2, nb)(turn)
    l_out = here(8, r.outm, r.out.at[:, y])
    routed = jnp.zeros((128, width), f32)
    for i in range(nb):
        routed = routed + tn(r.glog[i * rb : (i + 1) * rb, :], r.h1[own(i)])
    r.S[0] = routed[0:32]
    r.S[0, 31:32, :] = r.gain_rows[1:2, :]
    s_c = send(r.S.at[0], r.SR.at[0], over_c)
    got(f0_y)

    @pl.loop(0, 2 * nz)
    def _(t):
        a, b = t // 2, t % 2
        r.F[0, y, a, b, c] = r.F[0, y, a, b, c] + r.FY0[a, b]

    f0_z = [
        send(r.F.at[0, y, k, :, c], r.FZ0.at[i], to) for i, (k, to) in enumerate(zip(zs, over_z))
    ]

    woc = r.P.shape[4]
    for e in range(2):
        r.P[e] = (
            tn(r.gated[:, e * half : (e + 1) * half], r.gatt[...])
            .astype(bf16)
            .reshape(nz, 2, 2, woc, width)
        )
    p_c = send(r.P.at[:, :, :, 1 - c], r.PC, over_c)

    def back(i):
        nk = 256 * (i + 1)
        start = 128 * i * (i + 1)
        last = i == nb - 1
        v = nn(r.PT[start : start + nk, :], r.dOs[i].reshape(top * rb, 128))
        r.gV[0:nk, :] = v if last else r.gV[0:nk, :] + v

        @pl.loop(0, top // 2, unroll=4)
        def _(p):
            do = r.dOs[i, pl.ds(2 * p, 2)].reshape(256, 128)
            cols = cut(p, 256)
            dp = nt(r.VV[0:nk, :], do)
            pr = r.PT[start : start + nk, cols].astype(f32)
            s = jnp.sum(pr * dp, axis=0, keepdims=True)
            ds = (pr * (dp - s)).astype(bf16)
            r.PT[start : start + nk, cols] = ds
            dq = nn(r.KKT[:, 0:nk], ds)
            r.dQ[pl.ds(2 * p, 2)] = dq.T.reshape(2, rb, 128)

        @pl.loop(0, rb // 16)
        def _(t):
            at = cut(t, 16)
            atr = pl.ds(pl.multiple_of(i * rb + t * 16, 16), 16)
            mine = [r.idl[i, k, at, :] for k in range(top)]
            vals = [r.dQ[k, at, :] for k in range(top)]
            for g in range(groups):
                val = jnp.zeros((16, 128), f32)
                for k in range(top):
                    val = jnp.where(mine[k] == 2 * g, vals[k], val)
                r.gq[atr, pl.ds(128 * g, 128)] = val.astype(bf16) * 0.125

    def key_sums(i):
        v = nn(r.PT[128 * i * (i + 1) : 128 * (i + 1) * (i + 2), :], r.Qs[i].reshape(top * rb, 128))
        at = pl.ds(0, 256 * (i + 1))
        r.gK[at, :] = v if i == nb - 1 else r.gK[at, :] + v
        for s in range(2):
            at = pl.ds((2 * i + s) * rb, rb)
            a, b = r.gK[at, :], r.gV[at, :]
            a = a + pltpu.roll(a, 64, 1)
            b = b + pltpu.roll(b, 64, 1)
            r.kvs[i, s] = jnp.where(lane < 64, a, b).astype(bf16)
        return send(r.kvs.at[i, 1 - y], r.kvr.at[i], over_y)

    def finish(i):
        at = pl.ds(i * rb, rb)
        low = (r.kvs[i, y].astype(f32) + r.kvr[i].astype(f32)).astype(bf16)
        r.kvr[i] = low
        g = nn(r.glog[at, :], r.wrp[...]) + nt(low, r.wkvg[...].reshape(width, 128))
        for e in range(2):
            g = g + nt(r.gq[at, e * half : (e + 1) * half], r.WQ[e])
        normed, inv = norm_rows(r.tok[own(i)].astype(f32))
        r.gain_rows[0:1, :] += jnp.sum(g * normed, axis=0, keepdims=True)
        back = norm_back(g, normed, inv, r.gain1[...])
        r.gts[i] = (r.res[at, :] + back).astype(bf16)
        return here(9 + i, r.gts.at[i], r.gt.at[i, y])

    def give(i):
        return send(r.gts.at[i], r.gt.at[i, y], over_y)

    keys, ends = {}, []
    for i in range(nb - 1, 2, -1):
        back(i)
        keys[i] = key_sums(i)
    got(s_c)
    r.S[1] = r.S[0] + r.SR[0]
    s_x = send(r.S.at[1], r.SR.at[1], over_x)
    got(p_c)

    @pl.loop(0, 4 * nz)
    def _(t):
        e, a, b = t // (2 * nz), (t // 2) % nz, t % 2
        r.P[e, a, b, c] = r.P[e, a, b, c] + r.PC[e, a, b]

    p_x = send(r.P.at[:, :, 1 - x, c], r.PX, over_x)
    got(f1_xa, f1_xb)

    @pl.loop(0, nz)
    def _(a):
        r.F[1, 1 - y, a, x, c] = r.F[1, 1 - y, a, x, c] + r.FX1[0, a]
        r.F[1, y, a, x, c] = r.F[1, y, a, x, c] + r.FX1[1, a]

    f1_y = send(r.F.at[1, 1 - y, :, x, c], r.FY1, over_y)
    back(2)
    keys[2] = key_sums(2)
    for i in range(nb - 1, 2, -1):
        got(keys[i])
        ends.append(finish(i))
    gts_y = [give(i) for i in range(nb - 1, 2, -1)]
    got(s_x)
    r.S[2] = r.S[1] + r.SR[1]
    s_y = send(r.S.at[2], r.SR.at[2], over_y)
    got(*f0_z)
    for b in range(2):
        v = r.F[0, y, z, b, c].astype(f32)
        for k in range(nz - 1):
            v = v + r.FZ0[k, b].astype(f32)
        r.F[0, y, z, b, c] = v.astype(bf16)
    f0_x = send(r.F.at[0, y, z, 1 - x, c], r.FX0, over_x)
    back(1)
    keys[1] = key_sums(1)
    got(p_x)

    @pl.loop(0, 2 * nz)
    def _(t):
        e, a = t // nz, t % nz
        r.P[e, a, x, c] = r.P[e, a, x, c] + r.PX[e, a]

    p_y = send(r.P.at[1 - y, :, x, c], r.PY, over_y)
    got(f1_y)

    @pl.loop(0, nz)
    def _(a):
        r.F[1, y, a, x, c] = r.F[1, y, a, x, c] + r.FY1[a]

    f1_z = [
        send(r.F.at[1, y, k, x, c], r.FZ1.at[i], to) for i, (k, to) in enumerate(zip(zs, over_z))
    ]
    got(keys[2])
    ends.append(finish(2))
    back(0)
    for copy in [w_y0, w_y1, w3_x, w0_x, w1_x, w2_x, w0_c, w1_c, w2_c, w3_c,
                 *w0_z, *w1_z, *w2_z, *w3_z]:
        copy.wait_send()
        sent[:] = [other for other in sent if other is not copy]
    for e in range(2):
        r.Q[e] = (
            nn(r.h1T[...], r.gq[:, e * half : (e + 1) * half])
            .astype(bf16)
            .reshape(nz, 2, 2, shard, half)
        )
    q_c2 = send(r.Q.at[:, :, :, 1 - c], r.QC, over_c)
    keys[0] = key_sums(0)
    got(s_y)
    r.S[3] = r.S[2] + r.SR[2]
    r.SZ[z] = r.S[3]
    s_z = [send(r.S.at[3], r.SZ.at[z], to) for to in over_z]
    got(q_c2)

    @pl.loop(0, 4 * nz)
    def _(t):
        e, a, b = t // (2 * nz), (t // 2) % nz, t % 2
        r.Q[e, a, b, c] = r.Q[e, a, b, c] + r.QC[e, a, b]

    one, two = pl.ds(0, half // 2), pl.ds(half // 2, half // 2)
    qa_x = send(r.Q.at[:, :, 1 - x, c, :, one], r.QXA, over_x)
    qb_y = send(r.Q.at[1 - y, :, :, c, :, two], r.QYB, over_y)
    gts_y.append(give(2))
    got(keys[1])
    ends.append(finish(1))
    got(p_y)

    @pl.loop(0, nz)
    def _(a):
        r.P[y, a, x, c] = r.P[y, a, x, c] + r.PY[a]

    p_z = [send(r.P.at[y, k, x, c], r.PZ.at[i], to) for i, (k, to) in enumerate(zip(zs, over_z))]
    got(f0_x)
    v = r.F[0, y, z, x, c].astype(f32) + r.FX0[...].astype(f32)
    r.gwh[:, 0:ch] = v[:, 0:ch]
    r.gwT[:, 0:ch] = v[:, ch : 2 * ch]
    got(keys[0])
    ends.append(finish(0))
    r.K[...] = nn(r.h1T[...], r.kvr[...].reshape(nb * rb, 128)).reshape(nz, 2, 2, shard, 128)
    k_c = send(r.K.at[:, :, 1 - c], r.KC, over_c)
    r.G[0] = r.gain_rows[0:1, :]
    g1_c = send(r.G.at[0], r.GR.at[0], over_c)
    got(qa_x)

    @pl.loop(0, 2 * nz)
    def _(t):
        e, a = t // nz, t % nz
        r.Q[e, a, x, c, :, one] = r.Q[e, a, x, c, :, one] + r.QXA[e, a]

    qa_y = send(r.Q.at[1 - y, :, x, c, :, one], r.QYA, over_y)
    got(qb_y)

    @pl.loop(0, 2 * nz)
    def _(t):
        a, b = t // 2, t % 2
        r.Q[y, a, b, c, :, two] = r.Q[y, a, b, c, :, two] + r.QYB[a, b]

    qb_x = send(r.Q.at[y, :, 1 - x, c, :, two], r.QXB, over_x)
    gts_y.append(give(1))
    gts_y.append(give(0))
    got(k_c)

    @pl.loop(0, 2 * nz)
    def _(t):
        a, b = t // 2, t % 2
        r.K[a, b, c] = r.K[a, b, c] + r.KC[a, b]

    k_x = send(r.K.at[:, 1 - x, c], r.KX, over_x)
    got(g1_c)
    r.G[1] = r.G[0] + r.GR[0]
    g1_x = send(r.G.at[1], r.GR.at[1], over_x)
    got(*p_z)
    v = r.P[y, z, x, c].astype(f32)
    for k in range(nz - 1):
        v = v + r.PZ[k].astype(f32)
    r.PA[z, x, c] = v.astype(bf16)
    pa_z = [send(r.PA.at[z, x, c], r.PA.at[z, x, c], to) for to in over_z]

    got(qa_y, qb_x)

    @pl.loop(0, nz)
    def _(a):
        r.Q[y, a, x, c, :, one] = r.Q[y, a, x, c, :, one] + r.QYA[a]
        r.Q[y, a, x, c, :, two] = r.Q[y, a, x, c, :, two] + r.QXB[a]

    q_z = [send(r.Q.at[y, k, x, c], r.QZ.at[i], to) for i, (k, to) in enumerate(zip(zs, over_z))]
    got(k_x)

    @pl.loop(0, nz)
    def _(a):
        r.K[a, x, c] = r.K[a, x, c] + r.KX[a]

    k_z = [send(r.K.at[k, x, c], r.KZ.at[i], to) for i, (k, to) in enumerate(zip(zs, over_z))]
    got(g1_x)
    r.G[2] = r.G[1] + r.GR[1]
    g1_y = send(r.G.at[2], r.GR.at[2], over_y)
    got(*f1_z)
    v = r.F[1, y, z, x, c].astype(f32)
    for k in range(nz - 1):
        v = v + r.FZ1[k].astype(f32)
    r.gwh[:, ch : 2 * ch] = v[:, 0:ch]
    r.gwT[:, ch : 2 * ch] = v[:, ch : 2 * ch]
    got(*s_z)
    v = r.SZ[0]
    for k in range(1, nz):
        v = v + r.SZ[k]
    r.small[...] = v
    got(*pa_z)
    pa_x = send(r.PA.at[:, x, c], r.PA.at[:, x, c], over_x)
    got(*k_z)
    v = r.K[z, x, c]
    for k in range(nz - 1):
        v = v + r.KZ[k]
    r.KY[0] = v
    k_y = send(r.KY.at[0], r.KY.at[1], over_y)
    out_y = send(r.outx, r.out.at[:, y], over_y)
    got(*q_z)
    v = r.Q[y, z, x, c].astype(f32)
    for k in range(nz - 1):
        v = v + r.QZ[k].astype(f32)
    r.QA[z, x, c] = v.astype(bf16)
    view = r.QA.at[z, x, c, :, two]
    gb_x = send(view, view, over_x)
    view = r.QA.at[z, x, c, :, one]
    ga_z = [send(view, view, to) for to in over_z]
    got(g1_y)
    r.G[3] = r.G[2] + r.GR[2]
    r.GZ[z] = r.G[3]
    g1_z = [send(r.G.at[3], r.GZ.at[z], to) for to in over_z]
    got(gb_x)
    view = r.QA.at[z, :, c, :, two]
    gb_z = [send(view, view, to) for to in over_z]
    got(pa_x)
    pa_c = send(r.PA.at[:, :, c], r.PA.at[:, :, c], over_c)
    got(k_y)
    r.gkv[...] = r.KY[0] + r.KY[1]
    got(*ga_z)
    view = r.QA.at[:, x, c, :, one]
    ga_x = send(view, view, over_x)
    got(*g1_z)
    v = r.GZ[0]
    for k in range(1, nz):
        v = v + r.GZ[k]
    r.gain1_out[...] = v
    got(*gb_z)
    view = r.QA.at[:, :, c, :, two]
    gb_c = send(view, view, over_c)
    got(ga_x)
    view = r.QA.at[:, :, c, :, one]
    ga_c = send(view, view, over_c)
    got(pa_c, gb_c, ga_c)
    l_out.wait()
    for copy in ends:
        copy.wait()
    got(out_y, *gts_y)
    for copy in sent:
        copy.wait_send()


def close(out, gt, QA, PA, gwh, gwT, gkv, small, gain1,
          o_out, o_gt, o_wq, o_wo, o_wh, o_wT, o_k, o_v, o_wr, o_g1, o_g2,
          b_q, b_o, b_k, b_s, sem):
    pairs = ((QA, b_q), (PA, b_o), (gkv, b_k), (small, b_s),
             (gt, o_gt), (out, o_out), (gwh, o_wh), (gwT, o_wT), (gain1, o_g1))
    copies = [pltpu.make_async_copy(a, b, sem.at[k]) for k, (a, b) in enumerate(pairs)]
    for copy in copies:
        copy.start()
    copies[0].wait()
    o_wq[...] = b_q[...].astype(f32)
    copies[1].wait()
    o_wo[...] = b_o[...].astype(f32)
    copies[2].wait()
    o_k[...] = b_k[:, 0:64]
    o_v[...] = b_k[:, 64:128]
    copies[3].wait()
    o_wr[...] = b_s[0 : o_wr.shape[0], :]
    o_g2[...] = b_s[31:32, :]
    for copy in copies[4:]:
        copy.wait()


def shards(
    tokens, gain_attn, w_key, w_value, w_router, w_query, w_out, gain_ffn,
    w_hidden, w_output, expert_ids, lengths, grad_out,
):
    rows, width = tokens.shape
    dp = lax.axis_size("dp")
    inner = min(dp, 16)
    outer = dp // inner
    nz = inner // 4
    nb = rows // rb // 2
    top = expert_ids.shape[1]
    n_experts = w_router.shape[1]
    half = w_query.shape[1]
    ffh = w_hidden.shape[1]
    near = [[g * outer + k for k in range(outer)] for g in range(inner)]
    wt = w_output.T
    if outer > 1:
        w_key, w_value, w_hidden, wt = (
            lax.all_gather(v, "dp", axis=0, tiled=True, axis_index_groups=near)
            for v in (w_key, w_value, w_hidden, wt)
        )
    shard = width // inner
    woc = half // inner
    sds = jax.ShapeDtypeStruct
    spec = scratch(rows, width, nb, top, 2 * half, 2 * ffh, nz, shard)
    names = in_names + out_names + list(spec)
    vmem = pl.BlockSpec(memory_space=pltpu.VMEM)
    anyw = pl.BlockSpec(memory_space=pl.ANY)
    out, gt, QA, PA, gwh, gwT, gkv, small, gain1 = pl.pallas_call(
        functools.partial(kernel, names, outer),
        out_shape=(
            sds((nb, 2, rb, width // 2), bf16),
            sds((nb, 2, rb, width), bf16),
            sds((nz, 2, 2, shard, half), bf16),
            sds((nz, 2, 2, woc, width), bf16),
            sds((shard, ffh), f32),
            sds((shard, ffh), f32),
            sds((shard, 128), f32),
            sds((32, width), f32),
            sds((1, width), f32),
        ),
        in_specs=[pl.BlockSpec(memory_space=pltpu.SMEM)] + [anyw] + [vmem] * 6 + [anyw] * 5,
        out_specs=[anyw] * 2 + [vmem] * 7,
        scratch_shapes=list(spec.values()),
        compiler_params=pltpu.CompilerParams(
            collective_id=0, has_side_effects=True, vmem_limit_bytes=63 * 2**20
        ),
    )(
        lengths, tokens.reshape(2 * nb, rb, width), gain_attn[None], w_router.T, gain_ffn[None],
        expert_ids.T, w_key, w_value, w_query, w_out, w_hidden, wt,
        grad_out.reshape(nb, 2, rb, width // 2),
    )
    out, gt, gwq, gwo, gwh, gwT, gk, gv, gwr, g1, g2 = pl.pallas_call(
        close,
        out_shape=(
            sds(out.shape, bf16),
            sds(gt.shape, bf16),
            sds((width, half), f32),
            sds((half, width), f32),
            sds((shard, ffh), f32),
            sds((shard, ffh), f32),
            sds((shard, 64), f32),
            sds((shard, 64), f32),
            sds((n_experts, width), f32),
            sds((1, width), f32),
            sds((1, width), f32),
        ),
        in_specs=[anyw] * 9,
        out_specs=[vmem] * 11,
        scratch_shapes=[
            pltpu.VMEM((width, half), bf16),
            pltpu.VMEM((half, width), bf16),
            pltpu.VMEM((shard, 128), f32),
            pltpu.VMEM((32, width), f32),
            pltpu.SemaphoreType.DMA((9,)),
        ],
        compiler_params=pltpu.CompilerParams(vmem_limit_bytes=63 * 2**20),
    )(out, gt, QA.reshape(width, half), PA.reshape(half, width), gwh, gwT, gkv, small, gain1)
    if outer > 1:
        gwq, gwo, gwr, g1, g2 = lax.psum(
            (gwq, gwo, gwr, g1, g2), "dp", axis_index_groups=near
        )
        gwh, gwT, gk, gv = (
            lax.psum_scatter(v, "dp", scatter_dimension=0, tiled=True, axis_index_groups=near)
            for v in (gwh, gwT, gk, gv)
        )
    return (
        out.reshape(rows, width // 2), gt.reshape(rows, width), gk, gv, gwr.T, gwq, gwo,
        gwh, gwT.T, g1[0], g2[0],
    )


def solution(mesh):
    placed = (
        P("dp", None), P(), P("dp", None), P("dp", None), P(), P(None, "expert"),
        P("expert", None), P(), P("dp", "expert"), P("expert", "dp"), P("dp", None),
        P("dp"), P("dp", "expert"),
    )
    return jax.shard_map(
        shards,
        mesh=mesh,
        in_specs=placed,
        out_specs=(
            P("dp", "expert"), P("dp", None), P("dp", None), P("dp", None), P(),
            P(None, "expert"), P("expert", None), P("dp", "expert"), P("expert", "dp"),
            P(), P(),
        ),
        check_vma=False,
    )
```

```python
import functools

import jax
import jax.numpy as jnp
from jax import lax
from jax.experimental import pallas as pl
from jax.experimental.pallas import tpu as pltpu
from jax.sharding import PartitionSpec as P

f32 = jnp.float32
bf16 = jnp.bfloat16
eps = 1e-05
lowest = -1e30
rb = 128


def nn(left, right):
    return jnp.dot(left, right, preferred_element_type=f32)


def nt(left, right):
    return lax.dot_general(left, right, (((1,), (1,)), ((), ())), preferred_element_type=f32)


def tn(left, right):
    return lax.dot_general(left, right, (((0,), (0,)), ((), ())), preferred_element_type=f32)


def norm_rows(x):
    centred = x - jnp.mean(x, axis=-1, keepdims=True)
    inv = lax.rsqrt(jnp.mean(centred * centred, axis=-1, keepdims=True) + eps)
    return centred * inv, inv


def norm_back(u, normed, inv, gain):
    w = u * gain
    return inv * (
        w
        - jnp.mean(w, axis=-1, keepdims=True)
        - normed * jnp.mean(w * normed, axis=-1, keepdims=True)
    )


def lanes(shape):
    return lax.broadcasted_iota(jnp.int32, shape, len(shape) - 1)


MESH = pl.DeviceIdType.MESH

in_names = [
    "len_ref",
    "tok_in",
    "gain1",
    "wrt",
    "gain2",
    "idst",
    "wk_in",
    "wv_in",
    "wq_in",
    "wo_in",
    "wh_in",
    "wt_in",
    "go_in",
]
out_names = [
    "out",
    "gt",
    "QA",
    "PA",
    "gwh",
    "gwT",
    "gkv",
    "small",
    "gain1_out",
]


def scratch(rows, width, nb, top, fq, ff, nz, shard):
    vm = pltpu.VMEM
    own = rows // 2
    half = fq // 2
    total = 128 * nb * (nb + 1)
    ring = (nz, 2, 2)
    ch = ff // 4
    woc = half // (4 * nz)
    return {
        "tok": vm((2 * nb, rb, width), bf16),
        "outm": vm((nb, rb, width // 2), bf16),
        "gts": vm((nb, rb, width), bf16),
        "G": vm((4, 1, width), f32),
        "GR": vm((3, 1, width), f32),
        "GZ": vm((nz, 1, width), f32),
        "wkvg": vm(ring + (shard, 128), bf16),
        "W": vm((2, 2) + ring + (shard, 2 * ch), bf16),
        "WQ": vm((2, width, half), bf16),
        "WO": vm((2, half, width), bf16),
        "GO": vm((2, nb, rb, width // 2), bf16),
        "h1": vm((2 * nb, rb, width), bf16),
        "h1T": vm((width, own), bf16),
        "KK": vm((rows, 128), bf16),
        "VV": vm((rows, 128), bf16),
        "KKT": vm((128, rows), bf16),
        "VVT": vm((128, rows), bf16),
        "idl": vm((nb, top, rb, 128), jnp.int32),
        "gateb": vm((nb, top, rb, 128), f32),
        "dense": vm((own, 128), f32),
        "Qs": vm((nb, top, rb, 128), bf16),
        "PT": vm((total, top * rb), bf16),
        "O": vm((nb, top, rb, 128), f32),
        "wide": vm((rb, fq), f32),
        "gated": vm((own, fq), bf16),
        "n2": vm((own, width), f32),
        "r2": vm((own, 1), f32),
        "res": vm((own, width), f32),
        "h2": vm((own, width), bf16),
        "h2T": vm((width, own), bf16),
        "gfT": vm((width, own), bf16),
        "gf": vm((own, width), bf16),
        "gh2": vm((own, width), f32),
        "acc": vm((own, width), f32),
        "gatt": vm((own, width), bf16),
        "dOs": vm((nb, top, rb, 128), bf16),
        "glog": vm((own, 128), bf16),
        "AG": vm((own, 2 * ch), bf16),
        "wrp": vm((128, width), bf16),
        "gK": vm((rows, 128), f32),
        "gV": vm((rows, 128), f32),
        "dQ": vm((top, rb, 128), f32),
        "gain_rows": vm((2, width), f32),
        "outx": vm((nb, rb, width // 2), bf16),
        "kvs": vm((nb, 2, rb, 128), bf16),
        "kvr": vm((nb, rb, 128), bf16),
        "F": vm((2, 2) + ring + (shard, 2 * ch), bf16),
        "FC": vm((2, 2, nz, 2, shard, 2 * ch), bf16),
        "FY0": vm((nz, 2, shard, 2 * ch), bf16),
        "FZ0": vm((nz - 1, 2, shard, 2 * ch), bf16),
        "FX0": vm((shard, 2 * ch), bf16),
        "FX1": vm((2, nz, shard, 2 * ch), bf16),
        "FY1": vm((nz, shard, 2 * ch), bf16),
        "FZ1": vm((nz - 1, shard, 2 * ch), bf16),
        "QC": vm((2, nz, 2, shard, half), bf16),
        "QXA": vm((2, nz, shard, half // 2), bf16),
        "QYA": vm((nz, shard, half // 2), bf16),
        "QYB": vm((nz, 2, shard, half // 2), bf16),
        "QXB": vm((nz, shard, half // 2), bf16),
        "QZ": vm((nz - 1, shard, half), bf16),
        "P": vm((2,) + ring + (woc, width), bf16),
        "PC": vm((2, nz, 2, woc, width), bf16),
        "PX": vm((2, nz, woc, width), bf16),
        "PY": vm((nz, woc, width), bf16),
        "PZ": vm((nz - 1, woc, width), bf16),
        "K": vm(ring + (shard, 128), f32),
        "KC": vm((nz, 2, shard, 128), f32),
        "KX": vm((nz, shard, 128), f32),
        "KZ": vm((nz - 1, shard, 128), f32),
        "KY": vm((2, shard, 128), f32),
        "S": vm((4, 32, width), f32),
        "SR": vm((3, 32, width), f32),
        "SZ": vm((nz, 32, width), f32),
        "send": pltpu.SemaphoreType.DMA((128,)),
        "recv": pltpu.SemaphoreType.DMA((128,)),
        "local": pltpu.SemaphoreType.DMA((16,)),
    }


class Refs:
    pass


def kernel(names, outer, *refs):
    r = Refs()
    for name, ref in zip(names, refs):
        setattr(r, name, ref)
    nb = r.tok.shape[0] // 2
    width = r.tok.shape[2]
    top = r.idst.shape[0]
    fq = r.gated.shape[1]
    half = fq // 2
    groups = fq // 128
    r.gq = r.gated
    r.Q = r.W.at[0, :, :, :, :, :, 0:half]
    r.actS = r.AG.at[:, 0 : r.W.shape[6] // 2]
    r.giS = r.AG.at[:, r.W.shape[6] // 2 : r.W.shape[6]]
    nz = r.W.shape[2]
    ch = r.W.shape[6] // 2
    shard = r.W.shape[5]
    d = lax.axis_index("dp")
    y = lax.axis_index("expert")
    n, m = d // outer, d % outer
    z, x, c = n // 4, (n // 2) % 2, n % 2
    length = r.len_ref[0]

    def device(z, x, c, y):
        return ((z * 4 + x * 2 + c) * outer + m, y)

    over_c = device(z, x, 1 - c, y)
    over_x = device(z, 1 - x, c, y)
    over_y = device(z, x, c, 1 - y)
    zs = [(z + k) % nz for k in range(1, nz)]
    over_z = [device(k, x, c, y) for k in zs]
    used = [0]
    sent = []

    def send(source, target, to):
        k = used[0]
        used[0] += 1
        copy = pltpu.make_async_remote_copy(
            src_ref=source, dst_ref=target, send_sem=r.send.at[k], recv_sem=r.recv.at[k],
            device_id=to, device_id_type=MESH,
        )
        copy.start()
        sent.append(copy)
        return copy

    def here(k, source, target):
        copy = pltpu.make_async_copy(source, target, r.local.at[k])
        copy.start()
        return copy

    def got(*copies):
        for copy in copies:
            copy.wait_recv()

    def own(i):
        return 2 * i + y

    def cut(i, size):
        return pl.ds(pl.multiple_of(i * size, size), size)

    def valid_rows(i):
        return (rb * own(i) + lax.broadcasted_iota(jnp.int32, (rb, 1), 0) < length).astype(f32)

    l_tok = here(7, r.tok_in, r.tok)
    l_w = [
        here(2 * j + k, ref.at[:, j * ch : (j + 1) * ch],
             r.W.at[j, y, z, x, c, :, k * ch : (k + 1) * ch])
        for j in range(2)
        for k, ref in enumerate((r.wh_in, r.wt_in))
    ]
    l_q = here(4, r.wq_in, r.WQ.at[y])
    l_o = here(5, r.wo_in, r.WO.at[y])
    l_g = here(6, r.go_in.at[:, y], r.GO.at[y])
    r.wkvg[z, x, c] = jnp.concatenate((r.wk_in[...], r.wv_in[...]), axis=1)
    barrier = pltpu.get_barrier_semaphore()
    peers = [over_c, over_x, over_y] + over_z
    for peer in peers:
        pl.semaphore_signal(barrier, inc=1, device_id=peer, device_id_type=MESH)
    pl.semaphore_wait(barrier, len(peers))
    kv_z = [send(r.wkvg.at[z, x, c], r.wkvg.at[z, x, c], to) for to in over_z]
    l_w[0].wait()
    l_w[1].wait()
    w_y0 = send(r.W.at[0, y, z, x, c], r.W.at[0, y, z, x, c], over_y)
    qrows = cut(c, width // 2)
    q_y = send(r.wq_in.at[qrows, :], r.WQ.at[y, qrows, :], over_y)
    l_w[2].wait()
    l_w[3].wait()
    w_y1 = send(r.W.at[1, y, z, x, c], r.W.at[1, y, z, x, c], over_y)
    orows = cut(c, half // 2)
    o_y = send(r.wo_in.at[orows, :], r.WO.at[y, orows, :], over_y)
    g_y = send(r.go_in.at[:, 1 - y], r.GO.at[y], over_y)
    spare = jnp.zeros((128 - r.wrt.shape[0], width), f32)
    r.wrp[...] = jnp.concatenate((r.wrt[...].astype(f32), spare), axis=0).astype(bf16)

    def w_part(k):
        return r.W.at[k // 2, :, :, :, :, :, pl.ds((k % 2) * ch, ch)]

    def w_over_z(k, both=False):
        view = w_part(k).at[:, z, :, c] if both else w_part(k).at[:, z, x, c]
        return [send(view, view, to) for to in over_z]

    def w_over_x(k, line=True):
        view = w_part(k).at[:, :, x, c] if line else w_part(k).at[:, z, x, c]
        return send(view, view, over_x)

    def w_over_c(k):
        view = w_part(k).at[:, :, :, c]
        return send(view, view, over_c)
    l_tok.wait()

    @pl.loop(0, 2 * nb)
    def _(b):
        normed, _ = norm_rows(r.tok[b].astype(f32))
        r.h1[b] = (normed * r.gain1[...]).astype(bf16)
    got(*kv_z)
    kv_x = send(r.wkvg.at[:, x, c], r.wkvg.at[:, x, c], over_x)
    got(w_y0)
    w0_z = w_over_z(0)
    w1_z = w_over_z(1)

    lane = lanes((rb, 128))
    upper = (lane >= 64).astype(jnp.int32)

    def gates(i):
        h = r.h1[own(i)]
        at = cut(i, rb)
        r.h1T[:, at] = h.astype(f32).T.astype(bf16)
        logits = nt(h, r.wrp[...])
        ids = r.idst[:, cut(own(i), rb)].astype(f32).T.astype(jnp.int32)
        spread = [jnp.broadcast_to(ids[:, k : k + 1], (rb, 128)) for k in range(top)]
        chosen = lane == spread[0]
        for k in range(1, top):
            chosen = chosen | (lane == spread[k])
        most = jnp.max(jnp.where(chosen, logits, lowest), axis=-1, keepdims=True)
        e = jnp.where(chosen, jnp.exp(jnp.where(chosen, logits - most, 0.0)), 0.0)
        g = e / jnp.sum(e, axis=-1, keepdims=True)
        r.dense[at, :] = g
        for k in range(top):
            gk = jnp.sum(jnp.where(lane == spread[k], g, 0.0), axis=-1, keepdims=True)
            r.gateb[i, k] = jnp.broadcast_to(gk, (rb, 128))
            r.idl[i, k] = spread[k] - upper

    pl.loop(0, nb // 2)(gates)
    got(kv_x)
    kv_c = send(r.wkvg.at[:, :, c], r.wkvg.at[:, :, c], over_c)
    pl.loop(nb // 2, nb)(gates)
    got(kv_c)

    @pl.loop(0, 2 * nb)
    def _(b):
        kv = nn(r.h1[b], r.wkvg[...].reshape(width, 128))
        at = cut(b, rb)
        swapped = pltpu.roll(kv, 64, 1)
        k2 = jnp.where(lane < 64, kv, swapped)
        v2 = jnp.where(lane < 64, swapped, kv)
        r.KK[at, :] = k2.astype(bf16)
        r.VV[at, :] = v2.astype(bf16)
        r.KKT[:, at] = k2.T.astype(bf16)
        r.VVT[:, at] = v2.T.astype(bf16)
    got(*w0_z)
    w0_x = w_over_x(0)
    got(q_y)
    q_c = send(r.WQ.at[1 - y, qrows, :], r.WQ.at[1 - y, qrows, :], over_c)
    got(w_y1)
    w3_x = w_over_x(3, False)
    w2_z = w_over_z(2)
    l_q.wait()
    got(q_c)

    @pl.loop(0, nb)
    def _(i):
        h = r.h1[own(i)]
        for e in range(2):
            r.wide[:, e * half : (e + 1) * half] = 0.125 * nn(h, r.WQ[e])

        @pl.loop(0, rb // 16, unroll=4)
        def _(t):
            at = cut(t, 16)
            parts = [r.wide[at, pl.ds(128 * g, 128)] for g in range(groups)]
            for k in range(top):
                mine = r.idl[i, k, at, :]
                val = jnp.zeros((16, 128), f32)
                for g in range(groups):
                    val = jnp.where(mine == 2 * g, parts[g], val)
                r.Qs[i, k, at, :] = val.astype(bf16)
    diag = lax.broadcasted_iota(jnp.int32, (256, 256), 0) <= rb * y + lanes((256, 256)) % 128

    def attend(i):
        nk = 256 * i
        start = 128 * i * (i + 1)

        @pl.loop(0, top // 2, unroll=4)
        def _(p):
            q = r.Qs[i, pl.ds(2 * p, 2)].reshape(256, 128)
            cols = cut(p, 256)
            s1 = nt(r.KK[nk : nk + 256, :], q)
            s1 = jnp.where(diag, s1, lowest)
            most = jnp.max(s1, axis=0, keepdims=True)
            if nk:
                s0 = nt(r.KK[0:nk, :], q)
                most = jnp.maximum(most, jnp.max(s0, axis=0, keepdims=True))
                p0 = jnp.exp(s0 - most)
            p1 = jnp.exp(s1 - most)
            tot = jnp.sum(p1, axis=0, keepdims=True)
            if nk:
                tot = tot + jnp.sum(p0, axis=0, keepdims=True)
            inv = 1.0 / tot
            p1 = (p1 * inv).astype(bf16)
            r.PT[start + nk : start + nk + 256, cols] = p1
            o = nn(r.VVT[:, nk : nk + 256], p1)
            if nk:
                p0 = (p0 * inv).astype(bf16)
                r.PT[start : start + nk, cols] = p0
                o = o + nn(r.VVT[:, 0:nk], p0)
            r.O[i, pl.ds(2 * p, 2)] = o.T.reshape(2, rb, 128)

    got(w3_x)
    w3_z = w_over_z(3, True)
    got(*w1_z)
    w1_x = w_over_x(1)
    attend(0)
    attend(1)
    got(*w2_z)
    w2_x = w_over_x(2)
    got(w0_x)
    w0_c = w_over_c(0)
    attend(2)
    got(w1_x)
    w1_c = w_over_c(1)
    got(o_y)
    o_c = send(r.WO.at[1 - y, orows, :], r.WO.at[1 - y, orows, :], over_c)
    for i in range(3, nb):
        attend(i)
    l_o.wait()
    l_g.wait()
    got(o_c)
    got(g_y)
    def project(i):
        at = cut(i, rb)

        @pl.loop(0, rb // 16, unroll=4)
        def _(t):
            at = cut(t, 16)
            atr = pl.ds(pl.multiple_of(i * rb + t * 16, 16), 16)
            mine = [r.idl[i, k, at, :] for k in range(top)]
            vals = [r.gateb[i, k, at, :] * r.O[i, k, at, :] for k in range(top)]
            for g in range(groups):
                val = jnp.zeros((16, 128), f32)
                for k in range(top):
                    val = jnp.where(mine[k] == 2 * g, vals[k], val)
                r.gated[atr, pl.ds(128 * g, 128)] = val.astype(bf16)

        valid = valid_rows(i)
        att = nn(r.gated[at, 0:half], r.WO[0]) + nn(r.gated[at, half:fq], r.WO[1])
        row = r.tok[own(i)].astype(f32) + valid * att
        r.res[at, :] = row
        normed, inv = norm_rows(row)
        r.n2[at, :] = normed
        r.r2[at, :] = inv
        h = normed * r.gain2[...]
        r.h2[at, :] = h.astype(bf16)
        r.h2T[:, at] = h.T.astype(bf16)
        for s in range(2):
            side = pl.ds(s * (width // 2), width // 2)
            g = valid * r.GO[s, i].astype(f32)
            r.gf[at, side] = g.astype(bf16)
            r.gfT[side, at] = g.T.astype(bf16)

    pl.loop(0, nb)(project)

    c0 = 0.7978845608028654
    c1 = 0.044715

    def feed(j, e, first=False):

        w1 = r.W[j, e, :, :, :, :, 0:ch].reshape(width, ch)
        w2 = r.W[j, e, :, :, :, :, ch : 2 * ch].reshape(width, ch)
        for i in range(nb // 2):
            at = pl.ds(i * 256, 256)
            v = nn(r.h2[at, :], w1)
            ga = nn(r.gf[at, :], w2)
            vv = v * v
            hp = 0.5 + 0.5 * jnp.tanh(v * (c0 + (c0 * c1) * vv))
            act = v * hp
            slope = hp + act * (1.0 - hp) * (2 * c0 + (6 * c0 * c1) * vv)
            r.actS[at, :] = act.astype(bf16)
            r.giS[at, :] = (slope * ga).astype(bf16)
        a = nt(r.actS[...], w2)
        b = nt(r.giS[...], w1)
        if first:
            r.acc[...] = a
            r.gh2[...] = b
        else:
            r.acc[...] += a
            r.gh2[...] += b

        shape = (nz, 2, 2, shard, ch)
        r.F[j, e, :, :, :, :, 0:ch] = nn(r.h2T[...], r.giS[...]).astype(bf16).reshape(shape)
        r.F[j, e, :, :, :, :, ch : 2 * ch] = (
            nn(r.gfT[...], r.actS[...]).astype(bf16).reshape(shape)
        )
        return send(r.F.at[j, e, :, :, 1 - c], r.FC.at[j, e], over_c)

    def f_add_c(j, e):
        @pl.loop(0, 2 * nz)
        def _(t):
            a, b = t // 2, t % 2
            r.F[j, e, a, b, c] = r.F[j, e, a, b, c] + r.FC[j, e, a, b]
    got(w0_c, w1_c)
    f0p = feed(0, 1 - y, True)
    got(w2_x)
    w2_c = w_over_c(2)
    f0m = feed(0, y)
    got(f0p)
    f_add_c(0, 1 - y)
    f0_y = send(r.F.at[0, 1 - y, :, :, c], r.FY0, over_y)
    got(*w3_z)
    w3_c = w_over_c(3)
    got(f0m)
    f_add_c(0, y)
    got(w2_c, w3_c)
    f1p = feed(1, 1 - y)
    f1m = feed(1, y)
    got(f1p)
    f_add_c(1, 1 - y)
    f1_xa = send(r.F.at[1, 1 - y, :, 1 - x, c], r.FX1.at[0], over_x)
    r.gain_rows[...] = jnp.zeros_like(r.gain_rows)

    def turn(i):
        at = cut(i, rb)
        valid = valid_rows(i)
        outs = (r.res[at, :] + valid * r.acc[at, :]).astype(bf16)
        mine, other = outs[:, : width // 2], outs[:, width // 2 :]
        low = y == 0
        r.outm[i] = jnp.where(low, mine, other)
        r.outx[i] = jnp.where(low, other, mine)
        u, normed = r.gh2[at, :], r.n2[at, :]
        r.gain_rows[1:2, :] += jnp.sum(u * normed, axis=0, keepdims=True)
        back = norm_back(u, normed, r.r2[at, :], r.gain2[...])
        go = jnp.concatenate((r.GO[0, i], r.GO[1, i]), axis=1).astype(f32)
        gr = go + back
        r.res[at, :] = gr
        ga = (valid * gr).astype(bf16)
        r.gatt[at, :] = ga
        for e in range(2):
            r.wide[:, e * half : (e + 1) * half] = nt(ga, r.WO[e])

        @pl.loop(0, rb // 16, unroll=4)
        def _(t):
            at = cut(t, 16)
            atr = pl.ds(pl.multiple_of(i * rb + t * 16, 16), 16)
            parts = [r.wide[at, pl.ds(128 * g, 128)] for g in range(groups)]
            ln = lanes((16, 128))
            hf = (ln >= 64).astype(jnp.int32)
            gd = jnp.zeros((16, 128), f32)
            for k in range(top):
                mine = r.idl[i, k, at, :]
                val = jnp.zeros((16, 128), f32)
                for g in range(groups):
                    val = jnp.where(mine == 2 * g, parts[g], val)
                dot = jnp.sum(val * r.O[i, k, at, :], axis=-1, keepdims=True)
                gd = jnp.where(mine + hf == ln, dot, gd)
                r.dOs[i, k, at, :] = (r.gateb[i, k, at, :] * val).astype(bf16)
            dn = r.dense[atr, :]
            gs = dn * (gd - jnp.sum(dn * gd, axis=-1, keepdims=True))
            r.glog[atr, :] = gs.astype(bf16)

    pl.loop(0, nb // 2)(turn)
    got(f1m)
    f_add_c(1, y)
    f1_xb = send(r.F.at[1, y, :, 1 - x, c], r.FX1.at[1], over_x)
    pl.loop(nb // 2, nb)(turn)
    l_out = here(8, r.outm, r.out.at[:, y])
    routed = jnp.zeros((128, width), f32)
    for i in range(nb):
        routed = routed + tn(r.glog[i * rb : (i + 1) * rb, :], r.h1[own(i)])
    r.S[0] = routed[0:32]
    r.S[0, 31:32, :] = r.gain_rows[1:2, :]
    s_c = send(r.S.at[0], r.SR.at[0], over_c)
    got(f0_y)

    @pl.loop(0, 2 * nz)
    def _(t):
        a, b = t // 2, t % 2
        r.F[0, y, a, b, c] = r.F[0, y, a, b, c] + r.FY0[a, b]

    f0_z = [
        send(r.F.at[0, y, k, :, c], r.FZ0.at[i], to) for i, (k, to) in enumerate(zip(zs, over_z))
    ]

    woc = r.P.shape[4]
    for e in range(2):
        r.P[e] = (
            tn(r.gated[:, e * half : (e + 1) * half], r.gatt[...])
            .astype(bf16)
            .reshape(nz, 2, 2, woc, width)
        )
    p_c = send(r.P.at[:, :, :, 1 - c], r.PC, over_c)

    def back(i):
        nk = 256 * (i + 1)
        start = 128 * i * (i + 1)
        last = i == nb - 1
        v = nn(r.PT[start : start + nk, :], r.dOs[i].reshape(top * rb, 128))
        r.gV[0:nk, :] = v if last else r.gV[0:nk, :] + v

        @pl.loop(0, top // 2, unroll=4)
        def _(p):
            do = r.dOs[i, pl.ds(2 * p, 2)].reshape(256, 128)
            cols = cut(p, 256)
            dp = nt(r.VV[0:nk, :], do)
            pr = r.PT[start : start + nk, cols].astype(f32)
            s = jnp.sum(pr * dp, axis=0, keepdims=True)
            ds = (pr * (dp - s)).astype(bf16)
            r.PT[start : start + nk, cols] = ds
            dq = nn(r.KKT[:, 0:nk], ds)
            r.dQ[pl.ds(2 * p, 2)] = dq.T.reshape(2, rb, 128)

        @pl.loop(0, rb // 16, unroll=4)
        def _(t):
            at = cut(t, 16)
            atr = pl.ds(pl.multiple_of(i * rb + t * 16, 16), 16)
            mine = [r.idl[i, k, at, :] for k in range(top)]
            vals = [r.dQ[k, at, :] for k in range(top)]
            for g in range(groups):
                val = jnp.zeros((16, 128), f32)
                for k in range(top):
                    val = jnp.where(mine[k] == 2 * g, vals[k], val)
                r.gq[atr, pl.ds(128 * g, 128)] = val.astype(bf16) * 0.125

    def key_sums(i):
        v = nn(r.PT[128 * i * (i + 1) : 128 * (i + 1) * (i + 2), :], r.Qs[i].reshape(top * rb, 128))
        at = pl.ds(0, 256 * (i + 1))
        r.gK[at, :] = v if i == nb - 1 else r.gK[at, :] + v
        for s in range(2):
            at = pl.ds((2 * i + s) * rb, rb)
            a, b = r.gK[at, :], r.gV[at, :]
            a = a + pltpu.roll(a, 64, 1)
            b = b + pltpu.roll(b, 64, 1)
            r.kvs[i, s] = jnp.where(lane < 64, a, b).astype(bf16)
        return send(r.kvs.at[i, 1 - y], r.kvr.at[i], over_y)

    def finish(i):
        at = pl.ds(i * rb, rb)
        low = (r.kvs[i, y].astype(f32) + r.kvr[i].astype(f32)).astype(bf16)
        r.kvr[i] = low
        g = nn(r.glog[at, :], r.wrp[...]) + nt(low, r.wkvg[...].reshape(width, 128))
        for e in range(2):
            g = g + nt(r.gq[at, e * half : (e + 1) * half], r.WQ[e])
        normed, inv = norm_rows(r.tok[own(i)].astype(f32))
        r.gain_rows[0:1, :] += jnp.sum(g * normed, axis=0, keepdims=True)
        back = norm_back(g, normed, inv, r.gain1[...])
        r.gts[i] = (r.res[at, :] + back).astype(bf16)
        return here(9 + i, r.gts.at[i], r.gt.at[i, y])

    def give(i):
        return send(r.gts.at[i], r.gt.at[i, y], over_y)

    keys, ends = {}, []
    for i in range(nb - 1, 2, -1):
        back(i)
        keys[i] = key_sums(i)
    got(s_c)
    r.S[1] = r.S[0] + r.SR[0]
    s_x = send(r.S.at[1], r.SR.at[1], over_x)
    got(p_c)

    @pl.loop(0, 4 * nz)
    def _(t):
        e, a, b = t // (2 * nz), (t // 2) % nz, t % 2
        r.P[e, a, b, c] = r.P[e, a, b, c] + r.PC[e, a, b]

    p_x = send(r.P.at[:, :, 1 - x, c], r.PX, over_x)
    got(f1_xa, f1_xb)

    @pl.loop(0, nz)
    def _(a):
        r.F[1, 1 - y, a, x, c] = r.F[1, 1 - y, a, x, c] + r.FX1[0, a]
        r.F[1, y, a, x, c] = r.F[1, y, a, x, c] + r.FX1[1, a]

    f1_y = send(r.F.at[1, 1 - y, :, x, c], r.FY1, over_y)
    back(2)
    keys[2] = key_sums(2)
    for i in range(nb - 1, 2, -1):
        got(keys[i])
        ends.append(finish(i))
    gts_y = [give(i) for i in range(nb - 1, 2, -1)]
    got(s_x)
    r.S[2] = r.S[1] + r.SR[1]
    s_y = send(r.S.at[2], r.SR.at[2], over_y)
    got(*f0_z)
    for b in range(2):
        v = r.F[0, y, z, b, c].astype(f32)
        for k in range(nz - 1):
            v = v + r.FZ0[k, b].astype(f32)
        r.F[0, y, z, b, c] = v.astype(bf16)
    f0_x = send(r.F.at[0, y, z, 1 - x, c], r.FX0, over_x)
    back(1)
    keys[1] = key_sums(1)
    got(p_x)

    @pl.loop(0, 2 * nz)
    def _(t):
        e, a = t // nz, t % nz
        r.P[e, a, x, c] = r.P[e, a, x, c] + r.PX[e, a]

    p_y = send(r.P.at[1 - y, :, x, c], r.PY, over_y)
    got(f1_y)

    @pl.loop(0, nz)
    def _(a):
        r.F[1, y, a, x, c] = r.F[1, y, a, x, c] + r.FY1[a]

    f1_z = [
        send(r.F.at[1, y, k, x, c], r.FZ1.at[i], to) for i, (k, to) in enumerate(zip(zs, over_z))
    ]
    got(keys[2])
    ends.append(finish(2))
    back(0)
    for copy in [w_y0, w_y1, w3_x, w0_x, w1_x, w2_x, w0_c, w1_c, w2_c, w3_c,
                 *w0_z, *w1_z, *w2_z, *w3_z]:
        copy.wait_send()
        sent[:] = [other for other in sent if other is not copy]
    for e in range(2):
        r.Q[e] = (
            nn(r.h1T[...], r.gq[:, e * half : (e + 1) * half])
            .astype(bf16)
            .reshape(nz, 2, 2, shard, half)
        )
    q_c2 = send(r.Q.at[:, :, :, 1 - c], r.QC, over_c)
    keys[0] = key_sums(0)
    got(s_y)
    r.S[3] = r.S[2] + r.SR[2]
    r.SZ[z] = r.S[3]
    s_z = [send(r.S.at[3], r.SZ.at[z], to) for to in over_z]
    got(q_c2)

    @pl.loop(0, 4 * nz)
    def _(t):
        e, a, b = t // (2 * nz), (t // 2) % nz, t % 2
        r.Q[e, a, b, c] = r.Q[e, a, b, c] + r.QC[e, a, b]

    one, two = pl.ds(0, half // 2), pl.ds(half // 2, half // 2)
    qa_x = send(r.Q.at[:, :, 1 - x, c, :, one], r.QXA, over_x)
    qb_y = send(r.Q.at[1 - y, :, :, c, :, two], r.QYB, over_y)
    gts_y.append(give(2))
    got(keys[1])
    ends.append(finish(1))
    got(p_y)

    @pl.loop(0, nz)
    def _(a):
        r.P[y, a, x, c] = r.P[y, a, x, c] + r.PY[a]

    p_z = [send(r.P.at[y, k, x, c], r.PZ.at[i], to) for i, (k, to) in enumerate(zip(zs, over_z))]
    got(f0_x)
    v = r.F[0, y, z, x, c].astype(f32) + r.FX0[...].astype(f32)
    r.gwh[:, 0:ch] = v[:, 0:ch]
    r.gwT[:, 0:ch] = v[:, ch : 2 * ch]
    got(keys[0])
    ends.append(finish(0))
    r.K[...] = nn(r.h1T[...], r.kvr[...].reshape(nb * rb, 128)).reshape(nz, 2, 2, shard, 128)
    k_c = send(r.K.at[:, :, 1 - c], r.KC, over_c)
    r.G[0] = r.gain_rows[0:1, :]
    g1_c = send(r.G.at[0], r.GR.at[0], over_c)
    got(qa_x)

    @pl.loop(0, 2 * nz)
    def _(t):
        e, a = t // nz, t % nz
        r.Q[e, a, x, c, :, one] = r.Q[e, a, x, c, :, one] + r.QXA[e, a]

    qa_y = send(r.Q.at[1 - y, :, x, c, :, one], r.QYA, over_y)
    got(qb_y)

    @pl.loop(0, 2 * nz)
    def _(t):
        a, b = t // 2, t % 2
        r.Q[y, a, b, c, :, two] = r.Q[y, a, b, c, :, two] + r.QYB[a, b]

    qb_x = send(r.Q.at[y, :, 1 - x, c, :, two], r.QXB, over_x)
    gts_y.append(give(1))
    gts_y.append(give(0))
    got(k_c)

    @pl.loop(0, 2 * nz)
    def _(t):
        a, b = t // 2, t % 2
        r.K[a, b, c] = r.K[a, b, c] + r.KC[a, b]

    k_x = send(r.K.at[:, 1 - x, c], r.KX, over_x)
    got(g1_c)
    r.G[1] = r.G[0] + r.GR[0]
    g1_x = send(r.G.at[1], r.GR.at[1], over_x)
    got(*p_z)
    v = r.P[y, z, x, c].astype(f32)
    for k in range(nz - 1):
        v = v + r.PZ[k].astype(f32)
    r.PA[z, x, c] = v.astype(bf16)
    pa_z = [send(r.PA.at[z, x, c], r.PA.at[z, x, c], to) for to in over_z]

    got(qa_y, qb_x)

    @pl.loop(0, nz)
    def _(a):
        r.Q[y, a, x, c, :, one] = r.Q[y, a, x, c, :, one] + r.QYA[a]
        r.Q[y, a, x, c, :, two] = r.Q[y, a, x, c, :, two] + r.QXB[a]

    q_z = [send(r.Q.at[y, k, x, c], r.QZ.at[i], to) for i, (k, to) in enumerate(zip(zs, over_z))]
    got(k_x)

    @pl.loop(0, nz)
    def _(a):
        r.K[a, x, c] = r.K[a, x, c] + r.KX[a]

    k_z = [send(r.K.at[k, x, c], r.KZ.at[i], to) for i, (k, to) in enumerate(zip(zs, over_z))]
    got(g1_x)
    r.G[2] = r.G[1] + r.GR[1]
    g1_y = send(r.G.at[2], r.GR.at[2], over_y)
    got(*f1_z)
    v = r.F[1, y, z, x, c].astype(f32)
    for k in range(nz - 1):
        v = v + r.FZ1[k].astype(f32)
    r.gwh[:, ch : 2 * ch] = v[:, 0:ch]
    r.gwT[:, ch : 2 * ch] = v[:, ch : 2 * ch]
    got(*s_z)
    v = r.SZ[0]
    for k in range(1, nz):
        v = v + r.SZ[k]
    r.small[...] = v
    got(*pa_z)
    pa_x = send(r.PA.at[:, x, c], r.PA.at[:, x, c], over_x)
    got(*k_z)
    v = r.K[z, x, c]
    for k in range(nz - 1):
        v = v + r.KZ[k]
    r.KY[0] = v
    k_y = send(r.KY.at[0], r.KY.at[1], over_y)
    out_y = send(r.outx, r.out.at[:, y], over_y)
    got(*q_z)
    v = r.Q[y, z, x, c].astype(f32)
    for k in range(nz - 1):
        v = v + r.QZ[k].astype(f32)
    r.QA[z, x, c] = v.astype(bf16)
    view = r.QA.at[z, x, c, :, two]
    gb_x = send(view, view, over_x)
    view = r.QA.at[z, x, c, :, one]
    ga_z = [send(view, view, to) for to in over_z]
    got(g1_y)
    r.G[3] = r.G[2] + r.GR[2]
    r.GZ[z] = r.G[3]
    g1_z = [send(r.G.at[3], r.GZ.at[z], to) for to in over_z]
    got(gb_x)
    view = r.QA.at[z, :, c, :, two]
    gb_z = [send(view, view, to) for to in over_z]
    got(pa_x)
    pa_c = send(r.PA.at[:, :, c], r.PA.at[:, :, c], over_c)
    got(k_y)
    r.gkv[...] = r.KY[0] + r.KY[1]
    got(*ga_z)
    view = r.QA.at[:, x, c, :, one]
    ga_x = send(view, view, over_x)
    got(*g1_z)
    v = r.GZ[0]
    for k in range(1, nz):
        v = v + r.GZ[k]
    r.gain1_out[...] = v
    got(*gb_z)
    view = r.QA.at[:, :, c, :, two]
    gb_c = send(view, view, over_c)
    got(ga_x)
    view = r.QA.at[:, :, c, :, one]
    ga_c = send(view, view, over_c)
    got(pa_c, gb_c, ga_c)
    l_out.wait()
    for copy in ends:
        copy.wait()
    got(out_y, *gts_y)
    for copy in sent:
        copy.wait_send()


def close(out, gt, QA, PA, gwh, gwT, gkv, small, gain1,
          o_out, o_gt, o_wq, o_wo, o_wh, o_wT, o_k, o_v, o_wr, o_g1, o_g2,
          b_q, b_o, b_k, b_s, sem):
    pairs = ((QA, b_q), (PA, b_o), (gkv, b_k), (small, b_s),
             (gt, o_gt), (out, o_out), (gwh, o_wh), (gwT, o_wT), (gain1, o_g1))
    copies = [pltpu.make_async_copy(a, b, sem.at[k]) for k, (a, b) in enumerate(pairs)]
    for copy in copies:
        copy.start()
    copies[0].wait()
    o_wq[...] = b_q[...].astype(f32)
    copies[1].wait()
    o_wo[...] = b_o[...].astype(f32)
    copies[2].wait()
    o_k[...] = b_k[:, 0:64]
    o_v[...] = b_k[:, 64:128]
    copies[3].wait()
    o_wr[...] = b_s[0 : o_wr.shape[0], :]
    o_g2[...] = b_s[31:32, :]
    for copy in copies[4:]:
        copy.wait()


def shards(
    tokens, gain_attn, w_key, w_value, w_router, w_query, w_out, gain_ffn,
    w_hidden, w_output, expert_ids, lengths, grad_out,
):
    rows, width = tokens.shape
    dp = lax.axis_size("dp")
    inner = min(dp, 16)
    outer = dp // inner
    nz = inner // 4
    nb = rows // rb // 2
    top = expert_ids.shape[1]
    n_experts = w_router.shape[1]
    half = w_query.shape[1]
    ffh = w_hidden.shape[1]
    near = [[g * outer + k for k in range(outer)] for g in range(inner)]
    wt = w_output.T
    if outer > 1:
        w_key, w_value, w_hidden, wt = (
            lax.all_gather(v, "dp", axis=0, tiled=True, axis_index_groups=near)
            for v in (w_key, w_value, w_hidden, wt)
        )
    shard = width // inner
    woc = half // inner
    sds = jax.ShapeDtypeStruct
    spec = scratch(rows, width, nb, top, 2 * half, 2 * ffh, nz, shard)
    names = in_names + out_names + list(spec)
    vmem = pl.BlockSpec(memory_space=pltpu.VMEM)
    anyw = pl.BlockSpec(memory_space=pl.ANY)
    out, gt, QA, PA, gwh, gwT, gkv, small, gain1 = pl.pallas_call(
        functools.partial(kernel, names, outer),
        out_shape=(
            sds((nb, 2, rb, width // 2), bf16),
            sds((nb, 2, rb, width), bf16),
            sds((nz, 2, 2, shard, half), bf16),
            sds((nz, 2, 2, woc, width), bf16),
            sds((shard, ffh), f32),
            sds((shard, ffh), f32),
            sds((shard, 128), f32),
            sds((32, width), f32),
            sds((1, width), f32),
        ),
        in_specs=[pl.BlockSpec(memory_space=pltpu.SMEM)] + [anyw] + [vmem] * 6 + [anyw] * 5,
        out_specs=[anyw] * 2 + [vmem] * 7,
        scratch_shapes=list(spec.values()),
        compiler_params=pltpu.CompilerParams(
            collective_id=0, has_side_effects=True, vmem_limit_bytes=63 * 2**20
        ),
    )(
        lengths, tokens.reshape(2 * nb, rb, width), gain_attn[None], w_router.T, gain_ffn[None],
        expert_ids.T, w_key, w_value, w_query, w_out, w_hidden, wt,
        grad_out.reshape(nb, 2, rb, width // 2),
    )
    out, gt, gwq, gwo, gwh, gwT, gk, gv, gwr, g1, g2 = pl.pallas_call(
        close,
        out_shape=(
            sds(out.shape, bf16),
            sds(gt.shape, bf16),
            sds((width, half), f32),
            sds((half, width), f32),
            sds((shard, ffh), f32),
            sds((shard, ffh), f32),
            sds((shard, 64), f32),
            sds((shard, 64), f32),
            sds((n_experts, width), f32),
            sds((1, width), f32),
            sds((1, width), f32),
        ),
        in_specs=[anyw] * 9,
        out_specs=[vmem] * 11,
        scratch_shapes=[
            pltpu.VMEM((width, half), bf16),
            pltpu.VMEM((half, width), bf16),
            pltpu.VMEM((shard, 128), f32),
            pltpu.VMEM((32, width), f32),
            pltpu.SemaphoreType.DMA((9,)),
        ],
        compiler_params=pltpu.CompilerParams(vmem_limit_bytes=63 * 2**20),
    )(out, gt, QA.reshape(width, half), PA.reshape(half, width), gwh, gwT, gkv, small, gain1)
    if outer > 1:
        gwq, gwo, gwr, g1, g2 = lax.psum(
            (gwq, gwo, gwr, g1, g2), "dp", axis_index_groups=near
        )
        gwh, gwT, gk, gv = (
            lax.psum_scatter(v, "dp", scatter_dimension=0, tiled=True, axis_index_groups=near)
            for v in (gwh, gwT, gk, gv)
        )
    return (
        out.reshape(rows, width // 2), gt.reshape(rows, width), gk, gv, gwr.T, gwq, gwo,
        gwh, gwT.T, g1[0], g2[0],
    )


def solution(mesh):
    placed = (
        P("dp", None), P(), P("dp", None), P("dp", None), P(), P(None, "expert"),
        P("expert", None), P(), P("dp", "expert"), P("expert", "dp"), P("dp", None),
        P("dp"), P("dp", "expert"),
    )
    return jax.shard_map(
        shards,
        mesh=mesh,
        in_specs=placed,
        out_specs=(
            P("dp", "expert"), P("dp", None), P("dp", None), P("dp", None), P(),
            P(None, "expert"), P("expert", None), P("dp", "expert"), P("expert", "dp"),
            P(), P(),
        ),
        check_vma=False,
    )
```

```python
import functools

import jax
import jax.numpy as jnp
from jax import lax
from jax.experimental import pallas as pl
from jax.experimental.pallas import tpu as pltpu
from jax.sharding import PartitionSpec as P

f32 = jnp.float32
bf16 = jnp.bfloat16
eps = 1e-05
lowest = -1e30
rb = 128


def nn(left, right):
    return jnp.dot(left, right, preferred_element_type=f32)


def nt(left, right):
    return lax.dot_general(left, right, (((1,), (1,)), ((), ())), preferred_element_type=f32)


def tn(left, right):
    return lax.dot_general(left, right, (((0,), (0,)), ((), ())), preferred_element_type=f32)


def norm_rows(x):
    centred = x - jnp.mean(x, axis=-1, keepdims=True)
    inv = lax.rsqrt(jnp.mean(centred * centred, axis=-1, keepdims=True) + eps)
    return centred * inv, inv


def norm_back(u, normed, inv, gain):
    w = u * gain
    return inv * (
        w
        - jnp.mean(w, axis=-1, keepdims=True)
        - normed * jnp.mean(w * normed, axis=-1, keepdims=True)
    )


def lanes(shape):
    return lax.broadcasted_iota(jnp.int32, shape, len(shape) - 1)


MESH = pl.DeviceIdType.MESH

in_names = [
    "len_ref",
    "tok_in",
    "gain1",
    "wrt",
    "gain2",
    "idst",
    "wk_in",
    "wv_in",
    "wq_in",
    "wo_in",
    "wh_in",
    "wt_in",
    "go_in",
]
out_names = [
    "out",
    "gt",
    "QA",
    "PA",
    "gwh",
    "gwT",
    "gkv",
    "small",
    "gain1_out",
]


def scratch(rows, width, nb, top, fq, ff, nz, shard):
    vm = pltpu.VMEM
    own = rows // 2
    half = fq // 2
    total = 128 * nb * (nb + 1)
    ring = (nz, 2, 2)
    ch = ff // 4
    woc = half // (4 * nz)
    return {
        "tok": vm((2 * nb, rb, width), bf16),
        "outm": vm((nb, rb, width // 2), bf16),
        "gts": vm((nb, rb, width), bf16),
        "G": vm((4, 1, width), f32),
        "GR": vm((3, 1, width), f32),
        "GZ": vm((nz, 1, width), f32),
        "wkvg": vm(ring + (shard, 128), bf16),
        "W": vm((2, 2) + ring + (shard, 2 * ch), bf16),
        "WQ": vm((2, width, half), bf16),
        "WO": vm((2, half, width), bf16),
        "GO": vm((2, nb, rb, width // 2), bf16),
        "h1": vm((2 * nb, rb, width), bf16),
        "h1T": vm((width, own), bf16),
        "KK": vm((rows, 128), bf16),
        "VV": vm((rows, 128), bf16),
        "KKT": vm((128, rows), bf16),
        "VVT": vm((128, rows), bf16),
        "idl": vm((nb, top, rb, 128), jnp.int32),
        "gateb": vm((nb, top, rb, 128), f32),
        "dense": vm((own, 128), f32),
        "Qs": vm((nb, top, rb, 128), bf16),
        "PT": vm((total, top * rb), bf16),
        "O": vm((nb, top, rb, 128), f32),
        "wide": vm((2 * rb, fq), f32),
        "gated": vm((own, fq), bf16),
        "n2": vm((own, width), f32),
        "r2": vm((own, 1), f32),
        "res": vm((own, width), f32),
        "h2": vm((own, width), bf16),
        "h2T": vm((width, own), bf16),
        "gfT": vm((width, own), bf16),
        "gf": vm((own, width), bf16),
        "gh2": vm((own, width), f32),
        "acc": vm((own, width), f32),
        "gatt": vm((own, width), bf16),
        "dOs": vm((nb, top, rb, 128), bf16),
        "glog": vm((own, 128), bf16),
        "AG": vm((own, 2 * ch), bf16),
        "wrp": vm((128, width), bf16),
        "gK": vm((rows, 128), f32),
        "gV": vm((rows, 128), f32),
        "dQ": vm((top, rb, 128), f32),
        "gain_rows": vm((2, width), f32),
        "outx": vm((nb, rb, width // 2), bf16),
        "kvs": vm((nb, 2, rb, 128), bf16),
        "kvr": vm((nb, rb, 128), bf16),
        "F": vm((2, 2) + ring + (shard, 2 * ch), bf16),
        "FC": vm((2, 2, nz, 2, shard, 2 * ch), bf16),
        "FY0": vm((nz, 2, shard, 2 * ch), bf16),
        "FZ0": vm((nz - 1, 2, shard, 2 * ch), bf16),
        "FX0": vm((shard, 2 * ch), bf16),
        "FX1": vm((2, nz, shard, 2 * ch), bf16),
        "FY1": vm((nz, shard, 2 * ch), bf16),
        "FZ1": vm((nz - 1, shard, 2 * ch), bf16),
        "QC": vm((2, nz, 2, shard, half), bf16),
        "QXA": vm((2, nz, shard, half // 2), bf16),
        "QYA": vm((nz, shard, half // 2), bf16),
        "QYB": vm((nz, 2, shard, half // 2), bf16),
        "QXB": vm((nz, shard, half // 2), bf16),
        "QZ": vm((nz - 1, shard, half), bf16),
        "P": vm((2,) + ring + (woc, width), bf16),
        "PC": vm((2, nz, 2, woc, width), bf16),
        "PX": vm((2, nz, woc, width), bf16),
        "PY": vm((nz, woc, width), bf16),
        "PZ": vm((nz - 1, woc, width), bf16),
        "K": vm(ring + (shard, 128), f32),
        "KC": vm((nz, 2, shard, 128), f32),
        "KX": vm((nz, shard, 128), f32),
        "KZ": vm((nz - 1, shard, 128), f32),
        "KY": vm((2, shard, 128), f32),
        "S": vm((4, 32, width), f32),
        "SR": vm((3, 32, width), f32),
        "SZ": vm((nz, 32, width), f32),
        "send": pltpu.SemaphoreType.DMA((128,)),
        "recv": pltpu.SemaphoreType.DMA((128,)),
        "local": pltpu.SemaphoreType.DMA((16,)),
    }


class Refs:
    pass


def kernel(names, outer, *refs):
    r = Refs()
    for name, ref in zip(names, refs):
        setattr(r, name, ref)
    nb = r.tok.shape[0] // 2
    width = r.tok.shape[2]
    top = r.idst.shape[0]
    fq = r.gated.shape[1]
    half = fq // 2
    groups = fq // 128
    r.gq = r.gated
    r.Q = r.W.at[0, :, :, :, :, :, 0:half]
    r.actS = r.AG.at[:, 0 : r.W.shape[6] // 2]
    r.giS = r.AG.at[:, r.W.shape[6] // 2 : r.W.shape[6]]
    nz = r.W.shape[2]
    ch = r.W.shape[6] // 2
    shard = r.W.shape[5]
    d = lax.axis_index("dp")
    y = lax.axis_index("expert")
    n, m = d // outer, d % outer
    z, x, c = n // 4, (n // 2) % 2, n % 2
    length = r.len_ref[0]

    def device(z, x, c, y):
        return ((z * 4 + x * 2 + c) * outer + m, y)

    over_c = device(z, x, 1 - c, y)
    over_x = device(z, 1 - x, c, y)
    over_y = device(z, x, c, 1 - y)
    zs = [(z + k) % nz for k in range(1, nz)]
    over_z = [device(k, x, c, y) for k in zs]
    used = [0]
    sent = []

    def send(source, target, to):
        k = used[0]
        used[0] += 1
        copy = pltpu.make_async_remote_copy(
            src_ref=source, dst_ref=target, send_sem=r.send.at[k], recv_sem=r.recv.at[k],
            device_id=to, device_id_type=MESH,
        )
        copy.start()
        sent.append(copy)
        return copy

    def here(k, source, target):
        copy = pltpu.make_async_copy(source, target, r.local.at[k])
        copy.start()
        return copy

    def got(*copies):
        for copy in copies:
            copy.wait_recv()

    def own(i):
        return 2 * i + y

    def cut(i, size):
        return pl.ds(pl.multiple_of(i * size, size), size)

    def valid_rows(i):
        return (rb * own(i) + lax.broadcasted_iota(jnp.int32, (rb, 1), 0) < length).astype(f32)

    l_w = [
        here(2 * j + k, ref.at[:, j * ch : (j + 1) * ch],
             r.W.at[j, y, z, x, c, :, k * ch : (k + 1) * ch])
        for j in range(2)
        for k, ref in enumerate((r.wh_in, r.wt_in))
    ]
    l_tok = here(7, r.tok_in, r.tok)
    l_q = here(4, r.wq_in, r.WQ.at[y])
    l_o = here(5, r.wo_in, r.WO.at[y])
    l_g = here(6, r.go_in.at[:, y], r.GO.at[y])
    r.wkvg[z, x, c] = jnp.concatenate((r.wk_in[...], r.wv_in[...]), axis=1)
    barrier = pltpu.get_barrier_semaphore()
    peers = [over_c, over_x, over_y] + over_z
    for peer in peers:
        pl.semaphore_signal(barrier, inc=1, device_id=peer, device_id_type=MESH)
    pl.semaphore_wait(barrier, len(peers))
    kv_z = [send(r.wkvg.at[z, x, c], r.wkvg.at[z, x, c], to) for to in over_z]
    l_w[0].wait()
    l_w[1].wait()
    w_y0 = send(r.W.at[0, y, z, x, c], r.W.at[0, y, z, x, c], over_y)
    qrows = cut(c, width // 2)
    q_y = send(r.wq_in.at[qrows, :], r.WQ.at[y, qrows, :], over_y)
    l_w[2].wait()
    l_w[3].wait()
    w_y1 = send(r.W.at[1, y, z, x, c], r.W.at[1, y, z, x, c], over_y)
    orows = cut(c, half // 2)
    o_y = send(r.wo_in.at[orows, :], r.WO.at[y, orows, :], over_y)
    g_y = send(r.go_in.at[:, 1 - y], r.GO.at[y], over_y)
    spare = jnp.zeros((128 - r.wrt.shape[0], width), f32)
    r.wrp[...] = jnp.concatenate((r.wrt[...].astype(f32), spare), axis=0).astype(bf16)

    def w_part(k):
        return r.W.at[k // 2, :, :, :, :, :, pl.ds((k % 2) * ch, ch)]

    def w_over_z(k, both=False):
        view = w_part(k).at[:, z, :, c] if both else w_part(k).at[:, z, x, c]
        return [send(view, view, to) for to in over_z]

    def w_over_x(k, line=True):
        view = w_part(k).at[:, :, x, c] if line else w_part(k).at[:, z, x, c]
        return send(view, view, over_x)

    def w_over_c(k):
        view = w_part(k).at[:, :, :, c]
        return send(view, view, over_c)
    l_tok.wait()

    @pl.loop(0, 2 * nb)
    def _(b):
        normed, _ = norm_rows(r.tok[b].astype(f32))
        r.h1[b] = (normed * r.gain1[...]).astype(bf16)
    got(*kv_z)
    kv_x = send(r.wkvg.at[:, x, c], r.wkvg.at[:, x, c], over_x)
    got(w_y0)
    w0_z = w_over_z(0)
    w1_z = w_over_z(1)

    lane = lanes((rb, 128))
    upper = (lane >= 64).astype(jnp.int32)

    def gates(i):
        h = r.h1[own(i)]
        at = cut(i, rb)
        r.h1T[:, at] = h.astype(f32).T.astype(bf16)
        logits = nt(h, r.wrp[...])
        ids = r.idst[:, cut(own(i), rb)].astype(f32).T.astype(jnp.int32)
        spread = [jnp.broadcast_to(ids[:, k : k + 1], (rb, 128)) for k in range(top)]
        chosen = lane == spread[0]
        for k in range(1, top):
            chosen = chosen | (lane == spread[k])
        most = jnp.max(jnp.where(chosen, logits, lowest), axis=-1, keepdims=True)
        e = jnp.where(chosen, jnp.exp(jnp.where(chosen, logits - most, 0.0)), 0.0)
        g = e / jnp.sum(e, axis=-1, keepdims=True)
        r.dense[at, :] = g
        for k in range(top):
            gk = jnp.sum(jnp.where(lane == spread[k], g, 0.0), axis=-1, keepdims=True)
            r.gateb[i, k] = jnp.broadcast_to(gk, (rb, 128))
            r.idl[i, k] = spread[k] - upper

    pl.loop(0, nb // 2)(gates)
    got(kv_x)
    kv_c = send(r.wkvg.at[:, :, c], r.wkvg.at[:, :, c], over_c)
    pl.loop(nb // 2, nb)(gates)
    got(kv_c)

    @pl.loop(0, 2 * nb)
    def _(b):
        kv = nn(r.h1[b], r.wkvg[...].reshape(width, 128))
        at = cut(b, rb)
        swapped = pltpu.roll(kv, 64, 1)
        k2 = jnp.where(lane < 64, kv, swapped)
        v2 = jnp.where(lane < 64, swapped, kv)
        r.KK[at, :] = k2.astype(bf16)
        r.VV[at, :] = v2.astype(bf16)
        r.KKT[:, at] = k2.T.astype(bf16)
        r.VVT[:, at] = v2.T.astype(bf16)
    got(*w0_z)
    w0_x = w_over_x(0)
    got(q_y)
    q_c = send(r.WQ.at[1 - y, qrows, :], r.WQ.at[1 - y, qrows, :], over_c)
    got(w_y1)
    w3_x = w_over_x(3, False)
    w2_z = w_over_z(2)
    l_q.wait()
    got(q_c)

    def two_blocks(ref, u):
        return jnp.concatenate((ref[own(2 * u)], ref[own(2 * u + 1)]), axis=0)

    @pl.loop(0, nb // 2)
    def _(u):
        h = two_blocks(r.h1, u)
        for e in range(2):
            r.wide[:, e * half : (e + 1) * half] = 0.125 * nn(h, r.WQ[e])
        for s in range(2):
            i = 2 * u + s

            @pl.loop(0, rb // 16, unroll=4)
            def _(t):
                at = cut(t, 16)
                atw = pl.ds(pl.multiple_of(s * rb + t * 16, 16), 16)
                parts = [r.wide[atw, pl.ds(128 * g, 128)] for g in range(groups)]
                for k in range(top):
                    mine = r.idl[i, k, at, :]
                    val = jnp.zeros((16, 128), f32)
                    for g in range(groups):
                        val = jnp.where(mine == 2 * g, parts[g], val)
                    r.Qs[i, k, at, :] = val.astype(bf16)
    diag = lax.broadcasted_iota(jnp.int32, (256, 256), 0) <= rb * y + lanes((256, 256)) % 128

    def attend(i):
        nk = 256 * i
        start = 128 * i * (i + 1)

        @pl.loop(0, top // 2, unroll=4)
        def _(p):
            q = r.Qs[i, pl.ds(2 * p, 2)].reshape(256, 128)
            cols = cut(p, 256)
            s1 = nt(r.KK[nk : nk + 256, :], q)
            s1 = jnp.where(diag, s1, lowest)
            most = jnp.max(s1, axis=0, keepdims=True)
            if nk:
                s0 = nt(r.KK[0:nk, :], q)
                most = jnp.maximum(most, jnp.max(s0, axis=0, keepdims=True))
                p0 = jnp.exp(s0 - most)
            p1 = jnp.exp(s1 - most)
            tot = jnp.sum(p1, axis=0, keepdims=True)
            if nk:
                tot = tot + jnp.sum(p0, axis=0, keepdims=True)
            inv = 1.0 / tot
            p1 = (p1 * inv).astype(bf16)
            r.PT[start + nk : start + nk + 256, cols] = p1
            o = nn(r.VVT[:, nk : nk + 256], p1)
            if nk:
                p0 = (p0 * inv).astype(bf16)
                r.PT[start : start + nk, cols] = p0
                o = o + nn(r.VVT[:, 0:nk], p0)
            r.O[i, pl.ds(2 * p, 2)] = o.T.reshape(2, rb, 128)

    got(w3_x)
    w3_z = w_over_z(3, True)
    got(*w1_z)
    w1_x = w_over_x(1)
    attend(0)
    attend(1)
    got(*w2_z)
    w2_x = w_over_x(2)
    got(w0_x)
    w0_c = w_over_c(0)
    attend(2)
    got(w1_x)
    w1_c = w_over_c(1)
    got(o_y)
    o_c = send(r.WO.at[1 - y, orows, :], r.WO.at[1 - y, orows, :], over_c)
    for i in range(3, nb):
        attend(i)
    l_o.wait()
    l_g.wait()
    got(o_c)
    got(g_y)
    def project(u):
        for s in range(2):
            i = 2 * u + s

            @pl.loop(0, rb // 16, unroll=4)
            def _(t):
                at = cut(t, 16)
                atr = pl.ds(pl.multiple_of(i * rb + t * 16, 16), 16)
                mine = [r.idl[i, k, at, :] for k in range(top)]
                vals = [r.gateb[i, k, at, :] * r.O[i, k, at, :] for k in range(top)]
                for g in range(groups):
                    val = jnp.zeros((16, 128), f32)
                    for k in range(top):
                        val = jnp.where(mine[k] == 2 * g, vals[k], val)
                    r.gated[atr, pl.ds(128 * g, 128)] = val.astype(bf16)

        at = cut(u, 2 * rb)
        valid = valid_pair(u)
        att = nn(r.gated[at, 0:half], r.WO[0]) + nn(r.gated[at, half:fq], r.WO[1])
        row = two_blocks(r.tok, u).astype(f32) + valid * att
        r.res[at, :] = row
        normed, inv = norm_rows(row)
        r.n2[at, :] = normed
        r.r2[at, :] = inv
        h = normed * r.gain2[...]
        r.h2[at, :] = h.astype(bf16)
        r.h2T[:, at] = h.T.astype(bf16)
        for s in range(2):
            side = pl.ds(s * (width // 2), width // 2)
            g = valid * r.GO[s, pl.ds(2 * u, 2)].reshape(2 * rb, width // 2).astype(f32)
            r.gf[at, side] = g.astype(bf16)
            r.gfT[side, at] = g.T.astype(bf16)

    def valid_pair(u):
        return jnp.concatenate((valid_rows(2 * u), valid_rows(2 * u + 1)), axis=0)

    pl.loop(0, nb // 2)(project)

    c0 = 0.7978845608028654
    c1 = 0.044715

    def feed(j, e, first=False):

        w1 = r.W[j, e, :, :, :, :, 0:ch].reshape(width, ch)
        w2 = r.W[j, e, :, :, :, :, ch : 2 * ch].reshape(width, ch)
        for i in range(nb // 2):
            at = pl.ds(i * 256, 256)
            v = nn(r.h2[at, :], w1)
            ga = nn(r.gf[at, :], w2)
            vv = v * v
            hp = 0.5 + 0.5 * jnp.tanh(v * (c0 + (c0 * c1) * vv))
            act = v * hp
            slope = hp + act * (1.0 - hp) * (2 * c0 + (6 * c0 * c1) * vv)
            r.actS[at, :] = act.astype(bf16)
            r.giS[at, :] = (slope * ga).astype(bf16)
        a = nt(r.actS[...], w2)
        b = nt(r.giS[...], w1)
        if first:
            r.acc[...] = a
            r.gh2[...] = b
        else:
            r.acc[...] += a
            r.gh2[...] += b

        shape = (nz, 2, 2, shard, ch)
        r.F[j, e, :, :, :, :, 0:ch] = nn(r.h2T[...], r.giS[...]).astype(bf16).reshape(shape)
        r.F[j, e, :, :, :, :, ch : 2 * ch] = (
            nn(r.gfT[...], r.actS[...]).astype(bf16).reshape(shape)
        )
        return send(r.F.at[j, e, :, :, 1 - c], r.FC.at[j, e], over_c)

    def f_add_c(j, e):
        @pl.loop(0, 2 * nz)
        def _(t):
            a, b = t // 2, t % 2
            r.F[j, e, a, b, c] = r.F[j, e, a, b, c] + r.FC[j, e, a, b]
    got(w0_c, w1_c)
    f0p = feed(0, 1 - y, True)
    got(w2_x)
    w2_c = w_over_c(2)
    f0m = feed(0, y)
    got(f0p)
    f_add_c(0, 1 - y)
    f0_y = send(r.F.at[0, 1 - y, :, :, c], r.FY0, over_y)
    got(*w3_z)
    w3_c = w_over_c(3)
    got(f0m)
    f_add_c(0, y)
    got(w2_c, w3_c)
    f1p = feed(1, 1 - y)
    f1m = feed(1, y)
    got(f1p)
    f_add_c(1, 1 - y)
    f1_xa = send(r.F.at[1, 1 - y, :, 1 - x, c], r.FX1.at[0], over_x)
    r.gain_rows[...] = jnp.zeros_like(r.gain_rows)

    def turn(u):
        at = cut(u, 2 * rb)
        pair = pl.ds(2 * u, 2)
        valid = valid_pair(u)
        outs = (r.res[at, :] + valid * r.acc[at, :]).astype(bf16)
        mine, other = outs[:, : width // 2], outs[:, width // 2 :]
        low = y == 0
        shape = (2, rb, width // 2)
        r.outm[pair] = jnp.where(low, mine, other).reshape(shape)
        r.outx[pair] = jnp.where(low, other, mine).reshape(shape)
        u2, normed = r.gh2[at, :], r.n2[at, :]
        r.gain_rows[1:2, :] += jnp.sum(u2 * normed, axis=0, keepdims=True)
        back = norm_back(u2, normed, r.r2[at, :], r.gain2[...])
        flat = (2 * rb, width // 2)
        go = jnp.concatenate(
            (r.GO[0, pair].reshape(flat), r.GO[1, pair].reshape(flat)), axis=1
        ).astype(f32)
        gr = go + back
        r.res[at, :] = gr
        ga = (valid * gr).astype(bf16)
        r.gatt[at, :] = ga
        for e in range(2):
            r.wide[:, e * half : (e + 1) * half] = nt(ga, r.WO[e])
        for s in range(2):
            i = 2 * u + s

            @pl.loop(0, rb // 16, unroll=4)
            def _(t):
                at = cut(t, 16)
                atr = pl.ds(pl.multiple_of(i * rb + t * 16, 16), 16)
                atw = pl.ds(pl.multiple_of(s * rb + t * 16, 16), 16)
                parts = [r.wide[atw, pl.ds(128 * g, 128)] for g in range(groups)]
                ln = lanes((16, 128))
                hf = (ln >= 64).astype(jnp.int32)
                gd = jnp.zeros((16, 128), f32)
                for k in range(top):
                    mine = r.idl[i, k, at, :]
                    val = jnp.zeros((16, 128), f32)
                    for g in range(groups):
                        val = jnp.where(mine == 2 * g, parts[g], val)
                    dot = jnp.sum(val * r.O[i, k, at, :], axis=-1, keepdims=True)
                    gd = jnp.where(mine + hf == ln, dot, gd)
                    r.dOs[i, k, at, :] = (r.gateb[i, k, at, :] * val).astype(bf16)
                dn = r.dense[atr, :]
                gs = dn * (gd - jnp.sum(dn * gd, axis=-1, keepdims=True))
                r.glog[atr, :] = gs.astype(bf16)

    pl.loop(0, nb // 4)(turn)
    got(f1m)
    f_add_c(1, y)
    f1_xb = send(r.F.at[1, y, :, 1 - x, c], r.FX1.at[1], over_x)
    pl.loop(nb // 4, nb // 2)(turn)
    l_out = here(8, r.outm, r.out.at[:, y])
    routed = jnp.zeros((128, width), f32)
    for i in range(nb):
        routed = routed + tn(r.glog[i * rb : (i + 1) * rb, :], r.h1[own(i)])
    r.S[0] = routed[0:32]
    r.S[0, 31:32, :] = r.gain_rows[1:2, :]
    s_c = send(r.S.at[0], r.SR.at[0], over_c)
    got(f0_y)

    @pl.loop(0, 2 * nz)
    def _(t):
        a, b = t // 2, t % 2
        r.F[0, y, a, b, c] = r.F[0, y, a, b, c] + r.FY0[a, b]

    f0_z = [
        send(r.F.at[0, y, k, :, c], r.FZ0.at[i], to) for i, (k, to) in enumerate(zip(zs, over_z))
    ]

    woc = r.P.shape[4]
    for e in range(2):
        r.P[e] = (
            tn(r.gated[:, e * half : (e + 1) * half], r.gatt[...])
            .astype(bf16)
            .reshape(nz, 2, 2, woc, width)
        )
    p_c = send(r.P.at[:, :, :, 1 - c], r.PC, over_c)

    def back(i):
        nk = 256 * (i + 1)
        start = 128 * i * (i + 1)
        last = i == nb - 1
        v = nn(r.PT[start : start + nk, :], r.dOs[i].reshape(top * rb, 128))
        r.gV[0:nk, :] = v if last else r.gV[0:nk, :] + v

        @pl.loop(0, top // 2, unroll=4)
        def _(p):
            do = r.dOs[i, pl.ds(2 * p, 2)].reshape(256, 128)
            cols = cut(p, 256)
            dp = nt(r.VV[0:nk, :], do)
            pr = r.PT[start : start + nk, cols].astype(f32)
            s = jnp.sum(pr * dp, axis=0, keepdims=True)
            ds = (pr * (dp - s)).astype(bf16)
            r.PT[start : start + nk, cols] = ds
            dq = nn(r.KKT[:, 0:nk], ds)
            r.dQ[pl.ds(2 * p, 2)] = dq.T.reshape(2, rb, 128)

        @pl.loop(0, rb // 16, unroll=4)
        def _(t):
            at = cut(t, 16)
            atr = pl.ds(pl.multiple_of(i * rb + t * 16, 16), 16)
            mine = [r.idl[i, k, at, :] for k in range(top)]
            vals = [r.dQ[k, at, :] for k in range(top)]
            for g in range(groups):
                val = jnp.zeros((16, 128), f32)
                for k in range(top):
                    val = jnp.where(mine[k] == 2 * g, vals[k], val)
                r.gq[atr, pl.ds(128 * g, 128)] = val.astype(bf16) * 0.125

    def key_sums(i):
        v = nn(r.PT[128 * i * (i + 1) : 128 * (i + 1) * (i + 2), :], r.Qs[i].reshape(top * rb, 128))
        at = pl.ds(0, 256 * (i + 1))
        r.gK[at, :] = v if i == nb - 1 else r.gK[at, :] + v
        for s in range(2):
            at = pl.ds((2 * i + s) * rb, rb)
            a, b = r.gK[at, :], r.gV[at, :]
            a = a + pltpu.roll(a, 64, 1)
            b = b + pltpu.roll(b, 64, 1)
            r.kvs[i, s] = jnp.where(lane < 64, a, b).astype(bf16)
        return send(r.kvs.at[i, 1 - y], r.kvr.at[i], over_y)

    def finish(i):
        at = pl.ds(i * rb, rb)
        low = (r.kvs[i, y].astype(f32) + r.kvr[i].astype(f32)).astype(bf16)
        r.kvr[i] = low
        g = nn(r.glog[at, :], r.wrp[...]) + nt(low, r.wkvg[...].reshape(width, 128))
        for e in range(2):
            g = g + nt(r.gq[at, e * half : (e + 1) * half], r.WQ[e])
        normed, inv = norm_rows(r.tok[own(i)].astype(f32))
        r.gain_rows[0:1, :] += jnp.sum(g * normed, axis=0, keepdims=True)
        back = norm_back(g, normed, inv, r.gain1[...])
        r.gts[i] = (r.res[at, :] + back).astype(bf16)
        return here(9 + i, r.gts.at[i], r.gt.at[i, y])

    def give(i):
        return send(r.gts.at[i], r.gt.at[i, y], over_y)

    keys, ends = {}, []
    for i in range(nb - 1, 2, -1):
        back(i)
        keys[i] = key_sums(i)
    got(s_c)
    r.S[1] = r.S[0] + r.SR[0]
    s_x = send(r.S.at[1], r.SR.at[1], over_x)
    got(p_c)

    @pl.loop(0, 4 * nz)
    def _(t):
        e, a, b = t // (2 * nz), (t // 2) % nz, t % 2
        r.P[e, a, b, c] = r.P[e, a, b, c] + r.PC[e, a, b]

    p_x = send(r.P.at[:, :, 1 - x, c], r.PX, over_x)
    got(f1_xa, f1_xb)

    @pl.loop(0, nz)
    def _(a):
        r.F[1, 1 - y, a, x, c] = r.F[1, 1 - y, a, x, c] + r.FX1[0, a]
        r.F[1, y, a, x, c] = r.F[1, y, a, x, c] + r.FX1[1, a]

    f1_y = send(r.F.at[1, 1 - y, :, x, c], r.FY1, over_y)
    back(2)
    keys[2] = key_sums(2)
    for i in range(nb - 1, 2, -1):
        got(keys[i])
        ends.append(finish(i))
    gts_y = [give(i) for i in range(nb - 1, 2, -1)]
    got(s_x)
    r.S[2] = r.S[1] + r.SR[1]
    s_y = send(r.S.at[2], r.SR.at[2], over_y)
    got(*f0_z)
    for b in range(2):
        v = r.F[0, y, z, b, c].astype(f32)
        for k in range(nz - 1):
            v = v + r.FZ0[k, b].astype(f32)
        r.F[0, y, z, b, c] = v.astype(bf16)
    f0_x = send(r.F.at[0, y, z, 1 - x, c], r.FX0, over_x)
    back(1)
    keys[1] = key_sums(1)
    got(p_x)

    @pl.loop(0, 2 * nz)
    def _(t):
        e, a = t // nz, t % nz
        r.P[e, a, x, c] = r.P[e, a, x, c] + r.PX[e, a]

    p_y = send(r.P.at[1 - y, :, x, c], r.PY, over_y)
    got(f1_y)

    @pl.loop(0, nz)
    def _(a):
        r.F[1, y, a, x, c] = r.F[1, y, a, x, c] + r.FY1[a]

    f1_z = [
        send(r.F.at[1, y, k, x, c], r.FZ1.at[i], to) for i, (k, to) in enumerate(zip(zs, over_z))
    ]
    got(keys[2])
    ends.append(finish(2))
    back(0)
    for copy in [w_y0, w_y1, w3_x, w0_x, w1_x, w2_x, w0_c, w1_c, w2_c, w3_c,
                 *w0_z, *w1_z, *w2_z, *w3_z]:
        copy.wait_send()
        sent[:] = [other for other in sent if other is not copy]
    one, two = pl.ds(0, half // 2), pl.ds(half // 2, half // 2)
    q_c2 = []
    for part in range(2):
        side = pl.ds(part * (half // 2), half // 2)
        for e in range(2):
            at = pl.ds(e * half + part * (half // 2), half // 2)
            r.Q[e, :, :, :, :, side] = (
                nn(r.h1T[...], r.gq[:, at]).astype(bf16).reshape(nz, 2, 2, shard, half // 2)
            )
        q_c2.append(
            send(r.Q.at[:, :, :, 1 - c, :, side], r.QC.at[:, :, :, :, side], over_c)
        )
    keys[0] = key_sums(0)
    got(s_y)
    r.S[3] = r.S[2] + r.SR[2]
    r.SZ[z] = r.S[3]
    s_z = [send(r.S.at[3], r.SZ.at[z], to) for to in over_z]
    for part, side in enumerate((one, two)):
        got(q_c2[part])

        @pl.loop(0, 4 * nz)
        def _(t):
            e, a, b = t // (2 * nz), (t // 2) % nz, t % 2
            r.Q[e, a, b, c, :, side] = r.Q[e, a, b, c, :, side] + r.QC[e, a, b, :, side]

        if part == 0:
            qa_x = send(r.Q.at[:, :, 1 - x, c, :, one], r.QXA, over_x)
    qb_y = send(r.Q.at[1 - y, :, :, c, :, two], r.QYB, over_y)
    gts_y.append(give(2))
    got(keys[1])
    ends.append(finish(1))
    got(p_y)

    @pl.loop(0, nz)
    def _(a):
        r.P[y, a, x, c] = r.P[y, a, x, c] + r.PY[a]

    p_z = [send(r.P.at[y, k, x, c], r.PZ.at[i], to) for i, (k, to) in enumerate(zip(zs, over_z))]
    got(f0_x)
    v = r.F[0, y, z, x, c].astype(f32) + r.FX0[...].astype(f32)
    r.gwh[:, 0:ch] = v[:, 0:ch]
    r.gwT[:, 0:ch] = v[:, ch : 2 * ch]
    got(keys[0])
    ends.append(finish(0))
    r.K[...] = nn(r.h1T[...], r.kvr[...].reshape(nb * rb, 128)).reshape(nz, 2, 2, shard, 128)
    k_c = send(r.K.at[:, :, 1 - c], r.KC, over_c)
    r.G[0] = r.gain_rows[0:1, :]
    g1_c = send(r.G.at[0], r.GR.at[0], over_c)
    got(qa_x)

    @pl.loop(0, 2 * nz)
    def _(t):
        e, a = t // nz, t % nz
        r.Q[e, a, x, c, :, one] = r.Q[e, a, x, c, :, one] + r.QXA[e, a]

    qa_y = send(r.Q.at[1 - y, :, x, c, :, one], r.QYA, over_y)
    got(qb_y)

    @pl.loop(0, 2 * nz)
    def _(t):
        a, b = t // 2, t % 2
        r.Q[y, a, b, c, :, two] = r.Q[y, a, b, c, :, two] + r.QYB[a, b]

    qb_x = send(r.Q.at[y, :, 1 - x, c, :, two], r.QXB, over_x)
    gts_y.append(give(1))
    gts_y.append(give(0))
    got(k_c)

    @pl.loop(0, 2 * nz)
    def _(t):
        a, b = t // 2, t % 2
        r.K[a, b, c] = r.K[a, b, c] + r.KC[a, b]

    k_x = send(r.K.at[:, 1 - x, c], r.KX, over_x)
    got(g1_c)
    r.G[1] = r.G[0] + r.GR[0]
    g1_x = send(r.G.at[1], r.GR.at[1], over_x)
    got(*p_z)
    v = r.P[y, z, x, c].astype(f32)
    for k in range(nz - 1):
        v = v + r.PZ[k].astype(f32)
    r.PA[z, x, c] = v.astype(bf16)
    pa_z = [send(r.PA.at[z, x, c], r.PA.at[z, x, c], to) for to in over_z]

    got(qa_y, qb_x)

    @pl.loop(0, nz)
    def _(a):
        r.Q[y, a, x, c, :, one] = r.Q[y, a, x, c, :, one] + r.QYA[a]
        r.Q[y, a, x, c, :, two] = r.Q[y, a, x, c, :, two] + r.QXB[a]

    q_z = [send(r.Q.at[y, k, x, c], r.QZ.at[i], to) for i, (k, to) in enumerate(zip(zs, over_z))]
    got(k_x)

    @pl.loop(0, nz)
    def _(a):
        r.K[a, x, c] = r.K[a, x, c] + r.KX[a]

    k_z = [send(r.K.at[k, x, c], r.KZ.at[i], to) for i, (k, to) in enumerate(zip(zs, over_z))]
    got(g1_x)
    r.G[2] = r.G[1] + r.GR[1]
    g1_y = send(r.G.at[2], r.GR.at[2], over_y)
    got(*f1_z)
    v = r.F[1, y, z, x, c].astype(f32)
    for k in range(nz - 1):
        v = v + r.FZ1[k].astype(f32)
    r.gwh[:, ch : 2 * ch] = v[:, 0:ch]
    r.gwT[:, ch : 2 * ch] = v[:, ch : 2 * ch]
    got(*s_z)
    v = r.SZ[0]
    for k in range(1, nz):
        v = v + r.SZ[k]
    r.small[...] = v
    got(*pa_z)
    pa_x = send(r.PA.at[:, x, c], r.PA.at[:, x, c], over_x)
    got(*k_z)
    v = r.K[z, x, c]
    for k in range(nz - 1):
        v = v + r.KZ[k]
    r.KY[0] = v
    k_y = send(r.KY.at[0], r.KY.at[1], over_y)
    out_y = send(r.outx, r.out.at[:, y], over_y)
    got(*q_z)
    v = r.Q[y, z, x, c].astype(f32)
    for k in range(nz - 1):
        v = v + r.QZ[k].astype(f32)
    r.QA[z, x, c] = v.astype(bf16)
    view = r.QA.at[z, x, c, :, two]
    gb_x = send(view, view, over_x)
    view = r.QA.at[z, x, c, :, one]
    ga_z = [send(view, view, to) for to in over_z]
    got(g1_y)
    r.G[3] = r.G[2] + r.GR[2]
    r.GZ[z] = r.G[3]
    g1_z = [send(r.G.at[3], r.GZ.at[z], to) for to in over_z]
    got(gb_x)
    view = r.QA.at[z, :, c, :, two]
    gb_z = [send(view, view, to) for to in over_z]
    got(pa_x)
    pa_c = send(r.PA.at[:, :, c], r.PA.at[:, :, c], over_c)
    got(k_y)
    r.gkv[...] = r.KY[0] + r.KY[1]
    got(*ga_z)
    view = r.QA.at[:, x, c, :, one]
    ga_x = send(view, view, over_x)
    got(*g1_z)
    v = r.GZ[0]
    for k in range(1, nz):
        v = v + r.GZ[k]
    r.gain1_out[...] = v
    got(*gb_z)
    view = r.QA.at[:, :, c, :, two]
    gb_c = send(view, view, over_c)
    got(ga_x)
    view = r.QA.at[:, :, c, :, one]
    ga_c = send(view, view, over_c)
    got(pa_c, gb_c, ga_c)
    l_out.wait()
    for copy in ends:
        copy.wait()
    got(out_y, *gts_y)
    for copy in sent:
        copy.wait_send()


def close(out, gt, QA, PA, gwh, gwT, gkv, small, gain1,
          o_out, o_gt, o_wq, o_wo, o_wh, o_wT, o_k, o_v, o_wr, o_g1, o_g2,
          b_q, b_o, b_k, b_s, sem):
    pairs = ((QA, b_q), (PA, b_o), (gkv, b_k), (small, b_s),
             (gt, o_gt), (out, o_out), (gwh, o_wh), (gwT, o_wT), (gain1, o_g1))
    copies = [pltpu.make_async_copy(a, b, sem.at[k]) for k, (a, b) in enumerate(pairs)]
    for copy in copies:
        copy.start()
    copies[0].wait()
    o_wq[...] = b_q[...].astype(f32)
    copies[1].wait()
    o_wo[...] = b_o[...].astype(f32)
    copies[2].wait()
    o_k[...] = b_k[:, 0:64]
    o_v[...] = b_k[:, 64:128]
    copies[3].wait()
    o_wr[...] = b_s[0 : o_wr.shape[0], :]
    o_g2[...] = b_s[31:32, :]
    for copy in copies[4:]:
        copy.wait()


def shards(
    tokens, gain_attn, w_key, w_value, w_router, w_query, w_out, gain_ffn,
    w_hidden, w_output, expert_ids, lengths, grad_out,
):
    rows, width = tokens.shape
    dp = lax.axis_size("dp")
    inner = min(dp, 16)
    outer = dp // inner
    nz = inner // 4
    nb = rows // rb // 2
    top = expert_ids.shape[1]
    n_experts = w_router.shape[1]
    half = w_query.shape[1]
    ffh = w_hidden.shape[1]
    near = [[g * outer + k for k in range(outer)] for g in range(inner)]
    wt = w_output.T
    if outer > 1:
        w_key, w_value, w_hidden, wt = (
            lax.all_gather(v, "dp", axis=0, tiled=True, axis_index_groups=near)
            for v in (w_key, w_value, w_hidden, wt)
        )
    shard = width // inner
    woc = half // inner
    sds = jax.ShapeDtypeStruct
    spec = scratch(rows, width, nb, top, 2 * half, 2 * ffh, nz, shard)
    names = in_names + out_names + list(spec)
    vmem = pl.BlockSpec(memory_space=pltpu.VMEM)
    anyw = pl.BlockSpec(memory_space=pl.ANY)
    out, gt, QA, PA, gwh, gwT, gkv, small, gain1 = pl.pallas_call(
        functools.partial(kernel, names, outer),
        out_shape=(
            sds((nb, 2, rb, width // 2), bf16),
            sds((nb, 2, rb, width), bf16),
            sds((nz, 2, 2, shard, half), bf16),
            sds((nz, 2, 2, woc, width), bf16),
            sds((shard, ffh), f32),
            sds((shard, ffh), f32),
            sds((shard, 128), f32),
            sds((32, width), f32),
            sds((1, width), f32),
        ),
        in_specs=[pl.BlockSpec(memory_space=pltpu.SMEM)] + [anyw] + [vmem] * 6 + [anyw] * 5,
        out_specs=[anyw] * 2 + [vmem] * 7,
        scratch_shapes=list(spec.values()),
        compiler_params=pltpu.CompilerParams(
            collective_id=0, has_side_effects=True, vmem_limit_bytes=63 * 2**20
        ),
    )(
        lengths, tokens.reshape(2 * nb, rb, width), gain_attn[None], w_router.T, gain_ffn[None],
        expert_ids.T, w_key, w_value, w_query, w_out, w_hidden, wt,
        grad_out.reshape(nb, 2, rb, width // 2),
    )
    out, gt, gwq, gwo, gwh, gwT, gk, gv, gwr, g1, g2 = pl.pallas_call(
        close,
        out_shape=(
            sds(out.shape, bf16),
            sds(gt.shape, bf16),
            sds((width, half), f32),
            sds((half, width), f32),
            sds((shard, ffh), f32),
            sds((shard, ffh), f32),
            sds((shard, 64), f32),
            sds((shard, 64), f32),
            sds((n_experts, width), f32),
            sds((1, width), f32),
            sds((1, width), f32),
        ),
        in_specs=[anyw] * 9,
        out_specs=[vmem] * 11,
        scratch_shapes=[
            pltpu.VMEM((width, half), bf16),
            pltpu.VMEM((half, width), bf16),
            pltpu.VMEM((shard, 128), f32),
            pltpu.VMEM((32, width), f32),
            pltpu.SemaphoreType.DMA((9,)),
        ],
        compiler_params=pltpu.CompilerParams(vmem_limit_bytes=63 * 2**20),
    )(out, gt, QA.reshape(width, half), PA.reshape(half, width), gwh, gwT, gkv, small, gain1)
    if outer > 1:
        gwq, gwo, gwr, g1, g2 = lax.psum(
            (gwq, gwo, gwr, g1, g2), "dp", axis_index_groups=near
        )
        gwh, gwT, gk, gv = (
            lax.psum_scatter(v, "dp", scatter_dimension=0, tiled=True, axis_index_groups=near)
            for v in (gwh, gwT, gk, gv)
        )
    return (
        out.reshape(rows, width // 2), gt.reshape(rows, width), gk, gv, gwr.T, gwq, gwo,
        gwh, gwT.T, g1[0], g2[0],
    )


def solution(mesh):
    placed = (
        P("dp", None), P(), P("dp", None), P("dp", None), P(), P(None, "expert"),
        P("expert", None), P(), P("dp", "expert"), P("expert", "dp"), P("dp", None),
        P("dp"), P("dp", "expert"),
    )
    return jax.shard_map(
        shards,
        mesh=mesh,
        in_specs=placed,
        out_specs=(
            P("dp", "expert"), P("dp", None), P("dp", None), P("dp", None), P(),
            P(None, "expert"), P("expert", None), P("dp", "expert"), P("expert", "dp"),
            P(), P(),
        ),
        check_vma=False,
    )
```

```python
import functools

import jax
import jax.numpy as jnp
from jax import lax
from jax.experimental import pallas as pl
from jax.experimental.pallas import tpu as pltpu
from jax.sharding import PartitionSpec as P

f32 = jnp.float32
bf16 = jnp.bfloat16
eps = 1e-05
lowest = -1e30
rb = 128


def nn(left, right):
    return jnp.dot(left, right, preferred_element_type=f32)


def nt(left, right):
    return lax.dot_general(left, right, (((1,), (1,)), ((), ())), preferred_element_type=f32)


def tn(left, right):
    return lax.dot_general(left, right, (((0,), (0,)), ((), ())), preferred_element_type=f32)


def norm_rows(x):
    centred = x - jnp.mean(x, axis=-1, keepdims=True)
    inv = lax.rsqrt(jnp.mean(centred * centred, axis=-1, keepdims=True) + eps)
    return centred * inv, inv


def norm_back(u, normed, inv, gain):
    w = u * gain
    return inv * (
        w
        - jnp.mean(w, axis=-1, keepdims=True)
        - normed * jnp.mean(w * normed, axis=-1, keepdims=True)
    )


def lanes(shape):
    return lax.broadcasted_iota(jnp.int32, shape, len(shape) - 1)


MESH = pl.DeviceIdType.MESH

in_names = [
    "len_ref",
    "tok_in",
    "gain1",
    "wrt",
    "gain2",
    "idst",
    "wk_in",
    "wv_in",
    "wq_in",
    "wo_in",
    "wh_in",
    "wt_in",
    "go_in",
]
out_names = [
    "out",
    "gt",
    "QA",
    "PA",
    "gwh",
    "gwT",
    "gkv",
    "small",
    "gain1_out",
]


def scratch(rows, width, nb, top, fq, ff, nz, shard):
    vm = pltpu.VMEM
    own = rows // 2
    half = fq // 2
    total = 128 * nb * (nb + 1)
    ring = (nz, 2, 2)
    ch = ff // 4
    woc = half // (4 * nz)
    return {
        "tok": vm((2 * nb, rb, width), bf16),
        "outm": vm((nb, rb, width // 2), bf16),
        "gts": vm((nb, rb, width), bf16),
        "G": vm((4, 1, width), f32),
        "GR": vm((3, 1, width), f32),
        "GZ": vm((nz, 1, width), f32),
        "wkvg": vm(ring + (shard, 128), bf16),
        "W": vm((2, 2) + ring + (shard, 2 * ch), bf16),
        "WQ": vm((2, width, half), bf16),
        "WO": vm((2, half, width), bf16),
        "GO": vm((2, nb, rb, width // 2), bf16),
        "h1": vm((2 * nb, rb, width), bf16),
        "h1T": vm((width, own), bf16),
        "KK": vm((rows, 128), bf16),
        "VV": vm((rows, 128), bf16),
        "KKT": vm((128, rows), bf16),
        "VVT": vm((128, rows), bf16),
        "idl": vm((nb, top, rb, 128), jnp.int32),
        "gateb": vm((nb, top, rb, 128), f32),
        "dense": vm((own, 128), f32),
        "Qs": vm((nb, top, rb, 128), bf16),
        "PT": vm((total, top * rb), bf16),
        "O": vm((nb, top, rb, 128), f32),
        "wide": vm((2 * rb, fq), f32),
        "gated": vm((own, fq), bf16),
        "n2": vm((own, width), f32),
        "r2": vm((own, 1), f32),
        "res": vm((own, width), f32),
        "h2": vm((own, width), bf16),
        "h2T": vm((width, own), bf16),
        "gfT": vm((width, own), bf16),
        "gf": vm((own, width), bf16),
        "gh2": vm((own, width), f32),
        "acc": vm((own, width), f32),
        "gatt": vm((own, width), bf16),
        "dOs": vm((nb, top, rb, 128), bf16),
        "glog": vm((own, 128), bf16),
        "AG": vm((own, 2 * ch), bf16),
        "wrp": vm((128, width), bf16),
        "gK": vm((rows, 128), f32),
        "gV": vm((rows, 128), f32),
        "dQ": vm((top, rb, 128), f32),
        "gain_rows": vm((2, width), f32),
        "outx": vm((nb, rb, width // 2), bf16),
        "kvs": vm((nb, 2, rb, 128), bf16),
        "kvr": vm((nb, rb, 128), bf16),
        "F": vm((2, 2) + ring + (shard, 2 * ch), bf16),
        "FC": vm((2, 2, nz, 2, shard, 2 * ch), bf16),
        "FY0": vm((nz, 2, shard, 2 * ch), bf16),
        "FZ0": vm((nz - 1, 2, shard, 2 * ch), bf16),
        "FX0": vm((shard, 2 * ch), bf16),
        "FX1": vm((2, nz, shard, 2 * ch), bf16),
        "FY1": vm((nz, shard, 2 * ch), bf16),
        "FZ1": vm((nz - 1, shard, 2 * ch), bf16),
        "QC": vm((2, nz, 2, shard, half), bf16),
        "QXA": vm((2, nz, shard, half // 2), bf16),
        "QYA": vm((nz, shard, half // 2), bf16),
        "QYB": vm((nz, 2, shard, half // 2), bf16),
        "QXB": vm((nz, shard, half // 2), bf16),
        "QZ": vm((nz - 1, shard, half), bf16),
        "P": vm((2,) + ring + (woc, width), bf16),
        "PC": vm((2, nz, 2, woc, width), bf16),
        "PX": vm((2, nz, woc, width), bf16),
        "PY": vm((nz, woc, width), bf16),
        "PZ": vm((nz - 1, woc, width), bf16),
        "K": vm(ring + (shard, 128), f32),
        "KC": vm((nz, 2, shard, 128), f32),
        "KX": vm((nz, shard, 128), f32),
        "KZ": vm((nz - 1, shard, 128), f32),
        "KY": vm((2, shard, 128), f32),
        "S": vm((4, 32, width), bf16),
        "SR": vm((3, 32, width), bf16),
        "SZ": vm((nz, 32, width), bf16),
        "send": pltpu.SemaphoreType.DMA((128,)),
        "recv": pltpu.SemaphoreType.DMA((128,)),
        "local": pltpu.SemaphoreType.DMA((16,)),
    }


class Refs:
    pass


def kernel(names, outer, *refs):
    r = Refs()
    for name, ref in zip(names, refs):
        setattr(r, name, ref)
    nb = r.tok.shape[0] // 2
    width = r.tok.shape[2]
    top = r.idst.shape[0]
    fq = r.gated.shape[1]
    half = fq // 2
    groups = fq // 128
    r.gq = r.gated
    r.Q = r.W.at[0, :, :, :, :, :, 0:half]
    r.actS = r.AG.at[:, 0 : r.W.shape[6] // 2]
    r.giS = r.AG.at[:, r.W.shape[6] // 2 : r.W.shape[6]]
    nz = r.W.shape[2]
    ch = r.W.shape[6] // 2
    shard = r.W.shape[5]
    d = lax.axis_index("dp")
    y = lax.axis_index("expert")
    n, m = d // outer, d % outer
    z, x, c = n // 4, (n // 2) % 2, n % 2
    length = r.len_ref[0]

    def device(z, x, c, y):
        return ((z * 4 + x * 2 + c) * outer + m, y)

    over_c = device(z, x, 1 - c, y)
    over_x = device(z, 1 - x, c, y)
    over_y = device(z, x, c, 1 - y)
    zs = [(z + k) % nz for k in range(1, nz)]
    over_z = [device(k, x, c, y) for k in zs]
    used = [0]
    sent = []

    def send(source, target, to):
        k = used[0]
        used[0] += 1
        copy = pltpu.make_async_remote_copy(
            src_ref=source, dst_ref=target, send_sem=r.send.at[k], recv_sem=r.recv.at[k],
            device_id=to, device_id_type=MESH,
        )
        copy.start()
        sent.append(copy)
        return copy

    def here(k, source, target):
        copy = pltpu.make_async_copy(source, target, r.local.at[k])
        copy.start()
        return copy

    def got(*copies):
        for copy in copies:
            copy.wait_recv()

    def own(i):
        return 2 * i + y

    def cut(i, size):
        return pl.ds(pl.multiple_of(i * size, size), size)

    def valid_rows(i):
        return (rb * own(i) + lax.broadcasted_iota(jnp.int32, (rb, 1), 0) < length).astype(f32)

    l_w = [
        here(2 * j + k, ref.at[:, j * ch : (j + 1) * ch],
             r.W.at[j, y, z, x, c, :, k * ch : (k + 1) * ch])
        for j in range(2)
        for k, ref in enumerate((r.wh_in, r.wt_in))
    ]
    l_tok = here(7, r.tok_in, r.tok)
    l_q = here(4, r.wq_in, r.WQ.at[y])
    l_o = here(5, r.wo_in, r.WO.at[y])
    l_g = here(6, r.go_in.at[:, y], r.GO.at[y])
    r.wkvg[z, x, c] = jnp.concatenate((r.wk_in[...], r.wv_in[...]), axis=1)
    barrier = pltpu.get_barrier_semaphore()
    peers = [over_c, over_x, over_y] + over_z
    for peer in peers:
        pl.semaphore_signal(barrier, inc=1, device_id=peer, device_id_type=MESH)
    pl.semaphore_wait(barrier, len(peers))
    kv_z = [send(r.wkvg.at[z, x, c], r.wkvg.at[z, x, c], to) for to in over_z]
    l_w[0].wait()
    l_w[1].wait()
    w_y0 = send(r.W.at[0, y, z, x, c], r.W.at[0, y, z, x, c], over_y)
    qrows = cut(c, width // 2)
    q_y = send(r.wq_in.at[qrows, :], r.WQ.at[y, qrows, :], over_y)
    l_w[2].wait()
    l_w[3].wait()
    w_y1 = send(r.W.at[1, y, z, x, c], r.W.at[1, y, z, x, c], over_y)
    orows = cut(c, half // 2)
    o_y = send(r.wo_in.at[orows, :], r.WO.at[y, orows, :], over_y)
    g_y = send(r.go_in.at[:, 1 - y], r.GO.at[y], over_y)
    spare = jnp.zeros((128 - r.wrt.shape[0], width), f32)
    r.wrp[...] = jnp.concatenate((r.wrt[...].astype(f32), spare), axis=0).astype(bf16)

    def w_part(k):
        return r.W.at[k // 2, :, :, :, :, :, pl.ds((k % 2) * ch, ch)]

    def w_over_z(k, both=False):
        view = w_part(k).at[:, z, :, c] if both else w_part(k).at[:, z, x, c]
        return [send(view, view, to) for to in over_z]

    def w_over_x(k, line=True):
        view = w_part(k).at[:, :, x, c] if line else w_part(k).at[:, z, x, c]
        return send(view, view, over_x)

    def w_over_c(k):
        view = w_part(k).at[:, :, :, c]
        return send(view, view, over_c)
    l_tok.wait()

    @pl.loop(0, 2 * nb)
    def _(b):
        normed, _ = norm_rows(r.tok[b].astype(f32))
        r.h1[b] = (normed * r.gain1[...]).astype(bf16)
    got(*kv_z)
    kv_x = send(r.wkvg.at[:, x, c], r.wkvg.at[:, x, c], over_x)
    got(w_y0)
    w0_z = w_over_z(0)
    w1_z = w_over_z(1)

    lane = lanes((rb, 128))
    upper = (lane >= 64).astype(jnp.int32)

    def gates(i):
        h = r.h1[own(i)]
        at = cut(i, rb)
        r.h1T[:, at] = h.astype(f32).T.astype(bf16)
        logits = nt(h, r.wrp[...])
        ids = r.idst[:, cut(own(i), rb)].astype(f32).T.astype(jnp.int32)
        spread = [jnp.broadcast_to(ids[:, k : k + 1], (rb, 128)) for k in range(top)]
        chosen = lane == spread[0]
        for k in range(1, top):
            chosen = chosen | (lane == spread[k])
        most = jnp.max(jnp.where(chosen, logits, lowest), axis=-1, keepdims=True)
        e = jnp.where(chosen, jnp.exp(jnp.where(chosen, logits - most, 0.0)), 0.0)
        g = e / jnp.sum(e, axis=-1, keepdims=True)
        r.dense[at, :] = g
        for k in range(top):
            gk = jnp.sum(jnp.where(lane == spread[k], g, 0.0), axis=-1, keepdims=True)
            r.gateb[i, k] = jnp.broadcast_to(gk, (rb, 128))
            r.idl[i, k] = spread[k] - upper

    pl.loop(0, nb // 2)(gates)
    got(kv_x)
    kv_c = send(r.wkvg.at[:, :, c], r.wkvg.at[:, :, c], over_c)
    pl.loop(nb // 2, nb)(gates)
    got(kv_c)

    @pl.loop(0, 2 * nb)
    def _(b):
        kv = nn(r.h1[b], r.wkvg[...].reshape(width, 128))
        at = cut(b, rb)
        swapped = pltpu.roll(kv, 64, 1)
        k2 = jnp.where(lane < 64, kv, swapped)
        v2 = jnp.where(lane < 64, swapped, kv)
        r.KK[at, :] = k2.astype(bf16)
        r.VV[at, :] = v2.astype(bf16)
        r.KKT[:, at] = k2.T.astype(bf16)
        r.VVT[:, at] = v2.T.astype(bf16)
    got(*w0_z)
    w0_x = w_over_x(0)
    got(q_y)
    q_c = send(r.WQ.at[1 - y, qrows, :], r.WQ.at[1 - y, qrows, :], over_c)
    got(w_y1)
    w3_x = w_over_x(3, False)
    w2_z = w_over_z(2)
    l_q.wait()
    got(q_c)

    def two_blocks(ref, u):
        return jnp.concatenate((ref[own(2 * u)], ref[own(2 * u + 1)]), axis=0)

    @pl.loop(0, nb // 2)
    def _(u):
        h = two_blocks(r.h1, u)
        for e in range(2):
            r.wide[:, e * half : (e + 1) * half] = 0.125 * nn(h, r.WQ[e])
        for s in range(2):
            i = 2 * u + s

            @pl.loop(0, rb // 16, unroll=4)
            def _(t):
                at = cut(t, 16)
                atw = pl.ds(pl.multiple_of(s * rb + t * 16, 16), 16)
                parts = [r.wide[atw, pl.ds(128 * g, 128)] for g in range(groups)]
                for k in range(top):
                    mine = r.idl[i, k, at, :]
                    val = jnp.zeros((16, 128), f32)
                    for g in range(groups):
                        val = jnp.where(mine == 2 * g, parts[g], val)
                    r.Qs[i, k, at, :] = val.astype(bf16)
    diag = lax.broadcasted_iota(jnp.int32, (256, 256), 0) <= rb * y + lanes((256, 256)) % 128

    def attend(i):
        nk = 256 * i
        start = 128 * i * (i + 1)

        @pl.loop(0, top // 2, unroll=4)
        def _(p):
            q = r.Qs[i, pl.ds(2 * p, 2)].reshape(256, 128)
            cols = cut(p, 256)
            s1 = nt(r.KK[nk : nk + 256, :], q)
            s1 = jnp.where(diag, s1, lowest)
            most = jnp.max(s1, axis=0, keepdims=True)
            if nk:
                s0 = nt(r.KK[0:nk, :], q)
                most = jnp.maximum(most, jnp.max(s0, axis=0, keepdims=True))
                p0 = jnp.exp(s0 - most)
            p1 = jnp.exp(s1 - most)
            tot = jnp.sum(p1, axis=0, keepdims=True)
            if nk:
                tot = tot + jnp.sum(p0, axis=0, keepdims=True)
            inv = 1.0 / tot
            p1 = (p1 * inv).astype(bf16)
            r.PT[start + nk : start + nk + 256, cols] = p1
            o = nn(r.VVT[:, nk : nk + 256], p1)
            if nk:
                p0 = (p0 * inv).astype(bf16)
                r.PT[start : start + nk, cols] = p0
                o = o + nn(r.VVT[:, 0:nk], p0)
            r.O[i, pl.ds(2 * p, 2)] = o.T.reshape(2, rb, 128)

    got(w3_x)
    w3_z = w_over_z(3, True)
    got(*w1_z)
    w1_x = w_over_x(1)
    attend(0)
    attend(1)
    got(*w2_z)
    w2_x = w_over_x(2)
    got(w0_x)
    w0_c = w_over_c(0)
    attend(2)
    got(w1_x)
    w1_c = w_over_c(1)
    got(o_y)
    o_c = send(r.WO.at[1 - y, orows, :], r.WO.at[1 - y, orows, :], over_c)
    for i in range(3, nb):
        attend(i)
    l_o.wait()
    l_g.wait()
    got(o_c)
    got(g_y)
    def project(u):
        for s in range(2):
            i = 2 * u + s

            @pl.loop(0, rb // 16, unroll=4)
            def _(t):
                at = cut(t, 16)
                atr = pl.ds(pl.multiple_of(i * rb + t * 16, 16), 16)
                mine = [r.idl[i, k, at, :] for k in range(top)]
                vals = [r.gateb[i, k, at, :] * r.O[i, k, at, :] for k in range(top)]
                for g in range(groups):
                    val = jnp.zeros((16, 128), f32)
                    for k in range(top):
                        val = jnp.where(mine[k] == 2 * g, vals[k], val)
                    r.gated[atr, pl.ds(128 * g, 128)] = val.astype(bf16)

        at = cut(u, 2 * rb)
        valid = valid_pair(u)
        att = nn(r.gated[at, 0:half], r.WO[0]) + nn(r.gated[at, half:fq], r.WO[1])
        row = two_blocks(r.tok, u).astype(f32) + valid * att
        r.res[at, :] = row
        normed, inv = norm_rows(row)
        r.n2[at, :] = normed
        r.r2[at, :] = inv
        h = normed * r.gain2[...]
        r.h2[at, :] = h.astype(bf16)
        r.h2T[:, at] = h.T.astype(bf16)
        for s in range(2):
            side = pl.ds(s * (width // 2), width // 2)
            g = valid * r.GO[s, pl.ds(2 * u, 2)].reshape(2 * rb, width // 2).astype(f32)
            r.gf[at, side] = g.astype(bf16)
            r.gfT[side, at] = g.T.astype(bf16)

    def valid_pair(u):
        return jnp.concatenate((valid_rows(2 * u), valid_rows(2 * u + 1)), axis=0)

    pl.loop(0, nb // 2)(project)

    c0 = 0.7978845608028654
    c1 = 0.044715

    def feed(j, e, first=False):

        w1 = r.W[j, e, :, :, :, :, 0:ch].reshape(width, ch)
        w2 = r.W[j, e, :, :, :, :, ch : 2 * ch].reshape(width, ch)
        for i in range(nb // 2):
            at = pl.ds(i * 256, 256)
            v = nn(r.h2[at, :], w1)
            ga = nn(r.gf[at, :], w2)
            vv = v * v
            hp = 0.5 + 0.5 * jnp.tanh(v * (c0 + (c0 * c1) * vv))
            act = v * hp
            slope = hp + act * (1.0 - hp) * (2 * c0 + (6 * c0 * c1) * vv)
            r.actS[at, :] = act.astype(bf16)
            r.giS[at, :] = (slope * ga).astype(bf16)
        a = nt(r.actS[...], w2)
        b = nt(r.giS[...], w1)
        if first:
            r.acc[...] = a
            r.gh2[...] = b
        else:
            r.acc[...] += a
            r.gh2[...] += b

        shape = (nz, 2, 2, shard, ch)
        r.F[j, e, :, :, :, :, 0:ch] = nn(r.h2T[...], r.giS[...]).astype(bf16).reshape(shape)
        r.F[j, e, :, :, :, :, ch : 2 * ch] = (
            nn(r.gfT[...], r.actS[...]).astype(bf16).reshape(shape)
        )
        return send(r.F.at[j, e, :, :, 1 - c], r.FC.at[j, e], over_c)

    def f_add_c(j, e):
        @pl.loop(0, 2 * nz)
        def _(t):
            a, b = t // 2, t % 2
            r.F[j, e, a, b, c] = r.F[j, e, a, b, c] + r.FC[j, e, a, b]
    got(w0_c, w1_c)
    f0p = feed(0, 1 - y, True)
    got(w2_x)
    w2_c = w_over_c(2)
    f0m = feed(0, y)
    got(f0p)
    f_add_c(0, 1 - y)
    f0_y = send(r.F.at[0, 1 - y, :, :, c], r.FY0, over_y)
    got(*w3_z)
    w3_c = w_over_c(3)
    got(f0m)
    f_add_c(0, y)
    got(w2_c, w3_c)
    f1p = feed(1, 1 - y)
    f1m = feed(1, y)
    got(f1p)
    f_add_c(1, 1 - y)
    f1_xa = send(r.F.at[1, 1 - y, :, 1 - x, c], r.FX1.at[0], over_x)
    r.gain_rows[...] = jnp.zeros_like(r.gain_rows)

    def turn(u):
        at = cut(u, 2 * rb)
        pair = pl.ds(2 * u, 2)
        valid = valid_pair(u)
        outs = (r.res[at, :] + valid * r.acc[at, :]).astype(bf16)
        mine, other = outs[:, : width // 2], outs[:, width // 2 :]
        low = y == 0
        shape = (2, rb, width // 2)
        r.outm[pair] = jnp.where(low, mine, other).reshape(shape)
        r.outx[pair] = jnp.where(low, other, mine).reshape(shape)
        u2, normed = r.gh2[at, :], r.n2[at, :]
        r.gain_rows[1:2, :] += jnp.sum(u2 * normed, axis=0, keepdims=True)
        back = norm_back(u2, normed, r.r2[at, :], r.gain2[...])
        flat = (2 * rb, width // 2)
        go = jnp.concatenate(
            (r.GO[0, pair].reshape(flat), r.GO[1, pair].reshape(flat)), axis=1
        ).astype(f32)
        gr = go + back
        r.res[at, :] = gr
        ga = (valid * gr).astype(bf16)
        r.gatt[at, :] = ga
        for e in range(2):
            r.wide[:, e * half : (e + 1) * half] = nt(ga, r.WO[e])
        for s in range(2):
            i = 2 * u + s

            @pl.loop(0, rb // 16, unroll=4)
            def _(t):
                at = cut(t, 16)
                atr = pl.ds(pl.multiple_of(i * rb + t * 16, 16), 16)
                atw = pl.ds(pl.multiple_of(s * rb + t * 16, 16), 16)
                parts = [r.wide[atw, pl.ds(128 * g, 128)] for g in range(groups)]
                ln = lanes((16, 128))
                hf = (ln >= 64).astype(jnp.int32)
                gd = jnp.zeros((16, 128), f32)
                for k in range(top):
                    mine = r.idl[i, k, at, :]
                    val = jnp.zeros((16, 128), f32)
                    for g in range(groups):
                        val = jnp.where(mine == 2 * g, parts[g], val)
                    dot = jnp.sum(val * r.O[i, k, at, :], axis=-1, keepdims=True)
                    gd = jnp.where(mine + hf == ln, dot, gd)
                    r.dOs[i, k, at, :] = (r.gateb[i, k, at, :] * val).astype(bf16)
                dn = r.dense[atr, :]
                gs = dn * (gd - jnp.sum(dn * gd, axis=-1, keepdims=True))
                r.glog[atr, :] = gs.astype(bf16)

    pl.loop(0, nb // 4)(turn)
    got(f1m)
    f_add_c(1, y)
    f1_xb = send(r.F.at[1, y, :, 1 - x, c], r.FX1.at[1], over_x)
    pl.loop(nb // 4, nb // 2)(turn)
    l_out = here(8, r.outm, r.out.at[:, y])
    routed = jnp.zeros((128, width), f32)
    for i in range(nb):
        routed = routed + tn(r.glog[i * rb : (i + 1) * rb, :], r.h1[own(i)])
    bottom = lax.broadcasted_iota(jnp.int32, (32, width), 0) == 31
    r.S[0] = jnp.where(bottom, r.gain_rows[1:2, :], routed[0:32]).astype(bf16)
    s_c = send(r.S.at[0], r.SR.at[0], over_c)
    got(f0_y)

    @pl.loop(0, 2 * nz)
    def _(t):
        a, b = t // 2, t % 2
        r.F[0, y, a, b, c] = r.F[0, y, a, b, c] + r.FY0[a, b]

    f0_z = [
        send(r.F.at[0, y, k, :, c], r.FZ0.at[i], to) for i, (k, to) in enumerate(zip(zs, over_z))
    ]

    woc = r.P.shape[4]
    for e in range(2):
        r.P[e] = (
            tn(r.gated[:, e * half : (e + 1) * half], r.gatt[...])
            .astype(bf16)
            .reshape(nz, 2, 2, woc, width)
        )
    p_c = send(r.P.at[:, :, :, 1 - c], r.PC, over_c)

    def back(i):
        nk = 256 * (i + 1)
        start = 128 * i * (i + 1)
        last = i == nb - 1
        v = nn(r.PT[start : start + nk, :], r.dOs[i].reshape(top * rb, 128))
        r.gV[0:nk, :] = v if last else r.gV[0:nk, :] + v

        @pl.loop(0, top // 2, unroll=4)
        def _(p):
            do = r.dOs[i, pl.ds(2 * p, 2)].reshape(256, 128)
            cols = cut(p, 256)
            dp = nt(r.VV[0:nk, :], do)
            pr = r.PT[start : start + nk, cols].astype(f32)
            s = jnp.sum(pr * dp, axis=0, keepdims=True)
            ds = (pr * (dp - s)).astype(bf16)
            r.PT[start : start + nk, cols] = ds
            dq = nn(r.KKT[:, 0:nk], ds)
            r.dQ[pl.ds(2 * p, 2)] = dq.T.reshape(2, rb, 128)

        @pl.loop(0, rb // 16, unroll=4)
        def _(t):
            at = cut(t, 16)
            atr = pl.ds(pl.multiple_of(i * rb + t * 16, 16), 16)
            mine = [r.idl[i, k, at, :] for k in range(top)]
            vals = [r.dQ[k, at, :] for k in range(top)]
            for g in range(groups):
                val = jnp.zeros((16, 128), f32)
                for k in range(top):
                    val = jnp.where(mine[k] == 2 * g, vals[k], val)
                r.gq[atr, pl.ds(128 * g, 128)] = val.astype(bf16) * 0.125

    def key_sums(i):
        v = nn(r.PT[128 * i * (i + 1) : 128 * (i + 1) * (i + 2), :], r.Qs[i].reshape(top * rb, 128))
        at = pl.ds(0, 256 * (i + 1))
        r.gK[at, :] = v if i == nb - 1 else r.gK[at, :] + v
        for s in range(2):
            at = pl.ds((2 * i + s) * rb, rb)
            a, b = r.gK[at, :], r.gV[at, :]
            a = a + pltpu.roll(a, 64, 1)
            b = b + pltpu.roll(b, 64, 1)
            r.kvs[i, s] = jnp.where(lane < 64, a, b).astype(bf16)
        return send(r.kvs.at[i, 1 - y], r.kvr.at[i], over_y)

    def finish(i):
        at = pl.ds(i * rb, rb)
        low = (r.kvs[i, y].astype(f32) + r.kvr[i].astype(f32)).astype(bf16)
        r.kvr[i] = low
        g = r.acc[at, :] + nt(low, r.wkvg[...].reshape(width, 128))
        normed, inv = norm_rows(r.tok[own(i)].astype(f32))
        r.gain_rows[0:1, :] += jnp.sum(g * normed, axis=0, keepdims=True)
        back = norm_back(g, normed, inv, r.gain1[...])
        r.gts[i] = (r.res[at, :] + back).astype(bf16)
        return here(9 + i, r.gts.at[i], r.gt.at[i, y])

    def before(u):
        at = pl.ds(u * 2 * rb, 2 * rb)
        g = nn(r.glog[at, :], r.wrp[...])
        for e in range(2):
            g = g + nt(r.gq[at, e * half : (e + 1) * half], r.WQ[e])
        r.acc[at, :] = g

    def give(i):
        return send(r.gts.at[i], r.gt.at[i, y], over_y)

    keys, ends = {}, []
    for i in range(nb - 1, 2, -1):
        back(i)
        keys[i] = key_sums(i)
    got(s_c)
    r.S[1] = r.S[0] + r.SR[0]
    s_x = send(r.S.at[1], r.SR.at[1], over_x)
    got(p_c)

    @pl.loop(0, 4 * nz)
    def _(t):
        e, a, b = t // (2 * nz), (t // 2) % nz, t % 2
        r.P[e, a, b, c] = r.P[e, a, b, c] + r.PC[e, a, b]

    p_x = send(r.P.at[:, :, 1 - x, c], r.PX, over_x)
    got(f1_xa, f1_xb)

    @pl.loop(0, nz)
    def _(a):
        r.F[1, 1 - y, a, x, c] = r.F[1, 1 - y, a, x, c] + r.FX1[0, a]
        r.F[1, y, a, x, c] = r.F[1, y, a, x, c] + r.FX1[1, a]

    f1_y = send(r.F.at[1, 1 - y, :, x, c], r.FY1, over_y)
    back(2)
    keys[2] = key_sums(2)
    for u in range(1, nb // 2):
        before(u)
    for i in range(nb - 1, 2, -1):
        got(keys[i])
        ends.append(finish(i))
    gts_y = [give(i) for i in range(nb - 1, 2, -1)]
    got(s_x)
    r.S[2] = r.S[1] + r.SR[1]
    s_y = send(r.S.at[2], r.SR.at[2], over_y)
    got(*f0_z)
    for b in range(2):
        v = r.F[0, y, z, b, c].astype(f32)
        for k in range(nz - 1):
            v = v + r.FZ0[k, b].astype(f32)
        r.F[0, y, z, b, c] = v.astype(bf16)
    f0_x = send(r.F.at[0, y, z, 1 - x, c], r.FX0, over_x)
    back(1)
    keys[1] = key_sums(1)
    got(p_x)

    @pl.loop(0, 2 * nz)
    def _(t):
        e, a = t // nz, t % nz
        r.P[e, a, x, c] = r.P[e, a, x, c] + r.PX[e, a]

    p_y = send(r.P.at[1 - y, :, x, c], r.PY, over_y)
    got(f1_y)

    @pl.loop(0, nz)
    def _(a):
        r.F[1, y, a, x, c] = r.F[1, y, a, x, c] + r.FY1[a]

    f1_z = [
        send(r.F.at[1, y, k, x, c], r.FZ1.at[i], to) for i, (k, to) in enumerate(zip(zs, over_z))
    ]
    got(keys[2])
    ends.append(finish(2))
    back(0)
    for copy in [w_y0, w_y1, w3_x, w0_x, w1_x, w2_x, w0_c, w1_c, w2_c, w3_c,
                 *w0_z, *w1_z, *w2_z, *w3_z]:
        copy.wait_send()
        sent[:] = [other for other in sent if other is not copy]
    one, two = pl.ds(0, half // 2), pl.ds(half // 2, half // 2)
    q_c2 = []
    for part in range(2):
        side = pl.ds(part * (half // 2), half // 2)
        for e in range(2):
            at = pl.ds(e * half + part * (half // 2), half // 2)
            r.Q[e, :, :, :, :, side] = (
                nn(r.h1T[...], r.gq[:, at]).astype(bf16).reshape(nz, 2, 2, shard, half // 2)
            )
        q_c2.append(
            send(r.Q.at[:, :, :, 1 - c, :, side], r.QC.at[:, :, :, :, side], over_c)
        )
    keys[0] = key_sums(0)
    got(s_y)
    r.S[3] = r.S[2] + r.SR[2]
    r.SZ[z] = r.S[3]
    s_z = [send(r.S.at[3], r.SZ.at[z], to) for to in over_z]
    for part, side in enumerate((one, two)):
        got(q_c2[part])

        @pl.loop(0, 4 * nz)
        def _(t):
            e, a, b = t // (2 * nz), (t // 2) % nz, t % 2
            r.Q[e, a, b, c, :, side] = r.Q[e, a, b, c, :, side] + r.QC[e, a, b, :, side]

        if part == 0:
            qa_x = send(r.Q.at[:, :, 1 - x, c, :, one], r.QXA, over_x)
    qb_y = send(r.Q.at[1 - y, :, :, c, :, two], r.QYB, over_y)
    gts_y.append(give(2))
    before(0)
    got(keys[1])
    ends.append(finish(1))
    got(p_y)

    @pl.loop(0, nz)
    def _(a):
        r.P[y, a, x, c] = r.P[y, a, x, c] + r.PY[a]

    p_z = [send(r.P.at[y, k, x, c], r.PZ.at[i], to) for i, (k, to) in enumerate(zip(zs, over_z))]
    got(f0_x)
    v = r.F[0, y, z, x, c].astype(f32) + r.FX0[...].astype(f32)
    r.gwh[:, 0:ch] = v[:, 0:ch]
    r.gwT[:, 0:ch] = v[:, ch : 2 * ch]
    got(keys[0])
    ends.append(finish(0))
    r.K[...] = nn(r.h1T[...], r.kvr[...].reshape(nb * rb, 128)).reshape(nz, 2, 2, shard, 128)
    k_c = send(r.K.at[:, :, 1 - c], r.KC, over_c)
    r.G[0] = r.gain_rows[0:1, :]
    g1_c = send(r.G.at[0], r.GR.at[0], over_c)
    got(qa_x)

    @pl.loop(0, 2 * nz)
    def _(t):
        e, a = t // nz, t % nz
        r.Q[e, a, x, c, :, one] = r.Q[e, a, x, c, :, one] + r.QXA[e, a]

    qa_y = send(r.Q.at[1 - y, :, x, c, :, one], r.QYA, over_y)
    got(qb_y)

    @pl.loop(0, 2 * nz)
    def _(t):
        a, b = t // 2, t % 2
        r.Q[y, a, b, c, :, two] = r.Q[y, a, b, c, :, two] + r.QYB[a, b]

    qb_x = send(r.Q.at[y, :, 1 - x, c, :, two], r.QXB, over_x)
    gts_y.append(give(1))
    gts_y.append(give(0))
    got(k_c)

    @pl.loop(0, 2 * nz)
    def _(t):
        a, b = t // 2, t % 2
        r.K[a, b, c] = r.K[a, b, c] + r.KC[a, b]

    k_x = send(r.K.at[:, 1 - x, c], r.KX, over_x)
    got(g1_c)
    r.G[1] = r.G[0] + r.GR[0]
    g1_x = send(r.G.at[1], r.GR.at[1], over_x)
    got(*p_z)
    v = r.P[y, z, x, c].astype(f32)
    for k in range(nz - 1):
        v = v + r.PZ[k].astype(f32)
    r.PA[z, x, c] = v.astype(bf16)
    pa_z = [send(r.PA.at[z, x, c], r.PA.at[z, x, c], to) for to in over_z]

    got(qa_y, qb_x)

    @pl.loop(0, nz)
    def _(a):
        r.Q[y, a, x, c, :, one] = r.Q[y, a, x, c, :, one] + r.QYA[a]
        r.Q[y, a, x, c, :, two] = r.Q[y, a, x, c, :, two] + r.QXB[a]

    q_z = [send(r.Q.at[y, k, x, c], r.QZ.at[i], to) for i, (k, to) in enumerate(zip(zs, over_z))]
    got(k_x)

    @pl.loop(0, nz)
    def _(a):
        r.K[a, x, c] = r.K[a, x, c] + r.KX[a]

    k_z = [send(r.K.at[k, x, c], r.KZ.at[i], to) for i, (k, to) in enumerate(zip(zs, over_z))]
    got(g1_x)
    r.G[2] = r.G[1] + r.GR[1]
    g1_y = send(r.G.at[2], r.GR.at[2], over_y)
    got(*f1_z)
    v = r.F[1, y, z, x, c].astype(f32)
    for k in range(nz - 1):
        v = v + r.FZ1[k].astype(f32)
    r.gwh[:, ch : 2 * ch] = v[:, 0:ch]
    r.gwT[:, ch : 2 * ch] = v[:, ch : 2 * ch]
    got(*s_z)
    v = r.SZ[0].astype(f32)
    for k in range(1, nz):
        v = v + r.SZ[k].astype(f32)
    r.small[...] = v
    got(*pa_z)
    pa_x = send(r.PA.at[:, x, c], r.PA.at[:, x, c], over_x)
    got(*k_z)
    v = r.K[z, x, c]
    for k in range(nz - 1):
        v = v + r.KZ[k]
    r.KY[0] = v
    k_y = send(r.KY.at[0], r.KY.at[1], over_y)
    out_y = send(r.outx, r.out.at[:, y], over_y)
    got(*q_z)
    v = r.Q[y, z, x, c].astype(f32)
    for k in range(nz - 1):
        v = v + r.QZ[k].astype(f32)
    r.QA[z, x, c] = v.astype(bf16)
    view = r.QA.at[z, x, c, :, two]
    gb_x = send(view, view, over_x)
    view = r.QA.at[z, x, c, :, one]
    ga_z = [send(view, view, to) for to in over_z]
    got(g1_y)
    r.G[3] = r.G[2] + r.GR[2]
    r.GZ[z] = r.G[3]
    g1_z = [send(r.G.at[3], r.GZ.at[z], to) for to in over_z]
    got(gb_x)
    view = r.QA.at[z, :, c, :, two]
    gb_z = [send(view, view, to) for to in over_z]
    got(pa_x)
    pa_c = send(r.PA.at[:, :, c], r.PA.at[:, :, c], over_c)
    got(k_y)
    r.gkv[...] = r.KY[0] + r.KY[1]
    got(*ga_z)
    view = r.QA.at[:, x, c, :, one]
    ga_x = send(view, view, over_x)
    got(*g1_z)
    v = r.GZ[0]
    for k in range(1, nz):
        v = v + r.GZ[k]
    r.gain1_out[...] = v
    got(*gb_z)
    view = r.QA.at[:, :, c, :, two]
    gb_c = send(view, view, over_c)
    got(ga_x)
    view = r.QA.at[:, :, c, :, one]
    ga_c = send(view, view, over_c)
    got(pa_c, gb_c, ga_c)
    l_out.wait()
    for copy in ends:
        copy.wait()
    got(out_y, *gts_y)
    for copy in sent:
        copy.wait_send()


def close(out, gt, QA, PA, gwh, gwT, gkv, small, gain1,
          o_out, o_gt, o_wq, o_wo, o_wh, o_wT, o_k, o_v, o_wr, o_g1, o_g2,
          b_q, b_o, b_k, b_s, sem):
    pairs = ((QA, b_q), (PA, b_o), (gkv, b_k), (small, b_s),
             (gt, o_gt), (out, o_out), (gwh, o_wh), (gwT, o_wT), (gain1, o_g1))
    copies = [pltpu.make_async_copy(a, b, sem.at[k]) for k, (a, b) in enumerate(pairs)]
    for copy in copies:
        copy.start()
    copies[0].wait()
    o_wq[...] = b_q[...].astype(f32)
    copies[1].wait()
    o_wo[...] = b_o[...].astype(f32)
    copies[2].wait()
    o_k[...] = b_k[:, 0:64]
    o_v[...] = b_k[:, 64:128]
    copies[3].wait()
    o_wr[...] = b_s[0 : o_wr.shape[0], :]
    o_g2[...] = b_s[31:32, :]
    for copy in copies[4:]:
        copy.wait()


def shards(
    tokens, gain_attn, w_key, w_value, w_router, w_query, w_out, gain_ffn,
    w_hidden, w_output, expert_ids, lengths, grad_out,
):
    rows, width = tokens.shape
    dp = lax.axis_size("dp")
    inner = min(dp, 16)
    outer = dp // inner
    nz = inner // 4
    nb = rows // rb // 2
    top = expert_ids.shape[1]
    n_experts = w_router.shape[1]
    half = w_query.shape[1]
    ffh = w_hidden.shape[1]
    near = [[g * outer + k for k in range(outer)] for g in range(inner)]
    wt = w_output.T
    if outer > 1:
        w_key, w_value, w_hidden, wt = (
            lax.all_gather(v, "dp", axis=0, tiled=True, axis_index_groups=near)
            for v in (w_key, w_value, w_hidden, wt)
        )
    shard = width // inner
    woc = half // inner
    sds = jax.ShapeDtypeStruct
    spec = scratch(rows, width, nb, top, 2 * half, 2 * ffh, nz, shard)
    names = in_names + out_names + list(spec)
    vmem = pl.BlockSpec(memory_space=pltpu.VMEM)
    anyw = pl.BlockSpec(memory_space=pl.ANY)
    out, gt, QA, PA, gwh, gwT, gkv, small, gain1 = pl.pallas_call(
        functools.partial(kernel, names, outer),
        out_shape=(
            sds((nb, 2, rb, width // 2), bf16),
            sds((nb, 2, rb, width), bf16),
            sds((nz, 2, 2, shard, half), bf16),
            sds((nz, 2, 2, woc, width), bf16),
            sds((shard, ffh), f32),
            sds((shard, ffh), f32),
            sds((shard, 128), f32),
            sds((32, width), f32),
            sds((1, width), f32),
        ),
        in_specs=[pl.BlockSpec(memory_space=pltpu.SMEM)] + [anyw] + [vmem] * 6 + [anyw] * 5,
        out_specs=[anyw] * 2 + [vmem] * 7,
        scratch_shapes=list(spec.values()),
        compiler_params=pltpu.CompilerParams(
            collective_id=0, has_side_effects=True, vmem_limit_bytes=63 * 2**20
        ),
    )(
        lengths, tokens.reshape(2 * nb, rb, width), gain_attn[None], w_router.T, gain_ffn[None],
        expert_ids.T, w_key, w_value, w_query, w_out, w_hidden, wt,
        grad_out.reshape(nb, 2, rb, width // 2),
    )
    out, gt, gwq, gwo, gwh, gwT, gk, gv, gwr, g1, g2 = pl.pallas_call(
        close,
        out_shape=(
            sds(out.shape, bf16),
            sds(gt.shape, bf16),
            sds((width, half), f32),
            sds((half, width), f32),
            sds((shard, ffh), f32),
            sds((shard, ffh), f32),
            sds((shard, 64), f32),
            sds((shard, 64), f32),
            sds((n_experts, width), f32),
            sds((1, width), f32),
            sds((1, width), f32),
        ),
        in_specs=[anyw] * 9,
        out_specs=[vmem] * 11,
        scratch_shapes=[
            pltpu.VMEM((width, half), bf16),
            pltpu.VMEM((half, width), bf16),
            pltpu.VMEM((shard, 128), f32),
            pltpu.VMEM((32, width), f32),
            pltpu.SemaphoreType.DMA((9,)),
        ],
        compiler_params=pltpu.CompilerParams(vmem_limit_bytes=63 * 2**20),
    )(out, gt, QA.reshape(width, half), PA.reshape(half, width), gwh, gwT, gkv, small, gain1)
    if outer > 1:
        gwq, gwo, gwr, g1, g2 = lax.psum(
            (gwq, gwo, gwr, g1, g2), "dp", axis_index_groups=near
        )
        gwh, gwT, gk, gv = (
            lax.psum_scatter(v, "dp", scatter_dimension=0, tiled=True, axis_index_groups=near)
            for v in (gwh, gwT, gk, gv)
        )
    return (
        out.reshape(rows, width // 2), gt.reshape(rows, width), gk, gv, gwr.T, gwq, gwo,
        gwh, gwT.T, g1[0], g2[0],
    )


def solution(mesh):
    placed = (
        P("dp", None), P(), P("dp", None), P("dp", None), P(), P(None, "expert"),
        P("expert", None), P(), P("dp", "expert"), P("expert", "dp"), P("dp", None),
        P("dp"), P("dp", "expert"),
    )
    return jax.shard_map(
        shards,
        mesh=mesh,
        in_specs=placed,
        out_specs=(
            P("dp", "expert"), P("dp", None), P("dp", None), P("dp", None), P(),
            P(None, "expert"), P("expert", None), P("dp", "expert"), P("expert", "dp"),
            P(), P(),
        ),
        check_vma=False,
    )
```

```python
import functools

import jax
import jax.numpy as jnp
from jax import lax
from jax.experimental import pallas as pl
from jax.experimental.pallas import tpu as pltpu
from jax.sharding import PartitionSpec as P

f32 = jnp.float32
bf16 = jnp.bfloat16
eps = 1e-05
lowest = -1e30
rb = 128


def nn(left, right):
    return jnp.dot(left, right, preferred_element_type=f32)


def nt(left, right):
    return lax.dot_general(left, right, (((1,), (1,)), ((), ())), preferred_element_type=f32)


def tn(left, right):
    return lax.dot_general(left, right, (((0,), (0,)), ((), ())), preferred_element_type=f32)


def norm_rows(x):
    centred = x - jnp.mean(x, axis=-1, keepdims=True)
    inv = lax.rsqrt(jnp.mean(centred * centred, axis=-1, keepdims=True) + eps)
    return centred * inv, inv


def norm_back(u, normed, inv, gain):
    w = u * gain
    return inv * (
        w
        - jnp.mean(w, axis=-1, keepdims=True)
        - normed * jnp.mean(w * normed, axis=-1, keepdims=True)
    )


def lanes(shape):
    return lax.broadcasted_iota(jnp.int32, shape, len(shape) - 1)


MESH = pl.DeviceIdType.MESH

in_names = [
    "len_ref",
    "tok_in",
    "gain1",
    "wrt",
    "gain2",
    "idst",
    "wk_in",
    "wv_in",
    "wq_in",
    "wo_in",
    "wh_in",
    "wt_in",
    "go_in",
]
out_names = [
    "out",
    "gt",
    "QA",
    "PA",
    "gwh",
    "gwT",
    "gkv",
    "small",
    "gain1_out",
]


def scratch(rows, width, nb, top, fq, ff, nz, shard):
    vm = pltpu.VMEM
    own = rows // 2
    half = fq // 2
    total = 128 * nb * (nb + 1)
    ring = (nz, 2, 2)
    ch = ff // 4
    woc = half // (4 * nz)
    return {
        "tok": vm((2 * nb, rb, width), bf16),
        "outm": vm((nb, rb, width // 2), bf16),
        "gts": vm((nb, rb, width), bf16),
        "G": vm((4, 1, width), f32),
        "GR": vm((3, 1, width), f32),
        "GZ": vm((nz, 1, width), f32),
        "wkvg": vm(ring + (shard, 128), bf16),
        "W": vm((2, 2) + ring + (shard, 2 * ch), bf16),
        "WQ": vm((2, width, half), bf16),
        "WO": vm((2, half, width), bf16),
        "GO": vm((2, nb, rb, width // 2), bf16),
        "h1": vm((2 * nb, rb, width), bf16),
        "h1T": vm((width, own), bf16),
        "KK": vm((rows, 128), bf16),
        "VV": vm((rows, 128), bf16),
        "KKT": vm((128, rows), bf16),
        "VVT": vm((128, rows), bf16),
        "idl": vm((nb, top, rb, 128), jnp.int32),
        "gateb": vm((nb, top, rb, 128), f32),
        "dense": vm((own, 128), f32),
        "Qs": vm((nb, top, rb, 128), bf16),
        "PT": vm((total, top * rb), bf16),
        "O": vm((nb, top, rb, 128), f32),
        "wide": vm((2 * rb, fq), f32),
        "gated": vm((own, fq), bf16),
        "n2": vm((own, width), f32),
        "r2": vm((own, 1), f32),
        "res": vm((own, width), f32),
        "h2": vm((own, width), bf16),
        "h2T": vm((width, own), bf16),
        "gfT": vm((width, own), bf16),
        "gf": vm((own, width), bf16),
        "gh2": vm((own, width), f32),
        "acc": vm((own, width), f32),
        "gatt": vm((own, width), bf16),
        "dOs": vm((nb, top, rb, 128), bf16),
        "glog": vm((own, 128), bf16),
        "AG": vm((own, 2 * ch), bf16),
        "wrp": vm((128, width), bf16),
        "gK": vm((rows, 128), f32),
        "gV": vm((rows, 128), f32),
        "dQ": vm((top, rb, 128), f32),
        "gain_rows": vm((2, width), f32),
        "outx": vm((nb, rb, width // 2), bf16),
        "kvs": vm((nb, 2, rb, 128), bf16),
        "kvr": vm((nb, rb, 128), bf16),
        "F": vm((2, 2) + ring + (shard, 2 * ch), bf16),
        "FC": vm((2, 2, nz, 2, shard, 2 * ch), bf16),
        "FY0": vm((nz, 2, shard, 2 * ch), bf16),
        "FZ0": vm((nz - 1, 2, shard, 2 * ch), bf16),
        "FX0": vm((shard, 2 * ch), bf16),
        "FX1": vm((2, nz, shard, 2 * ch), bf16),
        "FY1": vm((nz, shard, 2 * ch), bf16),
        "FZ1": vm((nz - 1, shard, 2 * ch), bf16),
        "QC": vm((2, nz, 2, shard, half), bf16),
        "QXA": vm((2, nz, shard, half // 2), bf16),
        "QYA": vm((nz, shard, half // 2), bf16),
        "QYB": vm((nz, 2, shard, half // 2), bf16),
        "QXB": vm((nz, shard, half // 2), bf16),
        "QZ": vm((nz - 1, shard, half), bf16),
        "P": vm((2,) + ring + (woc, width), bf16),
        "PC": vm((2, nz, 2, woc, width), bf16),
        "PX": vm((2, nz, woc, width), bf16),
        "PY": vm((nz, woc, width), bf16),
        "PZ": vm((nz - 1, woc, width), bf16),
        "K": vm(ring + (shard, 128), f32),
        "KC": vm((nz, 2, shard, 128), f32),
        "KX": vm((nz, shard, 128), f32),
        "KZ": vm((nz - 1, shard, 128), f32),
        "KY": vm((2, shard, 128), f32),
        "S": vm((4, 32, width), bf16),
        "SR": vm((3, 32, width), bf16),
        "SZ": vm((nz, 32, width), bf16),
        "send": pltpu.SemaphoreType.DMA((128,)),
        "recv": pltpu.SemaphoreType.DMA((128,)),
        "local": pltpu.SemaphoreType.DMA((16,)),
    }


class Refs:
    pass


def kernel(names, outer, *refs):
    r = Refs()
    for name, ref in zip(names, refs):
        setattr(r, name, ref)
    nb = r.tok.shape[0] // 2
    width = r.tok.shape[2]
    top = r.idst.shape[0]
    fq = r.gated.shape[1]
    half = fq // 2
    groups = fq // 128
    r.gq = r.gated
    r.Q = r.W.at[0, :, :, :, :, :, 0:half]
    r.actS = r.AG.at[:, 0 : r.W.shape[6] // 2]
    r.giS = r.AG.at[:, r.W.shape[6] // 2 : r.W.shape[6]]
    nz = r.W.shape[2]
    ch = r.W.shape[6] // 2
    shard = r.W.shape[5]
    d = lax.axis_index("dp")
    y = lax.axis_index("expert")
    n, m = d // outer, d % outer
    z, x, c = n // 4, (n // 2) % 2, n % 2
    length = r.len_ref[0]

    def device(z, x, c, y):
        return ((z * 4 + x * 2 + c) * outer + m, y)

    over_c = device(z, x, 1 - c, y)
    over_x = device(z, 1 - x, c, y)
    over_y = device(z, x, c, 1 - y)
    zs = [(z + k) % nz for k in range(1, nz)]
    over_z = [device(k, x, c, y) for k in zs]
    used = [0]
    sent = []

    def send(source, target, to):
        k = used[0]
        used[0] += 1
        copy = pltpu.make_async_remote_copy(
            src_ref=source, dst_ref=target, send_sem=r.send.at[k], recv_sem=r.recv.at[k],
            device_id=to, device_id_type=MESH,
        )
        copy.start()
        sent.append(copy)
        return copy

    def here(k, source, target):
        copy = pltpu.make_async_copy(source, target, r.local.at[k])
        copy.start()
        return copy

    def got(*copies):
        for copy in copies:
            copy.wait_recv()

    def own(i):
        return 2 * i + y

    def cut(i, size):
        return pl.ds(pl.multiple_of(i * size, size), size)

    def valid_rows(i):
        return (rb * own(i) + lax.broadcasted_iota(jnp.int32, (rb, 1), 0) < length).astype(f32)

    l_w = [
        here(2 * j + k, ref.at[:, j * ch : (j + 1) * ch],
             r.W.at[j, y, z, x, c, :, k * ch : (k + 1) * ch])
        for j in range(2)
        for k, ref in enumerate((r.wh_in, r.wt_in))
    ]
    l_tok = here(7, r.tok_in, r.tok)
    l_q = here(4, r.wq_in, r.WQ.at[y])
    l_o = here(5, r.wo_in, r.WO.at[y])
    l_g = here(6, r.go_in.at[:, y], r.GO.at[y])
    r.wkvg[z, x, c] = jnp.concatenate((r.wk_in[...], r.wv_in[...]), axis=1)
    barrier = pltpu.get_barrier_semaphore()
    peers = [over_c, over_x, over_y] + over_z
    for peer in peers:
        pl.semaphore_signal(barrier, inc=1, device_id=peer, device_id_type=MESH)
    pl.semaphore_wait(barrier, len(peers))
    kv_z = [send(r.wkvg.at[z, x, c], r.wkvg.at[z, x, c], to) for to in over_z]
    l_w[0].wait()
    l_w[1].wait()
    w_y0 = send(r.W.at[0, y, z, x, c], r.W.at[0, y, z, x, c], over_y)
    qrows = cut(c, width // 2)
    q_y = send(r.wq_in.at[qrows, :], r.WQ.at[y, qrows, :], over_y)
    l_w[2].wait()
    l_w[3].wait()
    w_y1 = send(r.W.at[1, y, z, x, c], r.W.at[1, y, z, x, c], over_y)
    orows = cut(c, half // 2)
    o_y = send(r.wo_in.at[orows, :], r.WO.at[y, orows, :], over_y)
    g_y = send(r.go_in.at[:, 1 - y], r.GO.at[y], over_y)
    spare = jnp.zeros((128 - r.wrt.shape[0], width), f32)
    r.wrp[...] = jnp.concatenate((r.wrt[...].astype(f32), spare), axis=0).astype(bf16)

    def w_part(k):
        return r.W.at[k // 2, :, :, :, :, :, pl.ds((k % 2) * ch, ch)]

    def w_over_z(k, both=False):
        view = w_part(k).at[:, z, :, c] if both else w_part(k).at[:, z, x, c]
        return [send(view, view, to) for to in over_z]

    def w_over_x(k, line=True):
        view = w_part(k).at[:, :, x, c] if line else w_part(k).at[:, z, x, c]
        return send(view, view, over_x)

    def w_over_c(k):
        view = w_part(k).at[:, :, :, c]
        return send(view, view, over_c)
    l_tok.wait()

    @pl.loop(0, 2 * nb)
    def _(b):
        normed, _ = norm_rows(r.tok[b].astype(f32))
        r.h1[b] = (normed * r.gain1[...]).astype(bf16)
    got(*kv_z)
    kv_x = send(r.wkvg.at[:, x, c], r.wkvg.at[:, x, c], over_x)
    got(w_y0)
    w0_z = w_over_z(0)
    w1_z = w_over_z(1)

    lane = lanes((rb, 128))
    upper = (lane >= 64).astype(jnp.int32)

    def gates(i):
        h = r.h1[own(i)]
        at = cut(i, rb)
        r.h1T[:, at] = h.astype(f32).T.astype(bf16)
        logits = nt(h, r.wrp[...])
        ids = r.idst[:, cut(own(i), rb)].astype(f32).T.astype(jnp.int32)
        spread = [jnp.broadcast_to(ids[:, k : k + 1], (rb, 128)) for k in range(top)]
        chosen = lane == spread[0]
        for k in range(1, top):
            chosen = chosen | (lane == spread[k])
        most = jnp.max(jnp.where(chosen, logits, lowest), axis=-1, keepdims=True)
        e = jnp.where(chosen, jnp.exp(jnp.where(chosen, logits - most, 0.0)), 0.0)
        g = e / jnp.sum(e, axis=-1, keepdims=True)
        r.dense[at, :] = g
        for k in range(top):
            gk = jnp.sum(jnp.where(lane == spread[k], g, 0.0), axis=-1, keepdims=True)
            r.gateb[i, k] = jnp.broadcast_to(gk, (rb, 128))
            r.idl[i, k] = spread[k] - upper

    pl.loop(0, nb // 2)(gates)
    got(kv_x)
    kv_c = send(r.wkvg.at[:, :, c], r.wkvg.at[:, :, c], over_c)
    pl.loop(nb // 2, nb)(gates)
    got(kv_c)

    @pl.loop(0, 2 * nb)
    def _(b):
        kv = nn(r.h1[b], r.wkvg[...].reshape(width, 128))
        at = cut(b, rb)
        swapped = pltpu.roll(kv, 64, 1)
        k2 = jnp.where(lane < 64, kv, swapped)
        v2 = jnp.where(lane < 64, swapped, kv)
        r.KK[at, :] = k2.astype(bf16)
        r.VV[at, :] = v2.astype(bf16)
        r.KKT[:, at] = k2.T.astype(bf16)
        r.VVT[:, at] = v2.T.astype(bf16)
    got(*w0_z)
    w0_x = w_over_x(0)
    got(q_y)
    q_c = send(r.WQ.at[1 - y, qrows, :], r.WQ.at[1 - y, qrows, :], over_c)
    got(w_y1)
    w3_x = w_over_x(3, False)
    w2_z = w_over_z(2)
    l_q.wait()
    got(q_c)

    def two_blocks(ref, u):
        return jnp.concatenate((ref[own(2 * u)], ref[own(2 * u + 1)]), axis=0)

    @pl.loop(0, nb // 2)
    def _(u):
        h = two_blocks(r.h1, u)
        for e in range(2):
            r.wide[:, e * half : (e + 1) * half] = 0.125 * nn(h, r.WQ[e])
        for s in range(2):
            i = 2 * u + s

            @pl.loop(0, rb // 16, unroll=8)
            def _(t):
                at = cut(t, 16)
                atw = pl.ds(pl.multiple_of(s * rb + t * 16, 16), 16)
                parts = [r.wide[atw, pl.ds(128 * g, 128)] for g in range(groups)]
                for k in range(top):
                    mine = r.idl[i, k, at, :]
                    val = jnp.zeros((16, 128), f32)
                    for g in range(groups):
                        val = jnp.where(mine == 2 * g, parts[g], val)
                    r.Qs[i, k, at, :] = val.astype(bf16)
    diag = lax.broadcasted_iota(jnp.int32, (256, 256), 0) <= rb * y + lanes((256, 256)) % 128

    def attend(i):
        nk = 256 * i
        start = 128 * i * (i + 1)

        @pl.loop(0, top // 2, unroll=4)
        def _(p):
            q = r.Qs[i, pl.ds(2 * p, 2)].reshape(256, 128)
            cols = cut(p, 256)
            s1 = nt(r.KK[nk : nk + 256, :], q)
            s1 = jnp.where(diag, s1, lowest)
            most = jnp.max(s1, axis=0, keepdims=True)
            if nk:
                s0 = nt(r.KK[0:nk, :], q)
                most = jnp.maximum(most, jnp.max(s0, axis=0, keepdims=True))
                p0 = jnp.exp(s0 - most)
            p1 = jnp.exp(s1 - most)
            tot = jnp.sum(p1, axis=0, keepdims=True)
            if nk:
                tot = tot + jnp.sum(p0, axis=0, keepdims=True)
            inv = 1.0 / tot
            p1 = (p1 * inv).astype(bf16)
            r.PT[start + nk : start + nk + 256, cols] = p1
            o = nn(r.VVT[:, nk : nk + 256], p1)
            if nk:
                p0 = (p0 * inv).astype(bf16)
                r.PT[start : start + nk, cols] = p0
                o = o + nn(r.VVT[:, 0:nk], p0)
            r.O[i, pl.ds(2 * p, 2)] = o.T.reshape(2, rb, 128)

    got(w3_x)
    w3_z = w_over_z(3, True)
    got(*w1_z)
    w1_x = w_over_x(1)
    attend(0)
    attend(1)
    got(*w2_z)
    w2_x = w_over_x(2)
    got(w0_x)
    w0_c = w_over_c(0)
    attend(2)
    got(w1_x)
    w1_c = w_over_c(1)
    got(o_y)
    o_c = send(r.WO.at[1 - y, orows, :], r.WO.at[1 - y, orows, :], over_c)
    for i in range(3, nb):
        attend(i)
    l_o.wait()
    l_g.wait()
    got(o_c)
    got(g_y)
    def project(u):
        for s in range(2):
            i = 2 * u + s

            @pl.loop(0, rb // 16, unroll=8)
            def _(t):
                at = cut(t, 16)
                atr = pl.ds(pl.multiple_of(i * rb + t * 16, 16), 16)
                mine = [r.idl[i, k, at, :] for k in range(top)]
                vals = [r.gateb[i, k, at, :] * r.O[i, k, at, :] for k in range(top)]
                for g in range(groups):
                    val = jnp.zeros((16, 128), f32)
                    for k in range(top):
                        val = jnp.where(mine[k] == 2 * g, vals[k], val)
                    r.gated[atr, pl.ds(128 * g, 128)] = val.astype(bf16)

        at = cut(u, 2 * rb)
        valid = valid_pair(u)
        att = nn(r.gated[at, 0:half], r.WO[0]) + nn(r.gated[at, half:fq], r.WO[1])
        row = two_blocks(r.tok, u).astype(f32) + valid * att
        r.res[at, :] = row
        normed, inv = norm_rows(row)
        r.n2[at, :] = normed
        r.r2[at, :] = inv
        h = normed * r.gain2[...]
        r.h2[at, :] = h.astype(bf16)
        r.h2T[:, at] = h.T.astype(bf16)
        for s in range(2):
            side = pl.ds(s * (width // 2), width // 2)
            g = valid * r.GO[s, pl.ds(2 * u, 2)].reshape(2 * rb, width // 2).astype(f32)
            r.gf[at, side] = g.astype(bf16)
            r.gfT[side, at] = g.T.astype(bf16)

    def valid_pair(u):
        return jnp.concatenate((valid_rows(2 * u), valid_rows(2 * u + 1)), axis=0)

    pl.loop(0, nb // 2)(project)

    c0 = 0.7978845608028654
    c1 = 0.044715

    def feed(j, e, first=False):

        w1 = r.W[j, e, :, :, :, :, 0:ch].reshape(width, ch)
        w2 = r.W[j, e, :, :, :, :, ch : 2 * ch].reshape(width, ch)
        for i in range(nb // 2):
            at = pl.ds(i * 256, 256)
            v = nn(r.h2[at, :], w1)
            ga = nn(r.gf[at, :], w2)
            vv = v * v
            hp = 0.5 + 0.5 * jnp.tanh(v * (c0 + (c0 * c1) * vv))
            act = v * hp
            slope = hp + act * (1.0 - hp) * (2 * c0 + (6 * c0 * c1) * vv)
            r.actS[at, :] = act.astype(bf16)
            r.giS[at, :] = (slope * ga).astype(bf16)
        a = nt(r.actS[...], w2)
        b = nt(r.giS[...], w1)
        if first:
            r.acc[...] = a
            r.gh2[...] = b
        else:
            r.acc[...] += a
            r.gh2[...] += b

        shape = (nz, 2, 2, shard, ch)
        r.F[j, e, :, :, :, :, 0:ch] = nn(r.h2T[...], r.giS[...]).astype(bf16).reshape(shape)
        r.F[j, e, :, :, :, :, ch : 2 * ch] = (
            nn(r.gfT[...], r.actS[...]).astype(bf16).reshape(shape)
        )
        return send(r.F.at[j, e, :, :, 1 - c], r.FC.at[j, e], over_c)

    def f_add_c(j, e):
        @pl.loop(0, 2 * nz)
        def _(t):
            a, b = t // 2, t % 2
            r.F[j, e, a, b, c] = r.F[j, e, a, b, c] + r.FC[j, e, a, b]
    got(w0_c, w1_c)
    f0p = feed(0, 1 - y, True)
    got(w2_x)
    w2_c = w_over_c(2)
    f0m = feed(0, y)
    got(f0p)
    f_add_c(0, 1 - y)
    f0_y = send(r.F.at[0, 1 - y, :, :, c], r.FY0, over_y)
    got(*w3_z)
    w3_c = w_over_c(3)
    got(f0m)
    f_add_c(0, y)
    got(w2_c, w3_c)
    f1p = feed(1, 1 - y)
    f1m = feed(1, y)
    got(f1p)
    f_add_c(1, 1 - y)
    f1_xa = send(r.F.at[1, 1 - y, :, 1 - x, c], r.FX1.at[0], over_x)
    r.gain_rows[...] = jnp.zeros_like(r.gain_rows)

    def turn(u):
        at = cut(u, 2 * rb)
        pair = pl.ds(2 * u, 2)
        valid = valid_pair(u)
        outs = (r.res[at, :] + valid * r.acc[at, :]).astype(bf16)
        mine, other = outs[:, : width // 2], outs[:, width // 2 :]
        low = y == 0
        shape = (2, rb, width // 2)
        r.outm[pair] = jnp.where(low, mine, other).reshape(shape)
        r.outx[pair] = jnp.where(low, other, mine).reshape(shape)
        u2, normed = r.gh2[at, :], r.n2[at, :]
        r.gain_rows[1:2, :] += jnp.sum(u2 * normed, axis=0, keepdims=True)
        back = norm_back(u2, normed, r.r2[at, :], r.gain2[...])
        flat = (2 * rb, width // 2)
        go = jnp.concatenate(
            (r.GO[0, pair].reshape(flat), r.GO[1, pair].reshape(flat)), axis=1
        ).astype(f32)
        gr = go + back
        r.res[at, :] = gr
        ga = (valid * gr).astype(bf16)
        r.gatt[at, :] = ga
        for e in range(2):
            r.wide[:, e * half : (e + 1) * half] = nt(ga, r.WO[e])
        for s in range(2):
            i = 2 * u + s

            @pl.loop(0, rb // 16, unroll=8)
            def _(t):
                at = cut(t, 16)
                atr = pl.ds(pl.multiple_of(i * rb + t * 16, 16), 16)
                atw = pl.ds(pl.multiple_of(s * rb + t * 16, 16), 16)
                parts = [r.wide[atw, pl.ds(128 * g, 128)] for g in range(groups)]
                ln = lanes((16, 128))
                hf = (ln >= 64).astype(jnp.int32)
                gd = jnp.zeros((16, 128), f32)
                for k in range(top):
                    mine = r.idl[i, k, at, :]
                    val = jnp.zeros((16, 128), f32)
                    for g in range(groups):
                        val = jnp.where(mine == 2 * g, parts[g], val)
                    dot = jnp.sum(val * r.O[i, k, at, :], axis=-1, keepdims=True)
                    gd = jnp.where(mine + hf == ln, dot, gd)
                    r.dOs[i, k, at, :] = (r.gateb[i, k, at, :] * val).astype(bf16)
                dn = r.dense[atr, :]
                gs = dn * (gd - jnp.sum(dn * gd, axis=-1, keepdims=True))
                r.glog[atr, :] = gs.astype(bf16)

    pl.loop(0, nb // 4)(turn)
    got(f1m)
    f_add_c(1, y)
    f1_xb = send(r.F.at[1, y, :, 1 - x, c], r.FX1.at[1], over_x)
    pl.loop(nb // 4, nb // 2)(turn)
    l_out = here(8, r.outm, r.out.at[:, y])
    routed = jnp.zeros((128, width), f32)
    for i in range(nb):
        routed = routed + tn(r.glog[i * rb : (i + 1) * rb, :], r.h1[own(i)])
    bottom = lax.broadcasted_iota(jnp.int32, (32, width), 0) == 31
    r.S[0] = jnp.where(bottom, r.gain_rows[1:2, :], routed[0:32]).astype(bf16)
    s_c = send(r.S.at[0], r.SR.at[0], over_c)
    got(f0_y)

    @pl.loop(0, 2 * nz)
    def _(t):
        a, b = t // 2, t % 2
        r.F[0, y, a, b, c] = r.F[0, y, a, b, c] + r.FY0[a, b]

    f0_z = [
        send(r.F.at[0, y, k, :, c], r.FZ0.at[i], to) for i, (k, to) in enumerate(zip(zs, over_z))
    ]

    woc = r.P.shape[4]
    for e in range(2):
        r.P[e] = (
            tn(r.gated[:, e * half : (e + 1) * half], r.gatt[...])
            .astype(bf16)
            .reshape(nz, 2, 2, woc, width)
        )
    p_c = send(r.P.at[:, :, :, 1 - c], r.PC, over_c)

    def back(i):
        nk = 256 * (i + 1)
        start = 128 * i * (i + 1)
        last = i == nb - 1
        v = nn(r.PT[start : start + nk, :], r.dOs[i].reshape(top * rb, 128))
        r.gV[0:nk, :] = v if last else r.gV[0:nk, :] + v

        @pl.loop(0, top // 2, unroll=4)
        def _(p):
            do = r.dOs[i, pl.ds(2 * p, 2)].reshape(256, 128)
            cols = cut(p, 256)
            dp = nt(r.VV[0:nk, :], do)
            pr = r.PT[start : start + nk, cols].astype(f32)
            s = jnp.sum(pr * dp, axis=0, keepdims=True)
            ds = (pr * (dp - s)).astype(bf16)
            r.PT[start : start + nk, cols] = ds
            dq = nn(r.KKT[:, 0:nk], ds)
            r.dQ[pl.ds(2 * p, 2)] = dq.T.reshape(2, rb, 128)

        @pl.loop(0, rb // 16, unroll=8)
        def _(t):
            at = cut(t, 16)
            atr = pl.ds(pl.multiple_of(i * rb + t * 16, 16), 16)
            mine = [r.idl[i, k, at, :] for k in range(top)]
            vals = [r.dQ[k, at, :] for k in range(top)]
            for g in range(groups):
                val = jnp.zeros((16, 128), f32)
                for k in range(top):
                    val = jnp.where(mine[k] == 2 * g, vals[k], val)
                r.gq[atr, pl.ds(128 * g, 128)] = val.astype(bf16) * 0.125

    def key_sums(i):
        v = nn(r.PT[128 * i * (i + 1) : 128 * (i + 1) * (i + 2), :], r.Qs[i].reshape(top * rb, 128))
        at = pl.ds(0, 256 * (i + 1))
        r.gK[at, :] = v if i == nb - 1 else r.gK[at, :] + v
        for s in range(2):
            at = pl.ds((2 * i + s) * rb, rb)
            a, b = r.gK[at, :], r.gV[at, :]
            a = a + pltpu.roll(a, 64, 1)
            b = b + pltpu.roll(b, 64, 1)
            r.kvs[i, s] = jnp.where(lane < 64, a, b).astype(bf16)
        return send(r.kvs.at[i, 1 - y], r.kvr.at[i], over_y)

    def finish(i):
        at = pl.ds(i * rb, rb)
        low = (r.kvs[i, y].astype(f32) + r.kvr[i].astype(f32)).astype(bf16)
        r.kvr[i] = low
        g = r.acc[at, :] + nt(low, r.wkvg[...].reshape(width, 128))
        normed, inv = norm_rows(r.tok[own(i)].astype(f32))
        r.gain_rows[0:1, :] += jnp.sum(g * normed, axis=0, keepdims=True)
        back = norm_back(g, normed, inv, r.gain1[...])
        r.gts[i] = (r.res[at, :] + back).astype(bf16)
        return here(9 + i, r.gts.at[i], r.gt.at[i, y])

    def before(u):
        at = pl.ds(u * 2 * rb, 2 * rb)
        g = nn(r.glog[at, :], r.wrp[...])
        for e in range(2):
            g = g + nt(r.gq[at, e * half : (e + 1) * half], r.WQ[e])
        r.acc[at, :] = g

    def give(i):
        return send(r.gts.at[i], r.gt.at[i, y], over_y)

    keys, ends = {}, []
    for i in range(nb - 1, 2, -1):
        back(i)
        keys[i] = key_sums(i)
    got(s_c)
    r.S[1] = r.S[0] + r.SR[0]
    s_x = send(r.S.at[1], r.SR.at[1], over_x)
    got(p_c)

    @pl.loop(0, 4 * nz)
    def _(t):
        e, a, b = t // (2 * nz), (t // 2) % nz, t % 2
        r.P[e, a, b, c] = r.P[e, a, b, c] + r.PC[e, a, b]

    p_x = send(r.P.at[:, :, 1 - x, c], r.PX, over_x)
    got(f1_xa, f1_xb)

    @pl.loop(0, nz)
    def _(a):
        r.F[1, 1 - y, a, x, c] = r.F[1, 1 - y, a, x, c] + r.FX1[0, a]
        r.F[1, y, a, x, c] = r.F[1, y, a, x, c] + r.FX1[1, a]

    f1_y = send(r.F.at[1, 1 - y, :, x, c], r.FY1, over_y)
    back(2)
    keys[2] = key_sums(2)
    for u in range(1, nb // 2):
        before(u)
    for i in range(nb - 1, 2, -1):
        got(keys[i])
        ends.append(finish(i))
    gts_y = [give(i) for i in range(nb - 1, 2, -1)]
    got(s_x)
    r.S[2] = r.S[1] + r.SR[1]
    s_y = send(r.S.at[2], r.SR.at[2], over_y)
    got(*f0_z)
    for b in range(2):
        v = r.F[0, y, z, b, c].astype(f32)
        for k in range(nz - 1):
            v = v + r.FZ0[k, b].astype(f32)
        r.F[0, y, z, b, c] = v.astype(bf16)
    f0_x = send(r.F.at[0, y, z, 1 - x, c], r.FX0, over_x)
    back(1)
    keys[1] = key_sums(1)
    got(p_x)

    @pl.loop(0, 2 * nz)
    def _(t):
        e, a = t // nz, t % nz
        r.P[e, a, x, c] = r.P[e, a, x, c] + r.PX[e, a]

    p_y = send(r.P.at[1 - y, :, x, c], r.PY, over_y)
    got(f1_y)

    @pl.loop(0, nz)
    def _(a):
        r.F[1, y, a, x, c] = r.F[1, y, a, x, c] + r.FY1[a]

    f1_z = [
        send(r.F.at[1, y, k, x, c], r.FZ1.at[i], to) for i, (k, to) in enumerate(zip(zs, over_z))
    ]
    got(keys[2])
    ends.append(finish(2))
    back(0)
    for copy in [w_y0, w_y1, w3_x, w0_x, w1_x, w2_x, w0_c, w1_c, w2_c, w3_c,
                 *w0_z, *w1_z, *w2_z, *w3_z]:
        copy.wait_send()
        sent[:] = [other for other in sent if other is not copy]
    one, two = pl.ds(0, half // 2), pl.ds(half // 2, half // 2)
    q_c2 = []
    for part in range(2):
        side = pl.ds(part * (half // 2), half // 2)
        for e in range(2):
            at = pl.ds(e * half + part * (half // 2), half // 2)
            r.Q[e, :, :, :, :, side] = (
                nn(r.h1T[...], r.gq[:, at]).astype(bf16).reshape(nz, 2, 2, shard, half // 2)
            )
        q_c2.append(
            send(r.Q.at[:, :, :, 1 - c, :, side], r.QC.at[:, :, :, :, side], over_c)
        )
    keys[0] = key_sums(0)
    got(s_y)
    r.S[3] = r.S[2] + r.SR[2]
    r.SZ[z] = r.S[3]
    s_z = [send(r.S.at[3], r.SZ.at[z], to) for to in over_z]
    for part, side in enumerate((one, two)):
        got(q_c2[part])

        @pl.loop(0, 4 * nz)
        def _(t):
            e, a, b = t // (2 * nz), (t // 2) % nz, t % 2
            r.Q[e, a, b, c, :, side] = r.Q[e, a, b, c, :, side] + r.QC[e, a, b, :, side]

        if part == 0:
            qa_x = send(r.Q.at[:, :, 1 - x, c, :, one], r.QXA, over_x)
    qb_y = send(r.Q.at[1 - y, :, :, c, :, two], r.QYB, over_y)
    gts_y.append(give(2))
    before(0)
    got(keys[1])
    ends.append(finish(1))
    got(p_y)

    @pl.loop(0, nz)
    def _(a):
        r.P[y, a, x, c] = r.P[y, a, x, c] + r.PY[a]

    p_z = [send(r.P.at[y, k, x, c], r.PZ.at[i], to) for i, (k, to) in enumerate(zip(zs, over_z))]
    got(f0_x)
    v = r.F[0, y, z, x, c].astype(f32) + r.FX0[...].astype(f32)
    r.gwh[:, 0:ch] = v[:, 0:ch]
    r.gwT[:, 0:ch] = v[:, ch : 2 * ch]
    got(keys[0])
    ends.append(finish(0))
    r.K[...] = nn(r.h1T[...], r.kvr[...].reshape(nb * rb, 128)).reshape(nz, 2, 2, shard, 128)
    k_c = send(r.K.at[:, :, 1 - c], r.KC, over_c)
    r.G[0] = r.gain_rows[0:1, :]
    g1_c = send(r.G.at[0], r.GR.at[0], over_c)
    got(qa_x)

    @pl.loop(0, 2 * nz)
    def _(t):
        e, a = t // nz, t % nz
        r.Q[e, a, x, c, :, one] = r.Q[e, a, x, c, :, one] + r.QXA[e, a]

    qa_y = send(r.Q.at[1 - y, :, x, c, :, one], r.QYA, over_y)
    got(qb_y)

    @pl.loop(0, 2 * nz)
    def _(t):
        a, b = t // 2, t % 2
        r.Q[y, a, b, c, :, two] = r.Q[y, a, b, c, :, two] + r.QYB[a, b]

    qb_x = send(r.Q.at[y, :, 1 - x, c, :, two], r.QXB, over_x)
    gts_y.append(give(1))
    gts_y.append(give(0))
    got(k_c)

    @pl.loop(0, 2 * nz)
    def _(t):
        a, b = t // 2, t % 2
        r.K[a, b, c] = r.K[a, b, c] + r.KC[a, b]

    k_x = send(r.K.at[:, 1 - x, c], r.KX, over_x)
    got(g1_c)
    r.G[1] = r.G[0] + r.GR[0]
    g1_x = send(r.G.at[1], r.GR.at[1], over_x)
    got(*p_z)
    v = r.P[y, z, x, c].astype(f32)
    for k in range(nz - 1):
        v = v + r.PZ[k].astype(f32)
    r.PA[z, x, c] = v.astype(bf16)
    pa_z = [send(r.PA.at[z, x, c], r.PA.at[z, x, c], to) for to in over_z]

    got(qa_y, qb_x)

    @pl.loop(0, nz)
    def _(a):
        r.Q[y, a, x, c, :, one] = r.Q[y, a, x, c, :, one] + r.QYA[a]
        r.Q[y, a, x, c, :, two] = r.Q[y, a, x, c, :, two] + r.QXB[a]

    q_z = [send(r.Q.at[y, k, x, c], r.QZ.at[i], to) for i, (k, to) in enumerate(zip(zs, over_z))]
    got(k_x)

    @pl.loop(0, nz)
    def _(a):
        r.K[a, x, c] = r.K[a, x, c] + r.KX[a]

    k_z = [send(r.K.at[k, x, c], r.KZ.at[i], to) for i, (k, to) in enumerate(zip(zs, over_z))]
    got(g1_x)
    r.G[2] = r.G[1] + r.GR[1]
    g1_y = send(r.G.at[2], r.GR.at[2], over_y)
    got(*f1_z)
    v = r.F[1, y, z, x, c].astype(f32)
    for k in range(nz - 1):
        v = v + r.FZ1[k].astype(f32)
    r.gwh[:, ch : 2 * ch] = v[:, 0:ch]
    r.gwT[:, ch : 2 * ch] = v[:, ch : 2 * ch]
    got(*s_z)
    v = r.SZ[0].astype(f32)
    for k in range(1, nz):
        v = v + r.SZ[k].astype(f32)
    r.small[...] = v
    got(*pa_z)
    pa_x = send(r.PA.at[:, x, c], r.PA.at[:, x, c], over_x)
    got(*k_z)
    v = r.K[z, x, c]
    for k in range(nz - 1):
        v = v + r.KZ[k]
    r.KY[0] = v
    k_y = send(r.KY.at[0], r.KY.at[1], over_y)
    out_y = send(r.outx, r.out.at[:, y], over_y)
    got(*q_z)
    v = r.Q[y, z, x, c].astype(f32)
    for k in range(nz - 1):
        v = v + r.QZ[k].astype(f32)
    r.QA[z, x, c] = v.astype(bf16)
    view = r.QA.at[z, x, c, :, two]
    gb_x = send(view, view, over_x)
    view = r.QA.at[z, x, c, :, one]
    ga_z = [send(view, view, to) for to in over_z]
    got(g1_y)
    r.G[3] = r.G[2] + r.GR[2]
    r.GZ[z] = r.G[3]
    g1_z = [send(r.G.at[3], r.GZ.at[z], to) for to in over_z]
    got(gb_x)
    view = r.QA.at[z, :, c, :, two]
    gb_z = [send(view, view, to) for to in over_z]
    got(pa_x)
    pa_c = send(r.PA.at[:, :, c], r.PA.at[:, :, c], over_c)
    got(k_y)
    r.gkv[...] = r.KY[0] + r.KY[1]
    got(*ga_z)
    view = r.QA.at[:, x, c, :, one]
    ga_x = send(view, view, over_x)
    got(*g1_z)
    v = r.GZ[0]
    for k in range(1, nz):
        v = v + r.GZ[k]
    r.gain1_out[...] = v
    got(*gb_z)
    view = r.QA.at[:, :, c, :, two]
    gb_c = send(view, view, over_c)
    got(ga_x)
    view = r.QA.at[:, :, c, :, one]
    ga_c = send(view, view, over_c)
    got(pa_c, gb_c, ga_c)
    l_out.wait()
    for copy in ends:
        copy.wait()
    got(out_y, *gts_y)
    for copy in sent:
        copy.wait_send()


def close(out, gt, QA, PA, gwh, gwT, gkv, small, gain1,
          o_out, o_gt, o_wq, o_wo, o_wh, o_wT, o_k, o_v, o_wr, o_g1, o_g2,
          b_q, b_o, b_k, b_s, sem):
    pairs = ((QA, b_q), (PA, b_o), (gkv, b_k), (small, b_s),
             (gt, o_gt), (out, o_out), (gwh, o_wh), (gwT, o_wT), (gain1, o_g1))
    copies = [pltpu.make_async_copy(a, b, sem.at[k]) for k, (a, b) in enumerate(pairs)]
    for copy in copies:
        copy.start()
    copies[0].wait()
    o_wq[...] = b_q[...].astype(f32)
    copies[1].wait()
    o_wo[...] = b_o[...].astype(f32)
    copies[2].wait()
    o_k[...] = b_k[:, 0:64]
    o_v[...] = b_k[:, 64:128]
    copies[3].wait()
    o_wr[...] = b_s[0 : o_wr.shape[0], :]
    o_g2[...] = b_s[31:32, :]
    for copy in copies[4:]:
        copy.wait()


def shards(
    tokens, gain_attn, w_key, w_value, w_router, w_query, w_out, gain_ffn,
    w_hidden, w_output, expert_ids, lengths, grad_out,
):
    rows, width = tokens.shape
    dp = lax.axis_size("dp")
    inner = min(dp, 16)
    outer = dp // inner
    nz = inner // 4
    nb = rows // rb // 2
    top = expert_ids.shape[1]
    n_experts = w_router.shape[1]
    half = w_query.shape[1]
    ffh = w_hidden.shape[1]
    near = [[g * outer + k for k in range(outer)] for g in range(inner)]
    wt = w_output.T
    if outer > 1:
        w_key, w_value, w_hidden, wt = (
            lax.all_gather(v, "dp", axis=0, tiled=True, axis_index_groups=near)
            for v in (w_key, w_value, w_hidden, wt)
        )
    shard = width // inner
    woc = half // inner
    sds = jax.ShapeDtypeStruct
    spec = scratch(rows, width, nb, top, 2 * half, 2 * ffh, nz, shard)
    names = in_names + out_names + list(spec)
    vmem = pl.BlockSpec(memory_space=pltpu.VMEM)
    anyw = pl.BlockSpec(memory_space=pl.ANY)
    out, gt, QA, PA, gwh, gwT, gkv, small, gain1 = pl.pallas_call(
        functools.partial(kernel, names, outer),
        out_shape=(
            sds((nb, 2, rb, width // 2), bf16),
            sds((nb, 2, rb, width), bf16),
            sds((nz, 2, 2, shard, half), bf16),
            sds((nz, 2, 2, woc, width), bf16),
            sds((shard, ffh), f32),
            sds((shard, ffh), f32),
            sds((shard, 128), f32),
            sds((32, width), f32),
            sds((1, width), f32),
        ),
        in_specs=[pl.BlockSpec(memory_space=pltpu.SMEM)] + [anyw] + [vmem] * 6 + [anyw] * 5,
        out_specs=[anyw] * 2 + [vmem] * 7,
        scratch_shapes=list(spec.values()),
        compiler_params=pltpu.CompilerParams(
            collective_id=0, has_side_effects=True, vmem_limit_bytes=63 * 2**20
        ),
    )(
        lengths, tokens.reshape(2 * nb, rb, width), gain_attn[None], w_router.T, gain_ffn[None],
        expert_ids.T, w_key, w_value, w_query, w_out, w_hidden, wt,
        grad_out.reshape(nb, 2, rb, width // 2),
    )
    out, gt, gwq, gwo, gwh, gwT, gk, gv, gwr, g1, g2 = pl.pallas_call(
        close,
        out_shape=(
            sds(out.shape, bf16),
            sds(gt.shape, bf16),
            sds((width, half), f32),
            sds((half, width), f32),
            sds((shard, ffh), f32),
            sds((shard, ffh), f32),
            sds((shard, 64), f32),
            sds((shard, 64), f32),
            sds((n_experts, width), f32),
            sds((1, width), f32),
            sds((1, width), f32),
        ),
        in_specs=[anyw] * 9,
        out_specs=[vmem] * 11,
        scratch_shapes=[
            pltpu.VMEM((width, half), bf16),
            pltpu.VMEM((half, width), bf16),
            pltpu.VMEM((shard, 128), f32),
            pltpu.VMEM((32, width), f32),
            pltpu.SemaphoreType.DMA((9,)),
        ],
        compiler_params=pltpu.CompilerParams(vmem_limit_bytes=63 * 2**20),
    )(out, gt, QA.reshape(width, half), PA.reshape(half, width), gwh, gwT, gkv, small, gain1)
    if outer > 1:
        gwq, gwo, gwr, g1, g2 = lax.psum(
            (gwq, gwo, gwr, g1, g2), "dp", axis_index_groups=near
        )
        gwh, gwT, gk, gv = (
            lax.psum_scatter(v, "dp", scatter_dimension=0, tiled=True, axis_index_groups=near)
            for v in (gwh, gwT, gk, gv)
        )
    return (
        out.reshape(rows, width // 2), gt.reshape(rows, width), gk, gv, gwr.T, gwq, gwo,
        gwh, gwT.T, g1[0], g2[0],
    )


def solution(mesh):
    placed = (
        P("dp", None), P(), P("dp", None), P("dp", None), P(), P(None, "expert"),
        P("expert", None), P(), P("dp", "expert"), P("expert", "dp"), P("dp", None),
        P("dp"), P("dp", "expert"),
    )
    return jax.shard_map(
        shards,
        mesh=mesh,
        in_specs=placed,
        out_specs=(
            P("dp", "expert"), P("dp", None), P("dp", None), P("dp", None), P(),
            P(None, "expert"), P("expert", None), P("dp", "expert"), P("expert", "dp"),
            P(), P(),
        ),
        check_vma=False,
    )
```
